32 devices in a mesh: pipe: 2 (over core), dp: 8 (over z, x), sub: 2 (over y).
Axes of the slice: x: 2, y: 2, z: 4, core: 2. Of those that a mesh axis runs over, the one named last changes fastest.
Arguments:
- inputs: bfloat16 [2, 16, 512, 768], P(None, ('dp', 'sub')), may hold values from -6 to 6
- cotangent: bfloat16 [2, 16, 512, 768], P(None, ('dp', 'sub')), may hold values from -6 to 6
- lengths: int32 [2, 16], P(None, ('dp', 'sub')), may hold values from 64 to 512, as said below
- attend_gain: float32 [2, 768], P('pipe'), may hold values from 0.5 to 1.5
- attend_shift: float32 [2, 768], P('pipe'), may hold values from -1.8 to 1.8
- joint_weight: bfloat16 [2, 768, 2304], P('pipe'), may hold values from -0.21875 to 0.21875
- joint_bias: float32 [2, 1536], P('pipe'), may hold values from -3 to 3
- project_weight: bfloat16 [2, 768, 768], P('pipe'), may hold values from -15 to 15
- project_bias: float32 [2, 768], P('pipe'), may hold values from -6 to 6
- feed_gain: float32 [2, 768], P('pipe'), may hold values from 0.5 to 1.5
- feed_shift: float32 [2, 768], P('pipe'), may hold values from -1.8 to 1.8
- expand_weight: bfloat16 [2, 768, 3072], P('pipe'), may hold values from -0.21875 to 0.21875
- expand_bias: float32 [2, 3072], P('pipe'), may hold values from -3 to 3
- shrink_weight: bfloat16 [2, 3072, 768], P('pipe'), may hold values from -0.875 to 0.875
- shrink_bias: float32 [2, 768], P('pipe'), may hold values from -6 to 6
Outputs:
- section_outputs: bfloat16 [2, 2, 16, 512, 768], P('pipe', None, ('dp', 'sub'))
- section_input_grads: float32 [2, 2, 16, 512, 768], P('pipe', None, ('dp', 'sub'))
- grad_attend_gain: float32 [2, 768], P('pipe')
- grad_attend_shift: float32 [2, 768], P('pipe')
- grad_joint_weight: float32 [2, 768, 2304], P('pipe')
- grad_joint_bias: float32 [2, 1536], P('pipe')
- grad_project_weight: float32 [2, 768, 768], P('pipe')
- grad_project_bias: float32 [2, 768], P('pipe')
- grad_feed_gain: float32 [2, 768], P('pipe')
- grad_feed_shift: float32 [2, 768], P('pipe')
- grad_expand_weight: float32 [2, 768, 3072], P('pipe')
- grad_expand_bias: float32 [2, 3072], P('pipe')
- grad_shrink_weight: float32 [2, 3072, 768], P('pipe')
- grad_shrink_bias: float32 [2, 768], P('pipe')
The draws below stay inside these ranges and needn't reach their ends.
Inputs may be any that keep to these rules, and one draw needn't show every extreme that they name: `lengths`: each sequence's true length; positions from it to 511 are padding. Some sequence fills its whole bucket.
All inputs are finite; a program needn't handle non-finite values.
Results may differ from the reference program's by a relative error of at most 0.014.
Values may be sent and summed in bfloat16 or wider, within the bound.
A program may use at most 256 MiB of HBM per device.

```python
import jax
import jax.numpy as jnp
from jax import lax

D = 768
FF = 3072
SEQ = 512
MIN_LEN = 64
M = 2
SEQS = 16


def draw_lengths(key, part):
    key = jax.random.fold_in(key, 7)
    first_key, row_key, column_key = jax.random.split(key, 3)
    values = jax.random.randint(first_key, (M, SEQS), MIN_LEN, SEQ + 1)
    row_pick = jax.random.randint(row_key, (), 0, M)
    column_pick = jax.random.randint(column_key, (), 0, SEQS)
    row_index = lax.broadcasted_iota(jnp.int32, (M, SEQS), 0)
    column_index = lax.broadcasted_iota(jnp.int32, (M, SEQS), 1)
    chosen = (row_index == row_pick) & (column_index == column_pick)
    return jnp.where(chosen, SEQ, values).astype(jnp.int32)


def raised(result, rng, source, target, shards_of, factor):
    def block_of(position):
        return (jnp.arange(result.shape[position]) // (result.shape[position] // shards_of)).reshape((-1,) + (1,) * (result.ndim - 1 - position))

    one_side = jax.random.permutation(rng, shards_of)[block_of(target)]
    second = (block_of(target) + shards_of // 2) % shards_of
    return jnp.where((block_of(source) == one_side) | (block_of(source) == second), factor * result, result)


def level_of(rng, dims, shards, low, largest):
    def one(axis_at, blocks):
        heights = jax.random.uniform(jax.random.fold_in(jax.random.fold_in(rng, 6), axis_at), (blocks,), jnp.float32, low / len(shards), largest / len(shards))
        return jnp.repeat(jnp.exp(heights), dims[axis_at] // blocks).reshape((-1,) + (1,) * (len(dims) - axis_at - 1))

    loudness = one(*shards[0])
    for cut in shards[1:]:
        loudness = loudness * one(*cut)
    return loudness


def centred(key, extent, spread, limit, shards=(), kind=jnp.bfloat16):
    array = jax.random.normal(key, extent, jnp.float32) * spread
    if len(shards) > 0:
        array = level_of(key, extent, shards, -0.22, 0.18) * array
    return jnp.clip(array, min=-limit, max=limit).astype(kind)


def noise_with(key, extent, scale, most, pieces, heavy, kind=jnp.bfloat16):
    result = scale * jax.random.normal(key, extent, jnp.float32)
    if pieces:
        result = result * level_of(key, extent, pieces, -0.22, 0.18)
    return jnp.clip(raised(result, jax.random.fold_in(key, 3), *heavy), -most, most).astype(kind)


def setup_inputs(seed: int = 0) -> dict:
    key_of = jax.random.split(jax.random.key(seed), 16)
    return {
        "inputs": centred(key_of[0], (M, SEQS, SEQ, D), 1.0, 6.0, ((1, 16),)),
        "cotangent": noise_with(key_of[1], (M, SEQS, SEQ, D), 1.0, 6.0, ((1, 16),), (1, 3, 16, 2.0)),
        "lengths": draw_lengths(jax.random.fold_in(key_of[15], 71), 0),
        "attend_gain": jnp.clip(1.0 + 0.1 * jax.random.normal(key_of[3], (2, D), jnp.float32), 0.5, 1.5),
        "attend_shift": centred(key_of[4], (2, D), 0.3, 1.8, ((0, 2),), jnp.float32),
        "joint_weight": centred(key_of[5], (2, D, 3 * D), D ** -0.5, 0.21875, ((0, 2),)),
        "joint_bias": centred(key_of[6], (2, 2 * D), 0.5, 3.0, ((0, 2),), jnp.float32),
        "project_weight": centred(key_of[7], (2, D, D), 2.5, 15.0, ((0, 2),)),
        "project_bias": centred(key_of[8], (2, D), 1.0, 6.0, ((0, 2),), jnp.float32),
        "feed_gain": jnp.clip(1.0 + 0.1 * jax.random.normal(key_of[9], (2, D), jnp.float32), 0.5, 1.5),
        "feed_shift": centred(key_of[10], (2, D), 0.3, 1.8, ((0, 2),), jnp.float32),
        "expand_weight": centred(key_of[11], (2, D, FF), D ** -0.5, 0.21875, ((0, 2),)),
        "expand_bias": centred(key_of[12], (2, FF), 0.5, 3.0, ((0, 2),), jnp.float32),
        "shrink_weight": centred(key_of[13], (2, FF, D), (FF // 64) ** -0.5, 0.875, ((0, 2),)),
        "shrink_bias": centred(key_of[14], (2, D), 1.0, 6.0, ((0, 2),), jnp.float32),
    }


@jax.custom_vjp
def low(v):
    return lax.optimization_barrier(v.astype(jnp.bfloat16)).astype(jnp.float32)

@jax.custom_vjp
def low_back(v):
    return v

def low_keep(v):
    return (low(v), None)

def low_pass(kept, grad):
    return (grad,)

def back_keep(v):
    return (v, None)

def back_low(kept, grad):
    return (low(grad),)
low.defvjp(low_keep, low_pass)
low_back.defvjp(back_keep, back_low)
exact_mode = lax.Precision.HIGHEST
branch_scale = 24.0 ** (-0.5)
head_scale = 0.125
norm_eps = 1e-05
gelu_scale = (2.0 / 3.141592653589793) ** 0.5
gelu_cubic = 0.044715
masked_score = -1e+30

def layer_norm(values, norm_gain, norm_shift):
    center = values - lax.optimization_barrier(jnp.mean(values, axis=-1, keepdims=True))
    inverse = lax.rsqrt(lax.optimization_barrier(jnp.mean(center * center, axis=-1, keepdims=True)) + norm_eps)
    return center * inverse * norm_gain + norm_shift

def gelu_value(hidden):
    inner = jnp.tanh(gelu_scale * (hidden + gelu_cubic * hidden * hidden * hidden))
    return 0.5 * hidden * (1.0 + inner)

def product(left, right):
    return jnp.dot(left, right, precision=exact_mode)

def attention(query, keys, values, length):
    seq_rows = query.shape[0]
    query_heads = query.reshape(seq_rows, -1, 64)
    key_heads = keys.reshape(seq_rows, -1, 64)
    value_heads = values.reshape(seq_rows, -1, 64)
    scores = low_back(jnp.einsum('qhd,khd->hqk', query_heads, key_heads, precision=exact_mode) * head_scale)
    positions = jnp.arange(seq_rows, dtype=jnp.int32)
    allowed = (positions[None, :] <= positions[:, None]) & (positions[None, :] < length)
    scores = jnp.where(allowed[None], scores, masked_score)
    highest = lax.optimization_barrier(jnp.max(scores, axis=-1, keepdims=True))
    exponent = jnp.exp(scores - highest)
    weights = exponent / lax.optimization_barrier(jnp.sum(exponent, axis=-1, keepdims=True))
    mixture = jnp.einsum('hqk,khd->qhd', low(weights), value_heads, precision=exact_mode)
    return mixture.reshape(seq_rows, -1)

def block(values, params, length):
    attend_gain, attend_shift, joint_weight, joint_bias, project_weight, project_bias, feed_gain, feed_shift, expand_weight, expand_bias, shrink_weight, shrink_bias = params
    width = values.shape[1]
    normed = low(layer_norm(values, attend_gain, attend_shift))
    full_bias = jnp.concatenate([joint_bias[:width], jnp.zeros((width,), jnp.float32), joint_bias[width:]])
    joint = low_back(product(normed, joint_weight) + full_bias)
    query = low(joint[:, :width])
    keys = low(joint[:, width:2 * width])
    values_part = low(joint[:, 2 * width:])
    attended = low(low_back(attention(query, keys, values_part, length)))
    branch = low_back(product(attended, project_weight) + project_bias)
    middle = values + branch_scale * branch
    normed_two = low(layer_norm(middle, feed_gain, feed_shift))
    hidden = low_back(product(normed_two, expand_weight) + expand_bias)
    active = low(gelu_value(hidden))
    branch_two = low_back(product(active, shrink_weight) + shrink_bias)
    return middle + branch_scale * branch_two

def reference(inputs, cotangent, lengths, attend_gain, attend_shift, joint_weight, joint_bias, project_weight, project_bias, feed_gain, feed_shift, expand_weight, expand_bias, shrink_weight, shrink_bias):
    params = tuple((item.astype(jnp.float32) for item in (attend_gain, attend_shift, joint_weight, joint_bias, project_weight, project_bias, feed_gain, feed_shift, expand_weight, expand_bias, shrink_weight, shrink_bias)))
    micro_count = lengths.shape[0]
    seq_count = lengths.shape[1]
    flat_inputs = inputs.reshape(-1, SEQ, D).astype(jnp.float32)
    flat_lengths = lengths.reshape(-1).astype(jnp.int32)
    probes = jnp.zeros_like(flat_inputs)

    def forward(weights, section_in, probe_in):

        def one_sequence(item):
            values, probe, length = item
            first = block(values, tuple((entry[0] for entry in weights)), length)
            passed = low(low_back(first)) + probe
            final = block(passed, tuple((entry[1] for entry in weights)), length)
            return (final, passed)
        return lax.map(jax.checkpoint(one_sequence), (section_in, probe_in, flat_lengths))
    (final, passed), pullback = jax.vjp(forward, params, flat_inputs, probes)
    positions = jnp.arange(SEQ, dtype=jnp.int32)
    live = (positions[None, :] < flat_lengths[:, None]).astype(jnp.float32)
    start_grad = cotangent.reshape(-1, SEQ, D).astype(jnp.float32) * live[:, :, None]
    weight_grads, input_grad, middle_grad = pullback((start_grad, jnp.zeros_like(passed)))
    full_shape = (micro_count, seq_count, SEQ, D)
    section_outputs = jnp.stack([passed.reshape(full_shape), final.reshape(full_shape)]).astype(jnp.bfloat16)
    section_input_grads = jnp.stack([input_grad.reshape(full_shape), middle_grad.reshape(full_shape)]).astype(jnp.float32)
    return (section_outputs, section_input_grads, weight_grads[0], weight_grads[1], weight_grads[2], weight_grads[3], weight_grads[4], weight_grads[5], weight_grads[6], weight_grads[7], weight_grads[8], weight_grads[9], weight_grads[10], weight_grads[11])
```

```python
import functools

import jax
import jax.numpy as jnp
from jax import lax
from jax.experimental import pallas as pl
from jax.experimental.pallas import tpu as pltpu
from jax.sharding import PartitionSpec as P

MESH = pl.DeviceIdType.MESH
branch_scale = 24.0 ** (-0.5)
head_scale = 0.125
norm_eps = 1e-05
gelu_scale = (2.0 / 3.141592653589793) ** 0.5
gelu_cubic = 0.044715
masked_score = -1e30
low = jnp.bfloat16
wide = jnp.float32
head_width = 64
pair_width = 128
query_rows = 256
block_rows = 768
block_cols = 256


def product(left, right):
    return jnp.dot(left, right, preferred_element_type=wide)


def back_product(left, right):
    return lax.dot_general(left, right, (((1,), (1,)), ((), ())), preferred_element_type=wide)


def flipped(matrix):
    return matrix.astype(wide).T


def sibling():
    return (1 - lax.axis_index("pipe"), lax.axis_index("dp"), lax.axis_index("sub"))


def greet_sibling():
    barrier = pltpu.get_barrier_semaphore()
    pl.semaphore_signal(barrier, inc=1, device_id=sibling(), device_id_type=MESH)
    pl.semaphore_wait(barrier, 1)


def pair_mask(half, value):
    lane = lax.broadcasted_iota(jnp.int32, (1, pair_width), 1)
    return jnp.where((lane // head_width) == half, value, 0.0).astype(low)


def score_rows(block):
    first = query_rows * (block * (block + 1) // 2)
    return first, query_rows * (block + 1)


def normalize(values):
    center = values - jnp.mean(values, axis=-1, keepdims=True)
    inverse = lax.rsqrt(jnp.mean(center * center, axis=-1, keepdims=True) + norm_eps)
    return center * inverse, inverse


def norm_slope(graded, normal, inverse):
    return inverse * (
        graded
        - jnp.mean(graded, axis=-1, keepdims=True)
        - normal * jnp.mean(graded * normal, axis=-1, keepdims=True)
    )


def half_stack(matrix, value):
    return jnp.concatenate(
        [matrix * pair_mask(0, value), matrix * pair_mask(1, value)], axis=0
    )


def sections_kernel(
    lengths,
    inputs,
    cotangent,
    joint_weight,
    project_weight,
    expand_weight,
    shrink_weight,
    attend_gain,
    attend_shift,
    joint_bias,
    project_bias,
    feed_gain,
    feed_shift,
    expand_bias,
    shrink_bias,
    outputs,
    input_grads,
    normed_out,
    attended_out,
    normed_two_out,
    active_out,
    shrink_grad_out,
    hidden_grad_out,
    joint_grad_out,
    branch_grad_out,
    small,
    normal_out,
    inverse_out,
    joint_out,
    probs_out,
    normal_two_out,
    inverse_two_out,
    slope_out,
    joint_w,
    project_w,
    expand_w,
    shrink_w,
    source,
    result,
    top_grad,
    normed,
    normal,
    inverse,
    joint,
    probs,
    attended,
    middle,
    normed_two,
    normal_two,
    inverse_two,
    active,
    slope,
    mask,
    shrink_grad,
    hidden_grad,
    joint_grad,
    branch_grad,
    attended_grad,
    source_grad,
    key_part,
    value_part,
    weight_sems,
    source_sems,
    send_sems,
    recv_sems,
    result_sems,
    left_sems,
    keep_sems,
    load_sems,
    grad_sems,
):
    first = lax.axis_index("pipe") == 0
    second = jnp.logical_not(first)
    micro_count, seq_rows, width = source.shape
    hidden_width = expand_w.shape[1]
    pair_count = width // pair_width
    block_count = seq_rows // query_rows
    last = micro_count - 1
    weight_loads = [
        pltpu.make_async_copy(place, buffer, weight_sems.at[index])
        for index, (place, buffer) in enumerate(
            (
                (joint_weight, joint_w),
                (project_weight, project_w),
                (expand_weight, expand_w),
                (shrink_weight, shrink_w),
            )
        )
    ]
    lefts = (
        (normed, normed_out),
        (attended, attended_out),
        (normed_two, normed_two_out),
        (active, active_out),
    )
    kept = (
        (normal, normal_out),
        (inverse, inverse_out),
        (joint, joint_out),
        (probs, probs_out),
        (normal_two, normal_two_out),
        (inverse_two, inverse_two_out),
        (slope, slope_out),
        (attended, attended_out),
    )
    grads = (
        (shrink_grad, shrink_grad_out),
        (hidden_grad, hidden_grad_out),
        (branch_grad, branch_grad_out),
        (joint_grad, joint_grad_out),
        (source_grad, input_grads),
    )

    def block_span(block):
        return slice(block * query_rows, (block + 1) * query_rows)

    def micro_rows(micro):
        return pl.ds(pl.multiple_of(micro * seq_rows, seq_rows), seq_rows)

    def input_load(micro):
        return pltpu.make_async_copy(inputs.at[micro], source.at[micro], source_sems.at[micro])

    def cotangent_load(micro):
        return pltpu.make_async_copy(
            cotangent.at[micro], top_grad.at[micro], source_sems.at[micro]
        )

    def onward(target, phase, micro, block):
        return pltpu.make_async_remote_copy(
            src_ref=result.at[micro, block_span(block)],
            dst_ref=target.at[micro, block_span(block)],
            send_sem=send_sems.at[micro, block],
            recv_sem=recv_sems.at[micro, block],
            device_id=sibling(),
            device_id_type=MESH,
        )

    def result_out(micro):
        return pltpu.make_async_copy(
            result.at[micro], outputs.at[micro], result_sems.at[micro]
        )

    def left_out(index, micro):
        buffer, place = lefts[index]
        return pltpu.make_async_copy(buffer, place.at[micro_rows(micro)], left_sems.at[index])

    def keep_place(index, micro):
        place = kept[index][1]
        return place.at[micro_rows(micro)] if index == 7 else place.at[micro]

    def keep_out(index, micro):
        return pltpu.make_async_copy(kept[index][0], keep_place(index, micro), keep_sems.at[index])

    def keep_load(index, micro):
        return pltpu.make_async_copy(keep_place(index, micro), kept[index][0], load_sems.at[index])

    def grad_out(index, micro):
        buffer, place = grads[index]
        return pltpu.make_async_copy(buffer, place.at[micro_rows(micro)], grad_sems.at[index])

    @pl.when(first)
    def _():
        for micro in range(micro_count):
            input_load(micro).start()

    weight_loads[0].start()

    @pl.when(second)
    def _():
        for micro in range(micro_count):
            cotangent_load(micro).start()

    for load in weight_loads[1:]:
        load.start()
    greet_sibling()
    small[...] = jnp.zeros_like(small)

    def pair_columns(part, pair):
        start = part * width + pair * pair_width
        return slice(start, start + pair_width)

    def attend_block(block):
        start, rows = score_rows(block)
        span = block_span(block)

        def scores_of(pair):
            keys = half_stack(joint[:rows, pair_columns(1, pair)], head_scale)
            return back_product(keys, joint[span, pair_columns(0, pair)])

        def mix(pair, weights):
            values = flipped(joint[:rows, pair_columns(2, pair)]).astype(low)
            halves = [
                product(values[half * head_width : (half + 1) * head_width], weights[half])
                for half in range(2)
            ]
            attended[span, pair_columns(0, pair)] = (
                jnp.concatenate(halves, axis=0).T.astype(low)
            )

        ahead = scores_of(0)
        behind = None
        for pair in range(pair_count):
            scores = ahead
            if pair + 1 < pair_count:
                ahead = scores_of(pair + 1)
            if behind is not None:
                mix(*behind)
            weights = []
            for half in range(2):
                masked = scores[half * rows : (half + 1) * rows] + mask[start : start + rows]
                exponent = jnp.exp(masked - jnp.max(masked, axis=0, keepdims=True))
                part = exponent * (1.0 / jnp.sum(exponent, axis=0, keepdims=True))
                part = part.astype(low)
                probs[2 * pair + half, start : start + rows] = part
                weights.append(part)
            behind = (pair, weights)
        mix(*behind)

    def forward_micro(micro, _):
        def before_write(left_indices, keep_indices):
            @pl.when(micro > 0)
            def _():
                for index in left_indices:
                    left_out(index, micro - 1).wait()
                for index in keep_indices:
                    keep_out(index, micro - 1).wait()

        def after_write(left_indices, keep_indices):
            for index in left_indices:
                left_out(index, micro).start()

            @pl.when(micro < last)
            def _():
                for index in keep_indices:
                    keep_out(index, micro).start()

        def weight_ready(index):
            @pl.when(micro == 0)
            def _():
                weight_loads[index].wait()

        length = lengths[micro, 0]
        for block in range(block_count):
            start, rows = score_rows(block)
            key_pos = lax.broadcasted_iota(jnp.int32, (rows, query_rows), 0)
            query_pos = block * query_rows + lax.broadcasted_iota(
                jnp.int32, (rows, query_rows), 1
            )
            allowed = (key_pos <= query_pos) & (key_pos < length)
            mask[start : start + rows] = jnp.where(allowed, 0.0, masked_score)

        @pl.when(first)
        def _():
            input_load(micro).wait()

        for block in range(block_count):
            span = block_span(block)
            final = block == block_count - 1

            @pl.when(second)
            def _():
                onward(source, 0, micro, block).wait_recv()

            if block == 0:
                before_write((0,), (0, 1))
            normal_one, inverse_one = normalize(source[micro, span].astype(wide))
            normal[span] = normal_one.astype(low)
            inverse[span] = jnp.broadcast_to(inverse_one, (query_rows, inverse.shape[1]))
            normed[span] = (normal_one * attend_gain[...] + attend_shift[...]).astype(low)
            if final:
                after_write((0,), (0, 1))
            if block == 0:
                before_write((), (2,))
                weight_ready(0)
            for part in range(3):
                columns = slice(part * width, (part + 1) * width)
                piece = product(normed[span], joint_w[:, columns])
                if part == 0:
                    piece = piece + joint_bias[:, :width]
                elif part == 2:
                    piece = piece + joint_bias[:, width:]
                joint[span, columns] = piece.astype(low)
            if final:
                after_write((), (2,))
            if block == 0:
                before_write((1,), (3,))
            attend_block(block)
            if final:
                after_write((1,), (3,))
            if block == 0:
                before_write((2,), (4, 5))
                weight_ready(1)
            middle[span] = source[micro, span].astype(wide) + branch_scale * (
                product(attended[span], project_w[...]) + project_bias[...]
            )
            normal_both, inverse_both = normalize(middle[span])
            normal_two[span] = normal_both.astype(low)
            inverse_two[span] = jnp.broadcast_to(inverse_both, (query_rows, inverse.shape[1]))
            normed_two[span] = (normal_both * feed_gain[...] + feed_shift[...]).astype(low)
            if final:
                after_write((2,), (4, 5))
            if block == 0:
                before_write((3,), (6,))
                weight_ready(2)
            for part in range(hidden_width // width):
                columns = slice(part * width, (part + 1) * width)
                hidden = product(normed_two[span], expand_w[:, columns]) + expand_bias[:, columns]
                square = hidden * hidden
                inner = jnp.tanh(hidden * (gelu_scale + (gelu_scale * gelu_cubic) * square))
                gate = 0.5 + 0.5 * inner
                value = hidden * gate
                active[span, columns] = value.astype(low)
                slope[span, columns] = (
                    gate
                    + value
                    * (1.0 - inner)
                    * (gelu_scale + (3.0 * gelu_scale * gelu_cubic) * square)
                ).astype(low)
            if final:
                after_write((3,), (6,))
            if block == 0:
                weight_ready(3)
            result[micro, span] = (
                middle[span]
                + branch_scale * (product(active[span], shrink_w[...]) + shrink_bias[...])
            ).astype(low)

            @pl.when(first)
            def _():
                onward(source, 0, micro, block).start()

        result_out(micro).start()
        return 0

    lax.fori_loop(0, micro_count, forward_micro, 0)
    for micro in range(micro_count):
        result_out(micro).wait()

    @pl.when(first)
    def _():
        for micro in range(micro_count):
            for block in range(block_count):
                onward(source, 0, micro, block).wait_send()

    def add_sum(row, values):
        small[row : row + 1] += jnp.sum(values, axis=0, keepdims=True)

    def attend_block_back(block):
        start, rows = score_rows(block)
        span = block_span(block)
        bottom = block == block_count - 1

        def weight_grad_of(pair):
            values = half_stack(joint[:rows, pair_columns(2, pair)], 1.0)
            return back_product(values, attended_grad[span, pair_columns(0, pair)])

        lane = lax.broadcasted_iota(jnp.int32, (1, pair_width), 1)
        upper = lane >= head_width
        ahead = weight_grad_of(0)
        for pair in range(pair_count):
            weight_grad = ahead
            if pair + 1 < pair_count:
                ahead = weight_grad_of(pair + 1)
            flat = pair_columns(0, pair)
            query = joint[span, flat]
            keys = flipped(joint[:rows, pair_columns(1, pair)]).astype(low)
            out_grad = attended_grad[span, flat]
            inner = (out_grad.astype(wide) * attended[span, flat].astype(wide)).T
            key_halves, value_halves, query_halves = [], [], []
            for half in range(2):
                head = slice(half * head_width, (half + 1) * head_width)
                delta = jnp.sum(inner[head], axis=0, keepdims=True)
                weights = probs[2 * pair + half, start : start + rows]
                score_grad = (
                    weights.astype(wide)
                    * (weight_grad[half * rows : (half + 1) * rows] - delta)
                ).astype(low)
                value_halves.append(product(weights, out_grad))
                key_halves.append(product(score_grad, query))
                query_halves.append(product(keys[head], score_grad))
            joint_grad[span, flat] = (
                jnp.concatenate(query_halves, axis=0).T * head_scale
            ).astype(low)
            key_grad = jnp.where(upper, key_halves[1], key_halves[0]) * head_scale
            value_grad = jnp.where(upper, value_halves[1], value_halves[0])
            done = rows - query_rows
            key_done, value_done = key_grad[done:], value_grad[done:]
            if not bottom:
                key_done = key_done + key_part[done:rows, flat]
                value_done = value_done + value_part[done:rows, flat]
            joint_grad[span, pair_columns(1, pair)] = key_done.astype(low)
            joint_grad[span, pair_columns(2, pair)] = value_done.astype(low)
            if done:
                if bottom:
                    key_part[:done, flat] = key_grad[:done]
                    value_part[:done, flat] = value_grad[:done]
                else:
                    key_part[:done, flat] += key_grad[:done]
                    value_part[:done, flat] += value_grad[:done]

    def backward_micro(step, _):
        micro = last - step

        def before_write(index):
            @pl.when(step > 0)
            def _():
                grad_out(index, micro + 1).wait()

        def loaded(*indices):
            @pl.when(step > 0)
            def _():
                for index in indices:
                    keep_load(index, micro).wait()

        def load_next(*indices):
            @pl.when(micro > 0)
            def _():
                for index in indices:
                    keep_load(index, micro - 1).start()

        last_row = jnp.where(first, seq_rows, lengths[micro, 0])

        @pl.when(second)
        def _():
            cotangent_load(micro).wait()

        for block in reversed(range(block_count)):
            span = block_span(block)
            opening = block == block_count - 1
            closing = block == 0

            @pl.when(first)
            def _():
                onward(top_grad, 1, micro, block).wait_recv()

            row_pos = block * query_rows + lax.broadcasted_iota(jnp.int32, (query_rows, 1), 0)
            output_grad = jnp.where(row_pos < last_row, top_grad[micro, span].astype(wide), 0.0)
            if opening:
                before_write(0)
            shrink_low = (branch_scale * output_grad).astype(low)
            shrink_grad[span] = shrink_low
            add_sum(5, shrink_low.astype(wide))
            middle[span] = output_grad
            if closing:
                grad_out(0, micro).start()
            if opening:
                before_write(1)
                loaded(6)
            for part in range(hidden_width // width):
                columns = slice(part * width, (part + 1) * width)
                grad = back_product(shrink_grad[span], shrink_w[columns, :])
                grad_low = (grad * slope[span, columns].astype(wide)).astype(low)
                hidden_grad[span, columns] = grad_low
                add_sum(8 + part, grad_low.astype(wide))
            if closing:
                load_next(6)
                grad_out(1, micro).start()
            normed_grad = back_product(hidden_grad[span], expand_w[...])
            if opening:
                loaded(4, 5)
            normal_wide = normal_two[span].astype(wide)
            add_sum(3, normed_grad * normal_wide)
            add_sum(4, normed_grad)
            middle[span] += norm_slope(
                normed_grad * feed_gain[...], normal_wide, inverse_two[span, :1]
            )
            if closing:
                load_next(4, 5)
            if opening:
                before_write(2)
            branch_low = (branch_scale * middle[span]).astype(low)
            branch_grad[span] = branch_low
            add_sum(2, branch_low.astype(wide))
            if closing:
                grad_out(2, micro).start()
            attended_grad[span] = back_product(branch_grad[span], project_w[...]).astype(low)
            if opening:
                before_write(3)
                loaded(2, 3, 7)
            attend_block_back(block)
            if closing:
                load_next(2, 3, 7)
                grad_out(3, micro).start()
            add_sum(6, joint_grad[span, :width].astype(wide))
            add_sum(7, joint_grad[span, 2 * width :].astype(wide))
            normed_grad = back_product(joint_grad[span], joint_w[...])
            if opening:
                before_write(4)
                loaded(0, 1)
            normal_wide = normal[span].astype(wide)
            add_sum(0, normed_grad * normal_wide)
            add_sum(1, normed_grad)
            total = middle[span] + norm_slope(
                normed_grad * attend_gain[...], normal_wide, inverse[span, :1]
            )
            if closing:
                load_next(0, 1)
            source_grad[span] = total
            result[micro, span] = total.astype(low)

            @pl.when(second)
            def _():
                onward(top_grad, 1, micro, block).start()

        grad_out(4, micro).start()
        return 0

    left_out(1, last).wait()
    lax.fori_loop(0, micro_count, backward_micro, 0)
    for index in (0, 2, 3):
        left_out(index, last).wait()
    for index in range(len(grads)):
        grad_out(index, 0).wait()

    @pl.when(second)
    def _():
        for micro in range(micro_count):
            for block in range(block_count):
                onward(top_grad, 1, micro, block).wait_send()


def run_sections(lengths, inputs, cotangent, weights):
    micro_count, seq_rows, width = inputs.shape
    hidden = weights["expand_weight"].shape[1]
    heads = width // head_width
    tokens = micro_count * seq_rows
    blocks = seq_rows // query_rows
    score_total = score_rows(blocks)[0]
    small_rows = -(-(8 + hidden // width) // 8) * 8
    hbm = pl.BlockSpec(memory_space=pl.ANY)
    vmem = pl.BlockSpec(memory_space=pltpu.VMEM)

    def row(name):
        return weights[name].reshape(1, -1)

    def shape(*dims, kind=low):
        return jax.ShapeDtypeStruct(dims, kind)

    return pl.pallas_call(
        sections_kernel,
        name="sections",
        out_shape=(
            shape(micro_count, seq_rows, width),
            shape(tokens, width, kind=wide),
            shape(tokens, width),
            shape(tokens, width),
            shape(tokens, width),
            shape(tokens, hidden),
            shape(tokens, width),
            shape(tokens, hidden),
            shape(tokens, 3 * width),
            shape(tokens, width),
            shape(small_rows, width, kind=wide),
            shape(micro_count, seq_rows, width),
            shape(micro_count, seq_rows, 128, kind=wide),
            shape(micro_count, seq_rows, 3 * width),
            shape(micro_count, heads, score_total, query_rows),
            shape(micro_count, seq_rows, width),
            shape(micro_count, seq_rows, 128, kind=wide),
            shape(micro_count, seq_rows, hidden),
        ),
        in_specs=[pl.BlockSpec(memory_space=pltpu.SMEM)] + [hbm] * 6 + [vmem] * 8,
        out_specs=tuple([hbm] * 10 + [vmem] + [hbm] * 7),
        scratch_shapes=[
            pltpu.VMEM((width, 3 * width), low),
            pltpu.VMEM((width, width), low),
            pltpu.VMEM((width, hidden), low),
            pltpu.VMEM((hidden, width), low),
            pltpu.VMEM((micro_count, seq_rows, width), low),
            pltpu.VMEM((micro_count, seq_rows, width), low),
            pltpu.VMEM((micro_count, seq_rows, width), low),
            pltpu.VMEM((seq_rows, width), low),
            pltpu.VMEM((seq_rows, width), low),
            pltpu.VMEM((seq_rows, 128), wide),
            pltpu.VMEM((seq_rows, 3 * width), low),
            pltpu.VMEM((heads, score_total, query_rows), low),
            pltpu.VMEM((seq_rows, width), low),
            pltpu.VMEM((seq_rows, width), wide),
            pltpu.VMEM((seq_rows, width), low),
            pltpu.VMEM((seq_rows, width), low),
            pltpu.VMEM((seq_rows, 128), wide),
            pltpu.VMEM((seq_rows, hidden), low),
            pltpu.VMEM((seq_rows, hidden), low),
            pltpu.VMEM((score_total, query_rows), wide),
            pltpu.VMEM((seq_rows, width), low),
            pltpu.VMEM((seq_rows, hidden), low),
            pltpu.VMEM((seq_rows, 3 * width), low),
            pltpu.VMEM((seq_rows, width), low),
            pltpu.VMEM((seq_rows, width), low),
            pltpu.VMEM((seq_rows, width), wide),
            pltpu.VMEM((max(seq_rows - query_rows, 8), width), wide),
            pltpu.VMEM((max(seq_rows - query_rows, 8), width), wide),
            pltpu.SemaphoreType.DMA((4,)),
            pltpu.SemaphoreType.DMA((micro_count,)),
            pltpu.SemaphoreType.DMA((micro_count, blocks)),
            pltpu.SemaphoreType.DMA((micro_count, blocks)),
            pltpu.SemaphoreType.DMA((micro_count,)),
            pltpu.SemaphoreType.DMA((4,)),
            pltpu.SemaphoreType.DMA((8,)),
            pltpu.SemaphoreType.DMA((8,)),
            pltpu.SemaphoreType.DMA((5,)),
        ],
        compiler_params=pltpu.CompilerParams(
            collective_id=1, has_side_effects=True, vmem_limit_bytes=62 * 2**20
        ),
    )(
        lengths,
        inputs,
        cotangent,
        weights["joint_weight"],
        weights["project_weight"],
        weights["expand_weight"],
        weights["shrink_weight"],
        row("attend_gain"),
        row("attend_shift"),
        row("joint_bias"),
        row("project_bias"),
        row("feed_gain"),
        row("feed_shift"),
        row("expand_bias"),
        row("shrink_bias"),
    )


def axis_bits(count):
    bits = []
    step = 1
    while step < count:
        bits.append(step)
        step *= 2
    assert step == count
    return bits


def exchange_orders(dp_count, sub_count):
    dp_bits = [("dp", step) for step in axis_bits(dp_count)]
    sub_bits = [("sub", step) for step in axis_bits(sub_count)]
    near, far = dp_bits[:1], dp_bits[1:]
    return (near + sub_bits + far, sub_bits + near + far, far + near + sub_bits)


def halved_stages(stage_count):
    rows, count = block_rows, 0
    while count < stage_count and (rows // 2) % 16 == 0:
        rows, count = rows // 2, count + 1
    return count


def partner_id(bit):
    axis, step = bit
    place = {name: lax.axis_index(name) for name in ("pipe", "dp", "sub")}
    place[axis] = place[axis] ^ step
    return (place["pipe"], place["dp"], place["sub"])


def own_bit(bit):
    axis, step = bit
    return (lax.axis_index(axis) // step) % 2


def grad_blocks(width, hidden):
    blocks = []
    for row in range(hidden // block_rows):
        for column in range(width // block_cols):
            blocks.append((0, row, column))
    for column in range(hidden // block_cols):
        blocks.append((1, 0, column))
    for column in range(3 * width // block_cols):
        blocks.append((2, 0, column))
    for column in range(width // block_cols):
        blocks.append((3, 0, column))
    return blocks


def make_groups(block_count):
    groups = []
    start, step = 0, 0
    while start < block_count:
        for kind, size in ((0, 2), (1, 2), (2, 1)):
            size = min(size, block_count - start)
            if kind == 2 and block_count - start == 2:
                size = 2
            if size:
                groups.append((kind, start, size, step))
            start += size
        step += 1
    return groups


def sum_kernel(
    orders, halvings, blocks, groups, *refs
):
    lefts, rights, small_in = refs[0:4], refs[4:8], refs[8]
    own, small_out = refs[9:11]
    left_bufs, right_bufs = refs[11:15], refs[15:19]
    arrivals = refs[19 : 19 + len(orders[0])]
    rest = refs[19 + len(orders[0]) :]
    small, small_got, load_sems, send_sems, recv_sems, free_sems, small_send, small_recv = rest
    stage_count = len(orders[0])

    loads = []
    for index in range(4):
        left_load = pltpu.make_async_copy(lefts[index], left_bufs[index], load_sems.at[2 * index])
        right_load = pltpu.make_async_copy(
            rights[index], right_bufs[index], load_sems.at[2 * index + 1]
        )
        left_load.start()
        right_load.start()
        loads.append((left_load, right_load))
    loaded = [False] * 4

    barrier = pltpu.get_barrier_semaphore()
    for bit in orders[0]:
        pl.semaphore_signal(barrier, inc=1, device_id=partner_id(bit), device_id_type=MESH)
    pl.semaphore_wait(barrier, stage_count)

    offsets = []
    for order in orders:
        offset, rows, places = 0, block_rows, []
        for stage, bit in enumerate(order):
            if stage < halvings:
                half = rows // 2
                mine = own_bit(bit)
                keep = offset + mine * half
                give = offset + (1 - mine) * half
                places.append((keep, give, half))
                offset, rows = keep, half
            else:
                places.append((offset, offset, rows))
        offsets.append(places)

    def rows_at(offset, rows):
        return pl.ds(pl.multiple_of(offset, 16), rows)

    def produce(block):
        index, row, column = blocks[block]
        if not loaded[index]:
            loads[index][0].wait()
            loads[index][1].wait()
            loaded[index] = True
        left = left_bufs[index][:, row * block_rows : (row + 1) * block_rows]
        right = right_bufs[index][:, column * block_cols : (column + 1) * block_cols]
        own[block] = lax.dot_general(
            left, right, (((0,), (0,)), ((), ())), preferred_element_type=jnp.float32
        ).astype(jnp.bfloat16)

    def message(group_index, step):
        kind, start, size, _ = groups[group_index]
        span = pl.ds(start, size)
        if step < stage_count:
            keep, give, rows = offsets[kind][step]
            source = own.at[span, rows_at(give, rows)]
            target = arrivals[step].at[span]
            bit = orders[kind][step]
        else:
            back = halvings - 1 - (step - stage_count)
            keep, give, rows = offsets[kind][back]
            source = own.at[span, rows_at(keep, rows)]
            target = own.at[span, rows_at(keep, rows)]
            bit = orders[kind][back]
        return pltpu.make_async_remote_copy(
            src_ref=source,
            dst_ref=target,
            send_sem=send_sems.at[group_index, step],
            recv_sem=recv_sems.at[group_index, step],
            device_id=partner_id(bit),
            device_id_type=MESH,
        )

    def receive(group_index, step):
        kind, start, size, _ = groups[group_index]
        span = pl.ds(start, size)
        if step < stage_count:
            message(group_index, step).wait()
            keep, give, rows = offsets[kind][step]
            place = rows_at(keep, rows)
            for block in range(start, start + size):
                own[block, place] = (
                    own[block, place].astype(jnp.float32)
                    + arrivals[step][block].astype(jnp.float32)
                ).astype(jnp.bfloat16)
            if step < halvings:
                pl.semaphore_signal(
                    free_sems.at[group_index, step],
                    inc=1,
                    device_id=partner_id(orders[kind][step]),
                    device_id_type=MESH,
                )
        else:
            back = halvings - 1 - (step - stage_count)
            keep, give, rows = offsets[kind][back]
            copy = pltpu.make_async_remote_copy(
                src_ref=own.at[span, rows_at(keep, rows)],
                dst_ref=own.at[span, rows_at(give, rows)],
                send_sem=send_sems.at[group_index, step],
                recv_sem=recv_sems.at[group_index, step],
                device_id=partner_id(orders[kind][back]),
                device_id_type=MESH,
            )
            copy.wait()

    def small_copy(stage):
        return pltpu.make_async_remote_copy(
            src_ref=small.at[stage],
            dst_ref=small_got.at[stage],
            send_sem=small_send.at[stage],
            recv_sem=small_recv.at[stage],
            device_id=partner_id(orders[0][stage]),
            device_id_type=MESH,
        )

    total_steps = stage_count + halvings
    last = max(group[3] for group in groups) + total_steps
    for tick in range(last + 1):
        for group_index, (kind, start, size, begin) in enumerate(groups):
            if begin == tick:
                for block in range(start, start + size):
                    produce(block)
                message(group_index, 0).start()
        if tick == 0:
            small[0] = small_in[...]
        elif tick <= stage_count:
            small_copy(tick - 1).wait()
            total = small[tick - 1] + small_got[tick - 1]
            if tick < stage_count:
                small[tick] = total
            else:
                small_out[...] = total
        if tick < stage_count:
            small_copy(tick).start()
        for step in reversed(range(1, total_steps + 1)):
            for group_index, (kind, start, size, begin) in enumerate(groups):
                if begin + step == tick:
                    receive(group_index, step - 1)
                    if step < total_steps:
                        if step >= stage_count:
                            back = halvings - 1 - (step - stage_count)
                            pl.semaphore_wait(free_sems.at[group_index, back], 1)
                        message(group_index, step).start()


def summed_grads(lefts, rights, small, dp_count, sub_count):
    tokens, width = lefts[3].shape
    hidden = lefts[0].shape[1]
    orders = exchange_orders(dp_count, sub_count)
    stage_count = len(orders[0])
    halvings = halved_stages(stage_count)
    blocks = grad_blocks(width, hidden)
    groups = make_groups(len(blocks))
    block_count = len(blocks)
    arrival_rows = [block_rows >> min(stage + 1, halvings) for stage in range(stage_count)]
    low = jnp.bfloat16
    return pl.pallas_call(
        functools.partial(sum_kernel, orders, halvings, blocks, groups),
        name="grad_sums",
        out_shape=(
            pltpu.VMEM((block_count, block_rows, block_cols), low),
            pltpu.VMEM(small.shape, jnp.float32),
        ),
        in_specs=[pl.BlockSpec(memory_space=pl.ANY)] * 8 + [pl.BlockSpec(memory_space=pltpu.VMEM)],
        out_specs=tuple([pl.BlockSpec(memory_space=pltpu.VMEM)] * 2),
        scratch_shapes=[pltpu.VMEM(array.shape, low) for array in lefts]
        + [pltpu.VMEM(array.shape, low) for array in rights]
        + [pltpu.VMEM((block_count, rows, block_cols), low) for rows in arrival_rows]
        + [
            pltpu.VMEM((stage_count, *small.shape), jnp.float32),
            pltpu.VMEM((stage_count, *small.shape), jnp.float32),
            pltpu.SemaphoreType.DMA((8,)),
            pltpu.SemaphoreType.DMA((len(groups), stage_count + halvings)),
            pltpu.SemaphoreType.DMA((len(groups), stage_count + halvings)),
            pltpu.SemaphoreType.REGULAR((len(groups), halvings)),
            pltpu.SemaphoreType.DMA((stage_count,)),
            pltpu.SemaphoreType.DMA((stage_count,)),
        ],
        compiler_params=pltpu.CompilerParams(
            collective_id=0, has_side_effects=True, vmem_limit_bytes=44 * 2**20
        ),
    )(*lefts, *rights, small)


stage_count_out = 6


def finish_kernel(
    blocks,
    own,
    small,
    outputs_in,
    grads_in,
    outputs,
    input_grads,
    attend_gain,
    attend_shift,
    joint,
    joint_bias,
    project,
    project_bias,
    feed_gain,
    feed_shift,
    expand,
    expand_bias,
    shrink,
    shrink_bias,
    stages,
    stage_sems,
    pass_sems,
):
    places = (shrink, expand, joint, project)
    width = shrink_bias.shape[1]
    passes = [
        pltpu.make_async_copy(outputs_in, outputs, pass_sems.at[0]),
        pltpu.make_async_copy(grads_in, input_grads, pass_sems.at[1]),
    ]
    for copy in passes:
        copy.start()

    def block_copy(block):
        index, row, column = blocks[block]
        slot = block % stage_count_out
        return pltpu.make_async_copy(
            stages.at[slot],
            places[index].at[
                pl.ds(row * block_rows, block_rows), pl.ds(column * block_cols, block_cols)
            ],
            stage_sems.at[slot],
        )

    for block in range(len(blocks)):
        if block >= stage_count_out:
            block_copy(block - stage_count_out).wait()
        stages[block % stage_count_out] = own[block].astype(jnp.float32)
        block_copy(block).start()
    for row, place in (
        (0, attend_gain),
        (1, attend_shift),
        (2, project_bias),
        (3, feed_gain),
        (4, feed_shift),
        (5, shrink_bias),
        (6, joint_bias),
        (8, expand_bias),
    ):
        for part in range(place.shape[1] // width):
            place[:, part * width : (part + 1) * width] = small[row + part : row + part + 1]
    for block in range(max(0, len(blocks) - stage_count_out), len(blocks)):
        block_copy(block).wait()
    for copy in passes:
        copy.wait()


def finished(own, small, outputs, input_grads, width, hidden):
    blocks = grad_blocks(width, hidden)
    hbm = pl.BlockSpec(memory_space=pl.ANY)
    vmem = pl.BlockSpec(memory_space=pltpu.VMEM)

    def shape(*dims):
        return jax.ShapeDtypeStruct(dims, jnp.float32)

    return pl.pallas_call(
        functools.partial(finish_kernel, blocks),
        name="finish",
        out_shape=(
            jax.ShapeDtypeStruct(outputs.shape, outputs.dtype),
            jax.ShapeDtypeStruct(input_grads.shape, input_grads.dtype),
            shape(1, width),
            shape(1, width),
            shape(width, 3 * width),
            shape(1, 2 * width),
            shape(width, width),
            shape(1, width),
            shape(1, width),
            shape(1, width),
            shape(width, hidden),
            shape(1, hidden),
            shape(hidden, width),
            shape(1, width),
        ),
        in_specs=[vmem, vmem, hbm, hbm],
        out_specs=(
            hbm, hbm, vmem, vmem, hbm, vmem, hbm, vmem, vmem, vmem, hbm, vmem, hbm, vmem
        ),
        scratch_shapes=[
            pltpu.VMEM((stage_count_out, block_rows, block_cols), jnp.float32),
            pltpu.SemaphoreType.DMA((stage_count_out,)),
            pltpu.SemaphoreType.DMA((2,)),
        ],
        compiler_params=pltpu.CompilerParams(vmem_limit_bytes=16 * 2**20),
    )(
        pltpu.with_memory_space_constraint(own, pltpu.VMEM),
        pltpu.with_memory_space_constraint(small, pltpu.VMEM),
        outputs,
        input_grads,
    )


weight_names = (
    "attend_gain",
    "attend_shift",
    "joint_weight",
    "joint_bias",
    "project_weight",
    "project_bias",
    "feed_gain",
    "feed_shift",
    "expand_weight",
    "expand_bias",
    "shrink_weight",
    "shrink_bias",
)


def body(inputs, cotangent, lengths, *params):
    weights = {name: param[0] for name, param in zip(weight_names, params)}
    micro_count, _, seq_rows, width = inputs.shape
    (
        outputs,
        input_grads,
        normed,
        attended,
        normed_two,
        active,
        shrink_grad,
        hidden_grad,
        joint_grad,
        branch_grad,
        small,
        *_,
    ) = run_sections(lengths, inputs[:, 0], cotangent[:, 0], weights)
    hidden = active.shape[1]
    own, small_sum = summed_grads(
        (active, normed_two, normed, attended),
        (shrink_grad, hidden_grad, joint_grad, branch_grad),
        small,
        lax.axis_size("dp"),
        lax.axis_size("sub"),
    )
    outputs, input_grads, *full_grads = finished(
        own, small_sum, outputs, input_grads, width, hidden
    )
    return (
        outputs[None, :, None],
        input_grads.reshape(1, micro_count, 1, seq_rows, width),
        *(grad if grad.shape[0] == 1 else grad[None] for grad in full_grads),
    )


def solution(mesh):
    in_specs = (
        P(None, ("dp", "sub"), None, None),
        P(None, ("dp", "sub"), None, None),
        P(None, ("dp", "sub")),
        P("pipe", None),
        P("pipe", None),
        P("pipe", None, None),
        P("pipe", None),
        P("pipe", None, None),
        P("pipe", None),
        P("pipe", None),
        P("pipe", None),
        P("pipe", None, None),
        P("pipe", None),
        P("pipe", None, None),
        P("pipe", None),
    )
    out_specs = (
        P("pipe", None, ("dp", "sub"), None, None),
        P("pipe", None, ("dp", "sub"), None, None),
        P("pipe", None),
        P("pipe", None),
        P("pipe", None, None),
        P("pipe", None),
        P("pipe", None, None),
        P("pipe", None),
        P("pipe", None),
        P("pipe", None),
        P("pipe", None, None),
        P("pipe", None),
        P("pipe", None, None),
        P("pipe", None),
    )
    return jax.shard_map(body, mesh=mesh, in_specs=in_specs, out_specs=out_specs, check_vma=False)
```

```python
import functools

import jax
import jax.numpy as jnp
from jax import lax
from jax.experimental import pallas as pl
from jax.experimental.pallas import tpu as pltpu
from jax.sharding import PartitionSpec as P

MESH = pl.DeviceIdType.MESH
branch_scale = 24.0 ** (-0.5)
head_scale = 0.125
norm_eps = 1e-05
gelu_scale = (2.0 / 3.141592653589793) ** 0.5
gelu_cubic = 0.044715
masked_score = -1e30
low = jnp.bfloat16
wide = jnp.float32
head_width = 64
pair_width = 128
query_rows = 256
block_rows = 768
block_cols = 256


def product(left, right):
    return jnp.dot(left, right, preferred_element_type=wide)


def back_product(left, right):
    return lax.dot_general(left, right, (((1,), (1,)), ((), ())), preferred_element_type=wide)


def flipped(matrix):
    return matrix.astype(wide).T


def sibling():
    return (1 - lax.axis_index("pipe"), lax.axis_index("dp"), lax.axis_index("sub"))


def greet_sibling():
    barrier = pltpu.get_barrier_semaphore()
    pl.semaphore_signal(barrier, inc=1, device_id=sibling(), device_id_type=MESH)
    pl.semaphore_wait(barrier, 1)


def pair_mask(half, value):
    lane = lax.broadcasted_iota(jnp.int32, (1, pair_width), 1)
    return jnp.where((lane // head_width) == half, value, 0.0).astype(low)


def score_rows(block):
    first = query_rows * (block * (block + 1) // 2)
    return first, query_rows * (block + 1)


def normalize(values):
    center = values - jnp.mean(values, axis=-1, keepdims=True)
    inverse = lax.rsqrt(jnp.mean(center * center, axis=-1, keepdims=True) + norm_eps)
    return center * inverse, inverse


def norm_slope(graded, normal, inverse):
    return inverse * (
        graded
        - jnp.mean(graded, axis=-1, keepdims=True)
        - normal * jnp.mean(graded * normal, axis=-1, keepdims=True)
    )


def half_stack(matrix, value):
    return jnp.concatenate(
        [matrix * pair_mask(0, value), matrix * pair_mask(1, value)], axis=0
    )


def sections_kernel(
    lengths,
    inputs,
    cotangent,
    joint_weight,
    project_weight,
    expand_weight,
    shrink_weight,
    attend_gain,
    attend_shift,
    joint_bias,
    project_bias,
    feed_gain,
    feed_shift,
    expand_bias,
    shrink_bias,
    outputs,
    input_grads,
    normed_out,
    attended_out,
    normed_two_out,
    active_out,
    shrink_grad_out,
    hidden_grad_out,
    joint_grad_out,
    branch_grad_out,
    small,
    normal_out,
    inverse_out,
    joint_out,
    probs_out,
    normal_two_out,
    inverse_two_out,
    slope_out,
    joint_w,
    project_w,
    expand_w,
    shrink_w,
    source,
    result,
    top_grad,
    normed,
    normal,
    inverse,
    joint,
    probs,
    attended,
    middle,
    normed_two,
    normal_two,
    inverse_two,
    active,
    slope,
    mask,
    shrink_grad,
    hidden_grad,
    joint_grad,
    branch_grad,
    attended_grad,
    source_grad,
    key_part,
    value_part,
    weight_sems,
    source_sems,
    send_sems,
    recv_sems,
    result_sems,
    left_sems,
    keep_sems,
    load_sems,
    grad_sems,
):
    first = lax.axis_index("pipe") == 0
    second = jnp.logical_not(first)
    micro_count, seq_rows, width = source.shape
    hidden_width = expand_w.shape[1]
    pair_count = width // pair_width
    block_count = seq_rows // query_rows
    last = micro_count - 1
    weight_loads = [
        pltpu.make_async_copy(place, buffer, weight_sems.at[index])
        for index, (place, buffer) in enumerate(
            (
                (joint_weight, joint_w),
                (project_weight, project_w),
                (expand_weight, expand_w),
                (shrink_weight, shrink_w),
            )
        )
    ]
    lefts = (
        (normed, normed_out),
        (attended, attended_out),
        (normed_two, normed_two_out),
        (active, active_out),
    )
    kept = (
        (normal, normal_out),
        (inverse, inverse_out),
        (joint, joint_out),
        (probs, probs_out),
        (normal_two, normal_two_out),
        (inverse_two, inverse_two_out),
        (slope, slope_out),
        (attended, attended_out),
    )
    grads = (
        (shrink_grad, shrink_grad_out),
        (hidden_grad, hidden_grad_out),
        (branch_grad, branch_grad_out),
        (joint_grad, joint_grad_out),
        (source_grad, input_grads),
    )

    def block_span(block):
        return slice(block * query_rows, (block + 1) * query_rows)

    def micro_rows(micro):
        return pl.ds(pl.multiple_of(micro * seq_rows, seq_rows), seq_rows)

    def input_load(micro):
        return pltpu.make_async_copy(inputs.at[micro], source.at[micro], source_sems.at[micro])

    def cotangent_load(micro):
        return pltpu.make_async_copy(
            cotangent.at[micro], top_grad.at[micro], source_sems.at[micro]
        )

    def onward(target, phase, micro, block):
        return pltpu.make_async_remote_copy(
            src_ref=result.at[micro, block_span(block)],
            dst_ref=target.at[micro, block_span(block)],
            send_sem=send_sems.at[micro, block],
            recv_sem=recv_sems.at[micro, block],
            device_id=sibling(),
            device_id_type=MESH,
        )

    def result_out(micro):
        return pltpu.make_async_copy(
            result.at[micro], outputs.at[micro], result_sems.at[micro]
        )

    def left_out(index, micro):
        buffer, place = lefts[index]
        return pltpu.make_async_copy(buffer, place.at[micro_rows(micro)], left_sems.at[index])

    def keep_place(index, micro):
        place = kept[index][1]
        return place.at[micro_rows(micro)] if index == 7 else place.at[micro]

    def keep_out(index, micro):
        return pltpu.make_async_copy(kept[index][0], keep_place(index, micro), keep_sems.at[index])

    def keep_load(index, micro):
        return pltpu.make_async_copy(keep_place(index, micro), kept[index][0], load_sems.at[index])

    def grad_out(index, micro):
        buffer, place = grads[index]
        return pltpu.make_async_copy(buffer, place.at[micro_rows(micro)], grad_sems.at[index])

    @pl.when(first)
    def _():
        for micro in range(micro_count):
            input_load(micro).start()

    weight_loads[0].start()

    @pl.when(second)
    def _():
        for micro in range(micro_count):
            cotangent_load(micro).start()

    for load in weight_loads[1:]:
        load.start()
    greet_sibling()
    small[...] = jnp.zeros_like(small)

    def pair_columns(part, pair):
        start = part * width + pair * pair_width
        return slice(start, start + pair_width)

    def attend_block(block):
        start, rows = score_rows(block)
        span = block_span(block)

        def scores_of(pair):
            keys = half_stack(joint[:rows, pair_columns(1, pair)], head_scale)
            return back_product(keys, joint[span, pair_columns(0, pair)])

        def mix(pair, weights):
            values = flipped(joint[:rows, pair_columns(2, pair)]).astype(low)
            halves = [
                product(values[half * head_width : (half + 1) * head_width], weights[half])
                for half in range(2)
            ]
            attended[span, pair_columns(0, pair)] = (
                jnp.concatenate(halves, axis=0).T.astype(low)
            )

        ahead = scores_of(0)
        behind = None
        for pair in range(pair_count):
            scores = ahead
            if pair + 1 < pair_count:
                ahead = scores_of(pair + 1)
            if behind is not None:
                mix(*behind)
            weights = []
            for half in range(2):
                masked = scores[half * rows : (half + 1) * rows] + mask[start : start + rows]
                exponent = jnp.exp(masked - jnp.max(masked, axis=0, keepdims=True))
                part = exponent * (1.0 / jnp.sum(exponent, axis=0, keepdims=True))
                part = part.astype(low)
                probs[2 * pair + half, start : start + rows] = part
                weights.append(part)
            behind = (pair, weights)
        mix(*behind)

    def forward_micro(micro, _):
        def before_write(left_indices, keep_indices):
            @pl.when(micro > 0)
            def _():
                for index in left_indices:
                    left_out(index, micro - 1).wait()
                for index in keep_indices:
                    keep_out(index, micro - 1).wait()

        def after_write(left_indices, keep_indices):
            for index in left_indices:
                left_out(index, micro).start()

            @pl.when(micro < last)
            def _():
                for index in keep_indices:
                    keep_out(index, micro).start()

        def weight_ready(index):
            @pl.when(micro == 0)
            def _():
                weight_loads[index].wait()

        length = lengths[micro, 0]
        for block in range(block_count):
            start, rows = score_rows(block)
            key_pos = lax.broadcasted_iota(jnp.int32, (rows, query_rows), 0)
            query_pos = block * query_rows + lax.broadcasted_iota(
                jnp.int32, (rows, query_rows), 1
            )
            allowed = (key_pos <= query_pos) & (key_pos < length)
            mask[start : start + rows] = jnp.where(allowed, 0.0, masked_score)

        @pl.when(first)
        def _():
            input_load(micro).wait()

        for block in range(block_count):
            span = block_span(block)
            final = block == block_count - 1

            @pl.when(second)
            def _():
                onward(source, 0, micro, block).wait_recv()

            if block == 0:
                before_write((0,), (0, 1))
            normal_one, inverse_one = normalize(source[micro, span].astype(wide))
            normal[span] = normal_one.astype(low)
            inverse[span] = jnp.broadcast_to(inverse_one, (query_rows, inverse.shape[1]))
            normed[span] = (normal_one * attend_gain[...] + attend_shift[...]).astype(low)
            if final:
                after_write((0,), (0, 1))
            if block == 0:
                before_write((), (2,))
                weight_ready(0)
            for part in range(3):
                columns = slice(part * width, (part + 1) * width)
                piece = product(normed[span], joint_w[:, columns])
                if part == 0:
                    piece = piece + joint_bias[:, :width]
                elif part == 2:
                    piece = piece + joint_bias[:, width:]
                joint[span, columns] = piece.astype(low)
            if final:
                after_write((), (2,))
            if block == 0:
                before_write((1,), (3,))
            attend_block(block)
            if final:
                after_write((1,), (3,))
            if block == 0:
                before_write((2,), (4, 5))
                weight_ready(1)
            middle[span] = source[micro, span].astype(wide) + branch_scale * (
                product(attended[span], project_w[...]) + project_bias[...]
            )
            normal_both, inverse_both = normalize(middle[span])
            normal_two[span] = normal_both.astype(low)
            inverse_two[span] = jnp.broadcast_to(inverse_both, (query_rows, inverse.shape[1]))
            normed_two[span] = (normal_both * feed_gain[...] + feed_shift[...]).astype(low)
            if final:
                after_write((2,), (4, 5))
            if block == 0:
                before_write((3,), (6,))
                weight_ready(2)
            for part in range(hidden_width // width):
                columns = slice(part * width, (part + 1) * width)
                hidden = product(normed_two[span], expand_w[:, columns]) + expand_bias[:, columns]
                square = hidden * hidden
                inner = jnp.tanh(hidden * (gelu_scale + (gelu_scale * gelu_cubic) * square))
                gate = 0.5 + 0.5 * inner
                value = hidden * gate
                active[span, columns] = value.astype(low)
                slope[span, columns] = (
                    gate
                    + value
                    * (1.0 - inner)
                    * (gelu_scale + (3.0 * gelu_scale * gelu_cubic) * square)
                ).astype(low)
            if final:
                after_write((3,), (6,))
            if block == 0:
                weight_ready(3)
            result[micro, span] = (
                middle[span]
                + branch_scale * (product(active[span], shrink_w[...]) + shrink_bias[...])
            ).astype(low)

            @pl.when(first)
            def _():
                onward(source, 0, micro, block).start()

        result_out(micro).start()
        return 0

    lax.fori_loop(0, micro_count, forward_micro, 0)
    for micro in range(micro_count):
        result_out(micro).wait()

    @pl.when(first)
    def _():
        for micro in range(micro_count):
            for block in range(block_count):
                onward(source, 0, micro, block).wait_send()

    def add_sum(row, values):
        small[row : row + 1] += jnp.sum(values, axis=0, keepdims=True)

    def attend_block_back(block):
        start, rows = score_rows(block)
        span = block_span(block)
        bottom = block == block_count - 1

        def weight_grad_of(pair):
            values = half_stack(joint[:rows, pair_columns(2, pair)], 1.0)
            return back_product(values, attended_grad[span, pair_columns(0, pair)])

        lane = lax.broadcasted_iota(jnp.int32, (1, pair_width), 1)
        upper = lane >= head_width
        ahead = weight_grad_of(0)
        for pair in range(pair_count):
            weight_grad = ahead
            if pair + 1 < pair_count:
                ahead = weight_grad_of(pair + 1)
            flat = pair_columns(0, pair)
            query = joint[span, flat]
            keys = flipped(joint[:rows, pair_columns(1, pair)]).astype(low)
            out_grad = attended_grad[span, flat]
            inner = (out_grad.astype(wide) * attended[span, flat].astype(wide)).T
            key_halves, value_halves, query_halves = [], [], []
            for half in range(2):
                head = slice(half * head_width, (half + 1) * head_width)
                delta = jnp.sum(inner[head], axis=0, keepdims=True)
                weights = probs[2 * pair + half, start : start + rows]
                score_grad = (
                    weights.astype(wide)
                    * (weight_grad[half * rows : (half + 1) * rows] - delta)
                ).astype(low)
                value_halves.append(product(weights, out_grad))
                key_halves.append(product(score_grad, query))
                query_halves.append(product(keys[head], score_grad))
            joint_grad[span, flat] = (
                jnp.concatenate(query_halves, axis=0).T * head_scale
            ).astype(low)
            key_grad = jnp.where(upper, key_halves[1], key_halves[0]) * head_scale
            value_grad = jnp.where(upper, value_halves[1], value_halves[0])
            done = rows - query_rows
            key_done, value_done = key_grad[done:], value_grad[done:]
            if not bottom:
                key_done = key_done + key_part[done:rows, flat]
                value_done = value_done + value_part[done:rows, flat]
            joint_grad[span, pair_columns(1, pair)] = key_done.astype(low)
            joint_grad[span, pair_columns(2, pair)] = value_done.astype(low)
            if done:
                if bottom:
                    key_part[:done, flat] = key_grad[:done]
                    value_part[:done, flat] = value_grad[:done]
                else:
                    key_part[:done, flat] += key_grad[:done]
                    value_part[:done, flat] += value_grad[:done]

    def backward_micro(step, _):
        micro = last - step

        def before_write(index):
            @pl.when(step > 0)
            def _():
                grad_out(index, micro + 1).wait()

        def loaded(*indices):
            @pl.when(step > 0)
            def _():
                for index in indices:
                    keep_load(index, micro).wait()

        def load_next(*indices):
            @pl.when(micro > 0)
            def _():
                for index in indices:
                    keep_load(index, micro - 1).start()

        last_row = jnp.where(first, seq_rows, lengths[micro, 0])

        @pl.when(second)
        def _():
            cotangent_load(micro).wait()

        for block in reversed(range(block_count)):
            span = block_span(block)
            opening = block == block_count - 1
            closing = block == 0

            @pl.when(first)
            def _():
                onward(top_grad, 1, micro, block).wait_recv()

            row_pos = block * query_rows + lax.broadcasted_iota(jnp.int32, (query_rows, 1), 0)
            output_grad = jnp.where(row_pos < last_row, top_grad[micro, span].astype(wide), 0.0)
            if opening:
                before_write(0)
            shrink_low = (branch_scale * output_grad).astype(low)
            shrink_grad[span] = shrink_low
            add_sum(5, shrink_low.astype(wide))
            middle[span] = output_grad
            if closing:
                grad_out(0, micro).start()
            if opening:
                before_write(1)
                loaded(6)
            for part in range(hidden_width // width):
                columns = slice(part * width, (part + 1) * width)
                grad = back_product(shrink_grad[span], shrink_w[columns, :])
                grad_low = (grad * slope[span, columns].astype(wide)).astype(low)
                hidden_grad[span, columns] = grad_low
                add_sum(8 + part, grad_low.astype(wide))
            if closing:
                load_next(6)
                grad_out(1, micro).start()
            normed_grad = back_product(hidden_grad[span], expand_w[...])
            if opening:
                loaded(4, 5)
            normal_wide = normal_two[span].astype(wide)
            add_sum(3, normed_grad * normal_wide)
            add_sum(4, normed_grad)
            middle[span] += norm_slope(
                normed_grad * feed_gain[...], normal_wide, inverse_two[span, :1]
            )
            if closing:
                load_next(4, 5)
            if opening:
                before_write(2)
            branch_low = (branch_scale * middle[span]).astype(low)
            branch_grad[span] = branch_low
            add_sum(2, branch_low.astype(wide))
            if closing:
                grad_out(2, micro).start()
            attended_grad[span] = back_product(branch_grad[span], project_w[...]).astype(low)
            if opening:
                before_write(3)
                loaded(2, 3, 7)
            attend_block_back(block)
            if closing:
                load_next(2, 3, 7)
                grad_out(3, micro).start()
            add_sum(6, joint_grad[span, :width].astype(wide))
            add_sum(7, joint_grad[span, 2 * width :].astype(wide))
            normed_grad = back_product(joint_grad[span], joint_w[...])
            if opening:
                before_write(4)
                loaded(0, 1)
            normal_wide = normal[span].astype(wide)
            add_sum(0, normed_grad * normal_wide)
            add_sum(1, normed_grad)
            total = middle[span] + norm_slope(
                normed_grad * attend_gain[...], normal_wide, inverse[span, :1]
            )
            if closing:
                load_next(0, 1)
            source_grad[span] = total
            result[micro, span] = total.astype(low)

            @pl.when(second)
            def _():
                onward(top_grad, 1, micro, block).start()

        grad_out(4, micro).start()
        return 0

    left_out(1, last).wait()
    lax.fori_loop(0, micro_count, backward_micro, 0)
    for index in (0, 2, 3):
        left_out(index, last).wait()
    for index in range(len(grads)):
        grad_out(index, 0).wait()

    @pl.when(second)
    def _():
        for micro in range(micro_count):
            for block in range(block_count):
                onward(top_grad, 1, micro, block).wait_send()


def run_sections(lengths, inputs, cotangent, weights):
    micro_count, seq_rows, width = inputs.shape
    hidden = weights["expand_weight"].shape[1]
    heads = width // head_width
    tokens = micro_count * seq_rows
    blocks = seq_rows // query_rows
    score_total = score_rows(blocks)[0]
    small_rows = -(-(8 + hidden // width) // 8) * 8
    hbm = pl.BlockSpec(memory_space=pl.ANY)
    vmem = pl.BlockSpec(memory_space=pltpu.VMEM)

    def row(name):
        return weights[name].reshape(1, -1)

    def shape(*dims, kind=low):
        return jax.ShapeDtypeStruct(dims, kind)

    return pl.pallas_call(
        sections_kernel,
        name="sections",
        out_shape=(
            shape(micro_count, seq_rows, width),
            shape(tokens, width, kind=wide),
            shape(tokens, width),
            shape(tokens, width),
            shape(tokens, width),
            shape(tokens, hidden),
            shape(tokens, width),
            shape(tokens, hidden),
            shape(tokens, 3 * width),
            shape(tokens, width),
            shape(small_rows, width, kind=wide),
            shape(micro_count, seq_rows, width),
            shape(micro_count, seq_rows, 128, kind=wide),
            shape(micro_count, seq_rows, 3 * width),
            shape(micro_count, heads, score_total, query_rows),
            shape(micro_count, seq_rows, width),
            shape(micro_count, seq_rows, 128, kind=wide),
            shape(micro_count, seq_rows, hidden),
        ),
        in_specs=[pl.BlockSpec(memory_space=pltpu.SMEM)] + [hbm] * 6 + [vmem] * 8,
        out_specs=tuple([hbm] * 10 + [vmem] + [hbm] * 7),
        scratch_shapes=[
            pltpu.VMEM((width, 3 * width), low),
            pltpu.VMEM((width, width), low),
            pltpu.VMEM((width, hidden), low),
            pltpu.VMEM((hidden, width), low),
            pltpu.VMEM((micro_count, seq_rows, width), low),
            pltpu.VMEM((micro_count, seq_rows, width), low),
            pltpu.VMEM((micro_count, seq_rows, width), low),
            pltpu.VMEM((seq_rows, width), low),
            pltpu.VMEM((seq_rows, width), low),
            pltpu.VMEM((seq_rows, 128), wide),
            pltpu.VMEM((seq_rows, 3 * width), low),
            pltpu.VMEM((heads, score_total, query_rows), low),
            pltpu.VMEM((seq_rows, width), low),
            pltpu.VMEM((seq_rows, width), wide),
            pltpu.VMEM((seq_rows, width), low),
            pltpu.VMEM((seq_rows, width), low),
            pltpu.VMEM((seq_rows, 128), wide),
            pltpu.VMEM((seq_rows, hidden), low),
            pltpu.VMEM((seq_rows, hidden), low),
            pltpu.VMEM((score_total, query_rows), wide),
            pltpu.VMEM((seq_rows, width), low),
            pltpu.VMEM((seq_rows, hidden), low),
            pltpu.VMEM((seq_rows, 3 * width), low),
            pltpu.VMEM((seq_rows, width), low),
            pltpu.VMEM((seq_rows, width), low),
            pltpu.VMEM((seq_rows, width), wide),
            pltpu.VMEM((max(seq_rows - query_rows, 8), width), wide),
            pltpu.VMEM((max(seq_rows - query_rows, 8), width), wide),
            pltpu.SemaphoreType.DMA((4,)),
            pltpu.SemaphoreType.DMA((micro_count,)),
            pltpu.SemaphoreType.DMA((micro_count, blocks)),
            pltpu.SemaphoreType.DMA((micro_count, blocks)),
            pltpu.SemaphoreType.DMA((micro_count,)),
            pltpu.SemaphoreType.DMA((4,)),
            pltpu.SemaphoreType.DMA((8,)),
            pltpu.SemaphoreType.DMA((8,)),
            pltpu.SemaphoreType.DMA((5,)),
        ],
        compiler_params=pltpu.CompilerParams(
            collective_id=1, has_side_effects=True, vmem_limit_bytes=62 * 2**20
        ),
    )(
        lengths,
        inputs,
        cotangent,
        weights["joint_weight"],
        weights["project_weight"],
        weights["expand_weight"],
        weights["shrink_weight"],
        row("attend_gain"),
        row("attend_shift"),
        row("joint_bias"),
        row("project_bias"),
        row("feed_gain"),
        row("feed_shift"),
        row("expand_bias"),
        row("shrink_bias"),
    )


def axis_bits(count):
    bits = []
    step = 1
    while step < count:
        bits.append(step)
        step *= 2
    assert step == count
    return bits


line_length = 4


def line_place():
    return (lax.axis_index("dp") // 2) % line_length


def exchange_bits(dp_count, sub_count):
    bits = [("dp", step) for step in axis_bits(dp_count)]
    near, line, beyond = bits[0], bits[1:3], bits[3:]
    assert len(line) == 2 and sub_count == 2
    return near, ("sub", 1), line, beyond


def partner_id(bit):
    axis, step = bit
    place = {name: lax.axis_index(name) for name in ("pipe", "dp", "sub")}
    place[axis] = place[axis] ^ step
    return (place["pipe"], place["dp"], place["sub"])


def own_bit(bit):
    axis, step = bit
    return (lax.axis_index(axis) // step) % 2


def grad_blocks(width, hidden):
    blocks = []
    for row in range(hidden // block_rows):
        for column in range(width // block_cols):
            blocks.append((0, row, column))
    for column in range(hidden // block_cols):
        blocks.append((1, 0, column))
    for column in range(3 * width // block_cols):
        blocks.append((2, 0, column))
    for column in range(width // block_cols):
        blocks.append((3, 0, column))
    return blocks


opening_ticks = ((1, 3, 5, 7, 9, 11), (1, 3, 5, 7, 9, 11), (0, 0, 3, 9, 11, 12))
group_size = 2


def exchange_groups():
    groups = []
    for kind, ticks in enumerate(opening_ticks):
        for number, tick in enumerate(ticks):
            groups.append((kind + number % 2 if kind == 2 else kind, tick))
    return sorted(groups, key=lambda group: group[1])


def kind_steps(kind, near, sub, beyond):
    line = [("line", turn) for turn in range(line_length - 1)]
    halves = [("half", sub), ("half", near)] if kind in (1, 3) else [("half", near), ("half", sub)]
    there = halves + line if kind < 2 else line + halves
    there = there + [("whole", bit) for bit in beyond]
    return there


def arrival_rows(steps):
    rows, places, start, line_rows = block_rows, [], 0, 0
    for name, turn in steps:
        if name == "half":
            rows //= 2
            places.append((start, rows))
            start += rows
        elif name == "line":
            if turn == 0:
                line_rows = rows // line_length
                rows = line_rows
            places.append((start, line_rows))
            start += line_rows * (1 if turn == 0 else 2)
        else:
            places.append((start, rows))
            start += rows
    return places, start


def rows_at(offset, rows):
    return pl.ds(pl.multiple_of(offset, 16), rows)


class Exchange:
    def __init__(self, bits, groups, own, arrivals, send_sems, recv_sems, free_sems):
        near, sub, _, beyond = bits
        self.groups, self.own, self.arrivals = groups, own, arrivals
        self.send_sems, self.recv_sems, self.free_sems = send_sems, recv_sems, free_sems
        self.place = line_place()
        self.there = [kind_steps(kind, near, sub, beyond) for kind in range(4)]
        self.there_count = len(self.there[0])
        self.total_steps = 2 * self.there_count - len(beyond)
        self.arrival_places = [arrival_rows(steps)[0] for steps in self.there]
        self.starts = []
        start = 0
        for kind, _ in groups:
            self.starts.append(start)
            start += arrival_rows(self.there[kind])[1]
        self.offsets = []
        for steps in self.there:
            offset, rows, places = 0, block_rows, []
            for name, what in steps:
                if name == "half":
                    half = rows // 2
                    mine = own_bit(what)
                    keep = offset + mine * half
                    places.append((keep, offset + (1 - mine) * half, half))
                    offset, rows = keep, half
                elif name == "line":
                    if what == 0:
                        line_start, rows = offset, rows // line_length
                        offset = line_start + self.place * rows
                    places.append((line_start, line_start, rows))
                else:
                    places.append((offset, offset, rows))
            self.offsets.append(places)

    def step_of(self, index, step):
        kind = self.groups[index][0]
        if step < self.there_count:
            return kind, step, False
        beyond = self.total_steps - 2 * self.there_count
        return kind, self.there_count - 1 + beyond - (step - self.there_count), True

    def rows(self, index, offset, rows):
        return self.own.at[pl.ds(group_size * index, group_size), rows_at(offset, rows)]

    def copy(self, index, step, side, source, target, device):
        return pltpu.make_async_remote_copy(
            src_ref=source,
            dst_ref=target,
            send_sem=self.send_sems.at[index, step, side],
            recv_sem=self.recv_sems.at[index, step, side],
            device_id=device,
            device_id_type=MESH,
        )

    def arrival(self, index, there, side):
        kind = self.groups[index][0]
        start, rows = self.arrival_places[kind][there]
        name, turn = self.there[kind][there]
        if name == "line" and turn > 0:
            start += side * rows
        return self.arrivals.at[:, pl.ds(self.starts[index] + start, rows)]

    def neighbour(self, side):
        shift = 2 if side else -2
        return (lax.axis_index("pipe"), lax.axis_index("dp") + shift, lax.axis_index("sub"))

    def line_sends(self, turn, back):
        place, top = self.place, line_length - 1
        if back:
            down = ((place + turn <= top) & (place > 0), place + turn)
            up = ((place - turn >= 0) & (place < top), place - turn)
        else:
            down = ((place >= top - turn) & (place > 0), place - top + turn)
            up = ((place <= turn) & (place < top), place + top - turn)
        return down, up

    def line_gets(self, turn, back):
        place, top = self.place, line_length - 1
        if back:
            below = ((place >= 1) & (place - 1 - turn >= 0), place - 1 - turn)
            above = ((place < top) & (place + 1 + turn <= top), place + 1 + turn)
        else:
            below = ((place >= 1) & (place - 1 <= turn), place + top - 1 - turn)
            above = ((place < top) & (place + 1 >= top - turn), place + 1 - top + turn)
        return below, above

    def line_copy(self, index, step, side, shard):
        kind, there, back = self.step_of(index, step)
        start, _, rows = self.offsets[kind][there]
        source = self.rows(index, start + shard * rows, rows)
        target = source if back else self.arrival(index, there, 1 - side)
        return pltpu.make_async_remote_copy(
            src_ref=source,
            dst_ref=target,
            send_sem=self.send_sems.at[index, step, side],
            recv_sem=self.recv_sems.at[index, step, 1 - side],
            device_id=self.neighbour(side),
            device_id_type=MESH,
        )

    def line_landing(self, index, step, side, shard):
        kind, there, back = self.step_of(index, step)
        start, _, rows = self.offsets[kind][there]
        place = self.rows(index, start + shard * rows, rows)
        target = place if back else self.arrival(index, there, side)
        return self.copy(index, step, side, place, target, self.neighbour(side))

    def pair_copy(self, index, step, landing):
        kind, there, back = self.step_of(index, step)
        keep, give, rows = self.offsets[kind][there]
        bit = self.there[kind][there][1]
        if back:
            source = self.rows(index, keep, rows)
            target = self.rows(index, give if landing else keep, rows)
        else:
            source = self.rows(index, give, rows)
            target = self.arrival(index, there, 0)
        return self.copy(index, step, 0, source, target, partner_id(bit))

    def add(self, index, there, side, offset, rows):
        total = self.rows(index, offset, rows)
        arrived = self.arrival(index, there, side)
        for member in range(group_size):
            total[member] = (
                total[member].astype(jnp.float32) + arrived[member].astype(jnp.float32)
            ).astype(jnp.bfloat16)

    def send(self, index, step):
        kind, there, back = self.step_of(index, step)
        name, what = self.there[kind][there]
        if name != "line":
            if back:
                pl.semaphore_wait(self.free_sems.at[index, there, 0], 1)
            self.pair_copy(index, step, False).start()
            return
        turn = line_length - 2 - what if back else what
        for side, (sends, shard) in enumerate(self.line_sends(turn, back)):

            @pl.when(sends)
            def _():
                if back:
                    pl.semaphore_wait(self.free_sems.at[index, there, side], 1)
                self.line_copy(index, step, side, shard).start()

    def receive(self, index, step):
        kind, there, back = self.step_of(index, step)
        name, what = self.there[kind][there]
        start, _, rows = self.offsets[kind][there]
        if name != "line":
            self.pair_copy(index, step, True).wait()
            if not back:
                self.add(index, there, 0, start, rows)
                if name == "half":
                    pl.semaphore_signal(
                        self.free_sems.at[index, there, 0],
                        inc=1,
                        device_id=partner_id(what),
                        device_id_type=MESH,
                    )
            return
        turn = line_length - 2 - what if back else what
        for side, (sends, shard) in enumerate(self.line_sends(turn, back)):

            @pl.when(sends)
            def _():
                self.line_copy(index, step, side, shard).wait_send()
                if not back:
                    pl.semaphore_signal(
                        self.free_sems.at[index, there, 1 - side],
                        inc=1,
                        device_id=self.neighbour(side),
                        device_id_type=MESH,
                    )

        for side, (gets, shard) in enumerate(self.line_gets(turn, back)):

            @pl.when(gets)
            def _():
                self.line_landing(index, step, side, shard).wait_recv()
                if not back:
                    self.add(index, there, side, start + shard * rows, rows)

    def advance(self, index, step):
        self.receive(index, step - 1)
        if step < self.total_steps:
            self.send(index, step)


def sum_kernel(bits, blocks, *refs):
    lefts, rights, small_in = refs[0:4], refs[4:8], refs[8]
    own, small_out = refs[9:11]
    left_bufs, right_bufs = refs[11:15], refs[15:19]
    arrivals, send_sems, recv_sems, free_sems = refs[19:23]
    small, small_got, load_sems, small_send, small_recv = refs[23:]
    near, sub, line, beyond = bits
    pairs = (near, sub, *line, *beyond)
    stage_count = len(pairs)

    loads = []
    for index in range(4):
        left_load = pltpu.make_async_copy(lefts[index], left_bufs[index], load_sems.at[2 * index])
        right_load = pltpu.make_async_copy(
            rights[index], right_bufs[index], load_sems.at[2 * index + 1]
        )
        left_load.start()
        right_load.start()
        loads.append((left_load, right_load))
    loaded = [False] * 4

    groups = exchange_groups()
    exchange = Exchange(bits, groups, own, arrivals, send_sems, recv_sems, free_sems)
    place = line_place()
    barrier = pltpu.get_barrier_semaphore()
    for bit in pairs:
        pl.semaphore_signal(barrier, inc=1, device_id=partner_id(bit), device_id_type=MESH)
    for side, near_end in enumerate((place > 0, place < line_length - 1)):

        @pl.when(near_end)
        def _():
            pl.semaphore_signal(
                barrier, inc=1, device_id=exchange.neighbour(side), device_id_type=MESH
            )

    ends = jnp.where((place == 0) | (place == line_length - 1), 1, 2)
    pl.semaphore_wait(barrier, stage_count + ends)

    def produce(block):
        index, row, column = blocks[block]
        if not loaded[index]:
            loads[index][0].wait()
            loads[index][1].wait()
            loaded[index] = True
        left = left_bufs[index][:, row * block_rows : (row + 1) * block_rows]
        right = right_bufs[index][:, column * block_cols : (column + 1) * block_cols]
        own[block] = lax.dot_general(
            left, right, (((0,), (0,)), ((), ())), preferred_element_type=jnp.float32
        ).astype(jnp.bfloat16)

    def small_copy(stage):
        return pltpu.make_async_remote_copy(
            src_ref=small.at[stage],
            dst_ref=small_got.at[stage],
            send_sem=small_send.at[stage],
            recv_sem=small_recv.at[stage],
            device_id=partner_id(pairs[stage]),
            device_id_type=MESH,
        )

    last = max(tick for _, tick in groups) + exchange.total_steps
    for tick in range(last + 1):
        for index, (kind, begin) in enumerate(groups):
            if begin == tick:
                for block in range(group_size * index, group_size * (index + 1)):
                    produce(block)
                exchange.send(index, 0)
        if tick == 0:
            small[0] = small_in[...]
        elif tick <= stage_count:
            small_copy(tick - 1).wait()
            total = small[tick - 1] + small_got[tick - 1]
            if tick < stage_count:
                small[tick] = total
            else:
                small_out[...] = total
        if tick < stage_count:
            small_copy(tick).start()
        for step in range(1, exchange.total_steps + 1):
            for index, (kind, begin) in enumerate(groups):
                if begin + step == tick:
                    exchange.advance(index, step)


def summed_grads(lefts, rights, small, dp_count, sub_count):
    tokens, width = lefts[3].shape
    hidden = lefts[0].shape[1]
    bits = exchange_bits(dp_count, sub_count)
    near, sub, line, beyond = bits
    stage_count = 2 + len(line) + len(beyond)
    blocks = grad_blocks(width, hidden)
    block_count = len(blocks)
    groups = exchange_groups()
    assert group_size * len(groups) == block_count
    there = kind_steps(0, near, sub, beyond)
    steps = 2 * len(there) - len(beyond)
    rows = sum(arrival_rows(kind_steps(kind, near, sub, beyond))[1] for kind, _ in groups)
    low = jnp.bfloat16
    hbm = pl.BlockSpec(memory_space=pl.ANY)
    vmem = pl.BlockSpec(memory_space=pltpu.VMEM)
    return pl.pallas_call(
        functools.partial(sum_kernel, bits, blocks),
        name="grad_sums",
        out_shape=(
            pltpu.VMEM((block_count, block_rows, block_cols), low),
            pltpu.VMEM(small.shape, jnp.float32),
        ),
        in_specs=[hbm] * 8 + [vmem],
        out_specs=(vmem, vmem),
        scratch_shapes=[pltpu.VMEM(array.shape, low) for array in lefts]
        + [pltpu.VMEM(array.shape, low) for array in rights]
        + [
            pltpu.VMEM((group_size, rows, block_cols), low),
            pltpu.SemaphoreType.DMA((len(groups), steps, 2)),
            pltpu.SemaphoreType.DMA((len(groups), steps, 2)),
            pltpu.SemaphoreType.REGULAR((len(groups), len(there), 2)),
            pltpu.VMEM((stage_count, *small.shape), jnp.float32),
            pltpu.VMEM((stage_count, *small.shape), jnp.float32),
            pltpu.SemaphoreType.DMA((8,)),
            pltpu.SemaphoreType.DMA((stage_count,)),
            pltpu.SemaphoreType.DMA((stage_count,)),
        ],
        compiler_params=pltpu.CompilerParams(
            collective_id=0, has_side_effects=True, vmem_limit_bytes=46 * 2**20
        ),
    )(*lefts, *rights, small)


stage_count_out = 6


def finish_kernel(
    blocks,
    own,
    small,
    outputs_in,
    grads_in,
    outputs,
    input_grads,
    attend_gain,
    attend_shift,
    joint,
    joint_bias,
    project,
    project_bias,
    feed_gain,
    feed_shift,
    expand,
    expand_bias,
    shrink,
    shrink_bias,
    stages,
    stage_sems,
    pass_sems,
):
    places = (shrink, expand, joint, project)
    width = shrink_bias.shape[1]
    passes = [
        pltpu.make_async_copy(outputs_in, outputs, pass_sems.at[0]),
        pltpu.make_async_copy(grads_in, input_grads, pass_sems.at[1]),
    ]
    for copy in passes:
        copy.start()

    def block_copy(block):
        index, row, column = blocks[block]
        slot = block % stage_count_out
        return pltpu.make_async_copy(
            stages.at[slot],
            places[index].at[
                pl.ds(row * block_rows, block_rows), pl.ds(column * block_cols, block_cols)
            ],
            stage_sems.at[slot],
        )

    for block in range(len(blocks)):
        if block >= stage_count_out:
            block_copy(block - stage_count_out).wait()
        stages[block % stage_count_out] = own[block].astype(jnp.float32)
        block_copy(block).start()
    for row, place in (
        (0, attend_gain),
        (1, attend_shift),
        (2, project_bias),
        (3, feed_gain),
        (4, feed_shift),
        (5, shrink_bias),
        (6, joint_bias),
        (8, expand_bias),
    ):
        for part in range(place.shape[1] // width):
            place[:, part * width : (part + 1) * width] = small[row + part : row + part + 1]
    for block in range(max(0, len(blocks) - stage_count_out), len(blocks)):
        block_copy(block).wait()
    for copy in passes:
        copy.wait()


def finished(own, small, outputs, input_grads, width, hidden):
    blocks = grad_blocks(width, hidden)
    hbm = pl.BlockSpec(memory_space=pl.ANY)
    vmem = pl.BlockSpec(memory_space=pltpu.VMEM)

    def shape(*dims):
        return jax.ShapeDtypeStruct(dims, jnp.float32)

    return pl.pallas_call(
        functools.partial(finish_kernel, blocks),
        name="finish",
        out_shape=(
            jax.ShapeDtypeStruct(outputs.shape, outputs.dtype),
            jax.ShapeDtypeStruct(input_grads.shape, input_grads.dtype),
            shape(1, width),
            shape(1, width),
            shape(width, 3 * width),
            shape(1, 2 * width),
            shape(width, width),
            shape(1, width),
            shape(1, width),
            shape(1, width),
            shape(width, hidden),
            shape(1, hidden),
            shape(hidden, width),
            shape(1, width),
        ),
        in_specs=[vmem, vmem, hbm, hbm],
        out_specs=(
            hbm, hbm, vmem, vmem, hbm, vmem, hbm, vmem, vmem, vmem, hbm, vmem, hbm, vmem
        ),
        scratch_shapes=[
            pltpu.VMEM((stage_count_out, block_rows, block_cols), jnp.float32),
            pltpu.SemaphoreType.DMA((stage_count_out,)),
            pltpu.SemaphoreType.DMA((2,)),
        ],
        compiler_params=pltpu.CompilerParams(vmem_limit_bytes=16 * 2**20),
    )(
        pltpu.with_memory_space_constraint(own, pltpu.VMEM),
        pltpu.with_memory_space_constraint(small, pltpu.VMEM),
        outputs,
        input_grads,
    )


weight_names = (
    "attend_gain",
    "attend_shift",
    "joint_weight",
    "joint_bias",
    "project_weight",
    "project_bias",
    "feed_gain",
    "feed_shift",
    "expand_weight",
    "expand_bias",
    "shrink_weight",
    "shrink_bias",
)


def body(inputs, cotangent, lengths, *params):
    weights = {name: param[0] for name, param in zip(weight_names, params)}
    micro_count, _, seq_rows, width = inputs.shape
    (
        outputs,
        input_grads,
        normed,
        attended,
        normed_two,
        active,
        shrink_grad,
        hidden_grad,
        joint_grad,
        branch_grad,
        small,
        *_,
    ) = run_sections(lengths, inputs[:, 0], cotangent[:, 0], weights)
    hidden = active.shape[1]
    own, small_sum = summed_grads(
        (active, normed_two, normed, attended),
        (shrink_grad, hidden_grad, joint_grad, branch_grad),
        small,
        lax.axis_size("dp"),
        lax.axis_size("sub"),
    )
    outputs, input_grads, *full_grads = finished(
        own, small_sum, outputs, input_grads, width, hidden
    )
    return (
        outputs[None, :, None],
        input_grads.reshape(1, micro_count, 1, seq_rows, width),
        *(grad if grad.shape[0] == 1 else grad[None] for grad in full_grads),
    )


def solution(mesh):
    in_specs = (
        P(None, ("dp", "sub"), None, None),
        P(None, ("dp", "sub"), None, None),
        P(None, ("dp", "sub")),
        P("pipe", None),
        P("pipe", None),
        P("pipe", None, None),
        P("pipe", None),
        P("pipe", None, None),
        P("pipe", None),
        P("pipe", None),
        P("pipe", None),
        P("pipe", None, None),
        P("pipe", None),
        P("pipe", None, None),
        P("pipe", None),
    )
    out_specs = (
        P("pipe", None, ("dp", "sub"), None, None),
        P("pipe", None, ("dp", "sub"), None, None),
        P("pipe", None),
        P("pipe", None),
        P("pipe", None, None),
        P("pipe", None),
        P("pipe", None, None),
        P("pipe", None),
        P("pipe", None),
        P("pipe", None),
        P("pipe", None, None),
        P("pipe", None),
        P("pipe", None, None),
        P("pipe", None),
    )
    return jax.shard_map(body, mesh=mesh, in_specs=in_specs, out_specs=out_specs, check_vma=False)
```

```python
import functools

import jax
import jax.numpy as jnp
from jax import lax
from jax.experimental import pallas as pl
from jax.experimental.pallas import tpu as pltpu
from jax.sharding import PartitionSpec as P

MESH = pl.DeviceIdType.MESH
branch_scale = 24.0 ** (-0.5)
head_scale = 0.125
norm_eps = 1e-05
gelu_scale = (2.0 / 3.141592653589793) ** 0.5
gelu_cubic = 0.044715
masked_score = -1e30
low = jnp.bfloat16
wide = jnp.float32
head_width = 64
pair_width = 128
query_rows = 256
block_rows = 768
block_cols = 256


def product(left, right):
    return jnp.dot(left, right, preferred_element_type=wide)


def back_product(left, right):
    return lax.dot_general(left, right, (((1,), (1,)), ((), ())), preferred_element_type=wide)


def flipped(matrix):
    return matrix.astype(wide).T


def sibling():
    return (1 - lax.axis_index("pipe"), lax.axis_index("dp"), lax.axis_index("sub"))


def greet_sibling():
    barrier = pltpu.get_barrier_semaphore()
    pl.semaphore_signal(barrier, inc=1, device_id=sibling(), device_id_type=MESH)
    pl.semaphore_wait(barrier, 1)


def pair_mask(half, value):
    lane = lax.broadcasted_iota(jnp.int32, (1, pair_width), 1)
    return jnp.where((lane // head_width) == half, value, 0.0).astype(low)


def score_rows(block):
    first = query_rows * (block * (block + 1) // 2)
    return first, query_rows * (block + 1)


def normalize(values):
    center = values - jnp.mean(values, axis=-1, keepdims=True)
    inverse = lax.rsqrt(jnp.mean(center * center, axis=-1, keepdims=True) + norm_eps)
    return center * inverse, inverse


def norm_slope(graded, normal, inverse):
    return inverse * (
        graded
        - jnp.mean(graded, axis=-1, keepdims=True)
        - normal * jnp.mean(graded * normal, axis=-1, keepdims=True)
    )


def half_stack(matrix, value):
    return jnp.concatenate(
        [matrix * pair_mask(0, value), matrix * pair_mask(1, value)], axis=0
    )


def sections_kernel(
    lengths_in,
    inputs,
    cotangent,
    joint_weight,
    project_weight,
    expand_weight,
    shrink_weight,
    attend_gain,
    attend_shift,
    joint_bias,
    project_bias,
    feed_gain,
    feed_shift,
    expand_bias,
    shrink_bias,
    outputs,
    input_grads,
    normed_out,
    attended_out,
    normed_two_out,
    active_out,
    shrink_grad_out,
    hidden_grad_out,
    joint_grad_out,
    branch_grad_out,
    small,
    normal_out,
    inverse_out,
    joint_out,
    probs_out,
    normal_two_out,
    inverse_two_out,
    slope_out,
    joint_w,
    project_w,
    expand_w,
    shrink_w,
    source,
    result,
    top_grad,
    normed,
    normal,
    inverse,
    joint,
    probs,
    attended,
    middle,
    normed_two,
    normal_two,
    inverse_two,
    active,
    slope,
    mask,
    shrink_grad,
    hidden_grad,
    joint_grad,
    branch_grad,
    attended_grad,
    source_grad,
    key_part,
    value_part,
    weight_sems,
    source_sems,
    send_sems,
    recv_sems,
    result_sems,
    left_sems,
    keep_sems,
    load_sems,
    grad_sems,
    lengths,
    lengths_sem,
):
    first = lax.axis_index("pipe") == 0
    second = jnp.logical_not(first)
    micro_count, seq_rows, width = source.shape
    hidden_width = expand_w.shape[1]
    pair_count = width // pair_width
    block_count = seq_rows // query_rows
    last = micro_count - 1
    weight_loads = [
        pltpu.make_async_copy(place, buffer, weight_sems.at[index])
        for index, (place, buffer) in enumerate(
            (
                (joint_weight, joint_w),
                (project_weight, project_w),
                (expand_weight, expand_w),
                (shrink_weight, shrink_w),
            )
        )
    ]
    lefts = (
        (normed, normed_out),
        (attended, attended_out),
        (normed_two, normed_two_out),
        (active, active_out),
    )
    kept = (
        (normal, normal_out),
        (inverse, inverse_out),
        (joint, joint_out),
        (probs, probs_out),
        (normal_two, normal_two_out),
        (inverse_two, inverse_two_out),
        (slope, slope_out),
        (attended, attended_out),
    )
    grads = (
        (shrink_grad, shrink_grad_out),
        (hidden_grad, hidden_grad_out),
        (branch_grad, branch_grad_out),
        (joint_grad, joint_grad_out),
        (source_grad, input_grads),
    )

    def block_span(block):
        return slice(block * query_rows, (block + 1) * query_rows)

    def micro_rows(micro):
        return pl.ds(pl.multiple_of(micro * seq_rows, seq_rows), seq_rows)

    def input_load(micro):
        return pltpu.make_async_copy(inputs.at[micro], source.at[micro], source_sems.at[micro])

    def cotangent_load(micro):
        return pltpu.make_async_copy(
            cotangent.at[micro], top_grad.at[micro], source_sems.at[micro]
        )

    def onward(target, phase, micro, block):
        return pltpu.make_async_remote_copy(
            src_ref=result.at[micro, block_span(block)],
            dst_ref=target.at[micro, block_span(block)],
            send_sem=send_sems.at[micro, block],
            recv_sem=recv_sems.at[micro, block],
            device_id=sibling(),
            device_id_type=MESH,
        )

    def result_out(micro):
        return pltpu.make_async_copy(
            result.at[micro], outputs.at[micro], result_sems.at[micro]
        )

    def left_out(index, micro):
        buffer, place = lefts[index]
        return pltpu.make_async_copy(buffer, place.at[micro_rows(micro)], left_sems.at[index])

    def keep_place(index, micro):
        place = kept[index][1]
        return place.at[micro_rows(micro)] if index == 7 else place.at[micro]

    def keep_out(index, micro):
        return pltpu.make_async_copy(kept[index][0], keep_place(index, micro), keep_sems.at[index])

    def keep_load(index, micro):
        return pltpu.make_async_copy(keep_place(index, micro), kept[index][0], load_sems.at[index])

    def grad_out(index, micro):
        buffer, place = grads[index]
        return pltpu.make_async_copy(buffer, place.at[micro_rows(micro)], grad_sems.at[index])

    lengths_load = pltpu.make_async_copy(lengths_in, lengths, lengths_sem)
    lengths_load.start()

    @pl.when(first)
    def _():
        for micro in range(micro_count):
            input_load(micro).start()

    weight_loads[0].start()

    @pl.when(second)
    def _():
        for micro in range(micro_count):
            cotangent_load(micro).start()

    for load in weight_loads[1:]:
        load.start()
    greet_sibling()
    small[...] = jnp.zeros_like(small)
    lengths_load.wait()

    def pair_columns(part, pair):
        start = part * width + pair * pair_width
        return slice(start, start + pair_width)

    def attend_block(block):
        start, rows = score_rows(block)
        span = block_span(block)

        def scores_of(pair):
            keys = half_stack(joint[:rows, pair_columns(1, pair)], head_scale)
            return back_product(keys, joint[span, pair_columns(0, pair)])

        def mix(pair, weights):
            values = flipped(joint[:rows, pair_columns(2, pair)]).astype(low)
            halves = [
                product(values[half * head_width : (half + 1) * head_width], weights[half])
                for half in range(2)
            ]
            attended[span, pair_columns(0, pair)] = (
                jnp.concatenate(halves, axis=0).T.astype(low)
            )

        ahead = scores_of(0)
        behind = None
        for pair in range(pair_count):
            scores = ahead
            if pair + 1 < pair_count:
                ahead = scores_of(pair + 1)
            if behind is not None:
                mix(*behind)
            weights = []
            for half in range(2):
                masked = scores[half * rows : (half + 1) * rows] + mask[start : start + rows]
                exponent = jnp.exp(masked - jnp.max(masked, axis=0, keepdims=True))
                part = exponent * (1.0 / jnp.sum(exponent, axis=0, keepdims=True))
                part = part.astype(low)
                probs[2 * pair + half, start : start + rows] = part
                weights.append(part)
            behind = (pair, weights)
        mix(*behind)

    def forward_micro(micro, _):
        def before_write(left_indices, keep_indices):
            @pl.when(micro > 0)
            def _():
                for index in left_indices:
                    left_out(index, micro - 1).wait()
                for index in keep_indices:
                    keep_out(index, micro - 1).wait()

        def after_write(left_indices, keep_indices):
            for index in left_indices:
                left_out(index, micro).start()

            @pl.when(micro < last)
            def _():
                for index in keep_indices:
                    keep_out(index, micro).start()

        def weight_ready(index):
            @pl.when(micro == 0)
            def _():
                weight_loads[index].wait()

        length = lengths[0, micro]
        for block in range(block_count):
            start, rows = score_rows(block)
            key_pos = lax.broadcasted_iota(jnp.int32, (rows, query_rows), 0)
            query_pos = block * query_rows + lax.broadcasted_iota(
                jnp.int32, (rows, query_rows), 1
            )
            allowed = (key_pos <= query_pos) & (key_pos < length)
            mask[start : start + rows] = jnp.where(allowed, 0.0, masked_score)

        @pl.when(first)
        def _():
            input_load(micro).wait()

        for block in range(block_count):
            span = block_span(block)
            final = block == block_count - 1

            @pl.when(second)
            def _():
                onward(source, 0, micro, block).wait_recv()

            if block == 0:
                before_write((0,), (0, 1))
            normal_one, inverse_one = normalize(source[micro, span].astype(wide))
            normal[span] = normal_one.astype(low)
            inverse[span] = jnp.broadcast_to(inverse_one, (query_rows, inverse.shape[1]))
            normed[span] = (normal_one * attend_gain[...] + attend_shift[...]).astype(low)
            if final:
                after_write((0,), (0, 1))
            if block == 0:
                before_write((), (2,))
                weight_ready(0)
            for part in range(3):
                columns = slice(part * width, (part + 1) * width)
                piece = product(normed[span], joint_w[:, columns])
                if part == 0:
                    piece = piece + joint_bias[:, :width]
                elif part == 2:
                    piece = piece + joint_bias[:, width:]
                joint[span, columns] = piece.astype(low)
            if final:
                after_write((), (2,))
            if block == 0:
                before_write((1,), (3,))
            attend_block(block)
            if final:
                after_write((1,), (3,))
            if block == 0:
                before_write((2,), (4, 5))
                weight_ready(1)
            middle[span] = source[micro, span].astype(wide) + branch_scale * (
                product(attended[span], project_w[...]) + project_bias[...]
            )
            normal_both, inverse_both = normalize(middle[span])
            normal_two[span] = normal_both.astype(low)
            inverse_two[span] = jnp.broadcast_to(inverse_both, (query_rows, inverse.shape[1]))
            normed_two[span] = (normal_both * feed_gain[...] + feed_shift[...]).astype(low)
            if final:
                after_write((2,), (4, 5))
            if block == 0:
                before_write((3,), (6,))
                weight_ready(2)
            for part in range(hidden_width // width):
                columns = slice(part * width, (part + 1) * width)
                hidden = product(normed_two[span], expand_w[:, columns]) + expand_bias[:, columns]
                square = hidden * hidden
                inner = jnp.tanh(hidden * (gelu_scale + (gelu_scale * gelu_cubic) * square))
                gate = 0.5 + 0.5 * inner
                value = hidden * gate
                active[span, columns] = value.astype(low)
                slope[span, columns] = (
                    gate
                    + value
                    * (1.0 - inner)
                    * (gelu_scale + (3.0 * gelu_scale * gelu_cubic) * square)
                ).astype(low)
            if final:
                after_write((3,), (6,))
            if block == 0:
                weight_ready(3)
            result[micro, span] = (
                middle[span]
                + branch_scale * (product(active[span], shrink_w[...]) + shrink_bias[...])
            ).astype(low)

            @pl.when(first)
            def _():
                onward(source, 0, micro, block).start()

        result_out(micro).start()
        return 0

    lax.fori_loop(0, micro_count, forward_micro, 0)
    for micro in range(micro_count):
        result_out(micro).wait()

    @pl.when(first)
    def _():
        for micro in range(micro_count):
            for block in range(block_count):
                onward(source, 0, micro, block).wait_send()

    def add_sum(row, values):
        small[row : row + 1] += jnp.sum(values, axis=0, keepdims=True)

    def attend_block_back(block):
        start, rows = score_rows(block)
        span = block_span(block)
        bottom = block == block_count - 1

        def weight_grad_of(pair):
            values = half_stack(joint[:rows, pair_columns(2, pair)], 1.0)
            return back_product(values, attended_grad[span, pair_columns(0, pair)])

        lane = lax.broadcasted_iota(jnp.int32, (1, pair_width), 1)
        upper = lane >= head_width
        ahead = weight_grad_of(0)
        for pair in range(pair_count):
            weight_grad = ahead
            if pair + 1 < pair_count:
                ahead = weight_grad_of(pair + 1)
            flat = pair_columns(0, pair)
            query = joint[span, flat]
            keys = flipped(joint[:rows, pair_columns(1, pair)]).astype(low)
            out_grad = attended_grad[span, flat]
            inner = (out_grad.astype(wide) * attended[span, flat].astype(wide)).T
            key_halves, value_halves, query_halves = [], [], []
            for half in range(2):
                head = slice(half * head_width, (half + 1) * head_width)
                delta = jnp.sum(inner[head], axis=0, keepdims=True)
                weights = probs[2 * pair + half, start : start + rows]
                score_grad = (
                    weights.astype(wide)
                    * (weight_grad[half * rows : (half + 1) * rows] - delta)
                ).astype(low)
                value_halves.append(product(weights, out_grad))
                key_halves.append(product(score_grad, query))
                query_halves.append(product(keys[head], score_grad))
            joint_grad[span, flat] = (
                jnp.concatenate(query_halves, axis=0).T * head_scale
            ).astype(low)
            key_grad = jnp.where(upper, key_halves[1], key_halves[0]) * head_scale
            value_grad = jnp.where(upper, value_halves[1], value_halves[0])
            done = rows - query_rows
            key_done, value_done = key_grad[done:], value_grad[done:]
            if not bottom:
                key_done = key_done + key_part[done:rows, flat]
                value_done = value_done + value_part[done:rows, flat]
            joint_grad[span, pair_columns(1, pair)] = key_done.astype(low)
            joint_grad[span, pair_columns(2, pair)] = value_done.astype(low)
            if done:
                if bottom:
                    key_part[:done, flat] = key_grad[:done]
                    value_part[:done, flat] = value_grad[:done]
                else:
                    key_part[:done, flat] += key_grad[:done]
                    value_part[:done, flat] += value_grad[:done]

    def backward_micro(step, _):
        micro = last - step

        def before_write(index):
            @pl.when(step > 0)
            def _():
                grad_out(index, micro + 1).wait()

        def loaded(*indices):
            @pl.when(step > 0)
            def _():
                for index in indices:
                    keep_load(index, micro).wait()

        def load_next(*indices):
            @pl.when(micro > 0)
            def _():
                for index in indices:
                    keep_load(index, micro - 1).start()

        last_row = jnp.where(first, seq_rows, lengths[0, micro])

        @pl.when(second)
        def _():
            cotangent_load(micro).wait()

        for block in reversed(range(block_count)):
            span = block_span(block)
            opening = block == block_count - 1
            closing = block == 0

            @pl.when(first)
            def _():
                onward(top_grad, 1, micro, block).wait_recv()

            row_pos = block * query_rows + lax.broadcasted_iota(jnp.int32, (query_rows, 1), 0)
            output_grad = jnp.where(row_pos < last_row, top_grad[micro, span].astype(wide), 0.0)
            if opening:
                before_write(0)
            shrink_low = (branch_scale * output_grad).astype(low)
            shrink_grad[span] = shrink_low
            add_sum(5, shrink_low.astype(wide))
            middle[span] = output_grad
            if closing:
                grad_out(0, micro).start()
            if opening:
                before_write(1)
                loaded(6)
            for part in range(hidden_width // width):
                columns = slice(part * width, (part + 1) * width)
                grad = back_product(shrink_grad[span], shrink_w[columns, :])
                grad_low = (grad * slope[span, columns].astype(wide)).astype(low)
                hidden_grad[span, columns] = grad_low
                add_sum(8 + part, grad_low.astype(wide))
            if closing:
                load_next(6)
                grad_out(1, micro).start()
            normed_grad = back_product(hidden_grad[span], expand_w[...])
            if opening:
                loaded(4, 5)
            normal_wide = normal_two[span].astype(wide)
            add_sum(3, normed_grad * normal_wide)
            add_sum(4, normed_grad)
            middle[span] += norm_slope(
                normed_grad * feed_gain[...], normal_wide, inverse_two[span, :1]
            )
            if closing:
                load_next(4, 5)
            if opening:
                before_write(2)
            branch_low = (branch_scale * middle[span]).astype(low)
            branch_grad[span] = branch_low
            add_sum(2, branch_low.astype(wide))
            if closing:
                grad_out(2, micro).start()
            attended_grad[span] = back_product(branch_grad[span], project_w[...]).astype(low)
            if opening:
                before_write(3)
                loaded(2, 3, 7)
            attend_block_back(block)
            if closing:
                load_next(2, 3, 7)
                grad_out(3, micro).start()
            add_sum(6, joint_grad[span, :width].astype(wide))
            add_sum(7, joint_grad[span, 2 * width :].astype(wide))
            normed_grad = back_product(joint_grad[span], joint_w[...])
            if opening:
                before_write(4)
                loaded(0, 1)
            normal_wide = normal[span].astype(wide)
            add_sum(0, normed_grad * normal_wide)
            add_sum(1, normed_grad)
            total = middle[span] + norm_slope(
                normed_grad * attend_gain[...], normal_wide, inverse[span, :1]
            )
            if closing:
                load_next(0, 1)
            source_grad[span] = total
            result[micro, span] = total.astype(low)

            @pl.when(second)
            def _():
                onward(top_grad, 1, micro, block).start()

        grad_out(4, micro).start()
        return 0

    left_out(1, last).wait()
    lax.fori_loop(0, micro_count, backward_micro, 0)
    for index in (0, 2, 3):
        left_out(index, last).wait()
    for index in range(len(grads)):
        grad_out(index, 0).wait()

    @pl.when(second)
    def _():
        for micro in range(micro_count):
            for block in range(block_count):
                onward(top_grad, 1, micro, block).wait_send()


def run_sections(lengths, inputs, cotangent, weights):
    micro_count, seq_rows, width = inputs.shape
    hidden = weights["expand_weight"].shape[1]
    heads = width // head_width
    tokens = micro_count * seq_rows
    blocks = seq_rows // query_rows
    score_total = score_rows(blocks)[0]
    small_rows = -(-(8 + hidden // width) // 8) * 8
    hbm = pl.BlockSpec(memory_space=pl.ANY)
    vmem = pl.BlockSpec(memory_space=pltpu.VMEM)

    def row(name):
        return weights[name].reshape(1, -1)

    def shape(*dims, kind=low):
        return jax.ShapeDtypeStruct(dims, kind)

    return pl.pallas_call(
        sections_kernel,
        name="sections",
        out_shape=(
            shape(micro_count, seq_rows, width),
            shape(tokens, width, kind=wide),
            shape(tokens, width),
            shape(tokens, width),
            shape(tokens, width),
            shape(tokens, hidden),
            shape(tokens, width),
            shape(tokens, hidden),
            shape(tokens, 3 * width),
            shape(tokens, width),
            shape(small_rows, width, kind=wide),
            shape(micro_count, seq_rows, width),
            shape(micro_count, seq_rows, 128, kind=wide),
            shape(micro_count, seq_rows, 3 * width),
            shape(micro_count, heads, score_total, query_rows),
            shape(micro_count, seq_rows, width),
            shape(micro_count, seq_rows, 128, kind=wide),
            shape(micro_count, seq_rows, hidden),
        ),
        in_specs=[hbm] * 7 + [vmem] * 8,
        out_specs=tuple([hbm] * 10 + [vmem] + [hbm] * 7),
        scratch_shapes=[
            pltpu.VMEM((width, 3 * width), low),
            pltpu.VMEM((width, width), low),
            pltpu.VMEM((width, hidden), low),
            pltpu.VMEM((hidden, width), low),
            pltpu.VMEM((micro_count, seq_rows, width), low),
            pltpu.VMEM((micro_count, seq_rows, width), low),
            pltpu.VMEM((micro_count, seq_rows, width), low),
            pltpu.VMEM((seq_rows, width), low),
            pltpu.VMEM((seq_rows, width), low),
            pltpu.VMEM((seq_rows, 128), wide),
            pltpu.VMEM((seq_rows, 3 * width), low),
            pltpu.VMEM((heads, score_total, query_rows), low),
            pltpu.VMEM((seq_rows, width), low),
            pltpu.VMEM((seq_rows, width), wide),
            pltpu.VMEM((seq_rows, width), low),
            pltpu.VMEM((seq_rows, width), low),
            pltpu.VMEM((seq_rows, 128), wide),
            pltpu.VMEM((seq_rows, hidden), low),
            pltpu.VMEM((seq_rows, hidden), low),
            pltpu.VMEM((score_total, query_rows), wide),
            pltpu.VMEM((seq_rows, width), low),
            pltpu.VMEM((seq_rows, hidden), low),
            pltpu.VMEM((seq_rows, 3 * width), low),
            pltpu.VMEM((seq_rows, width), low),
            pltpu.VMEM((seq_rows, width), low),
            pltpu.VMEM((seq_rows, width), wide),
            pltpu.VMEM((max(seq_rows - query_rows, 8), width), wide),
            pltpu.VMEM((max(seq_rows - query_rows, 8), width), wide),
            pltpu.SemaphoreType.DMA((4,)),
            pltpu.SemaphoreType.DMA((micro_count,)),
            pltpu.SemaphoreType.DMA((micro_count, blocks)),
            pltpu.SemaphoreType.DMA((micro_count, blocks)),
            pltpu.SemaphoreType.DMA((micro_count,)),
            pltpu.SemaphoreType.DMA((4,)),
            pltpu.SemaphoreType.DMA((8,)),
            pltpu.SemaphoreType.DMA((8,)),
            pltpu.SemaphoreType.DMA((5,)),
            pltpu.SMEM((1, micro_count), jnp.int32),
            pltpu.SemaphoreType.DMA,
        ],
        compiler_params=pltpu.CompilerParams(
            collective_id=1, has_side_effects=True, vmem_limit_bytes=62 * 2**20
        ),
    )(
        lengths.reshape(1, micro_count),
        inputs,
        cotangent,
        weights["joint_weight"],
        weights["project_weight"],
        weights["expand_weight"],
        weights["shrink_weight"],
        row("attend_gain"),
        row("attend_shift"),
        row("joint_bias"),
        row("project_bias"),
        row("feed_gain"),
        row("feed_shift"),
        row("expand_bias"),
        row("shrink_bias"),
    )


def axis_bits(count):
    bits = []
    step = 1
    while step < count:
        bits.append(step)
        step *= 2
    assert step == count
    return bits


line_length = 4


def line_place():
    return (lax.axis_index("dp") // 2) % line_length


def exchange_bits(dp_count, sub_count):
    bits = [("dp", step) for step in axis_bits(dp_count)]
    near, line, beyond = bits[0], bits[1:3], bits[3:]
    assert len(line) == 2 and sub_count == 2
    return near, ("sub", 1), line, beyond


def partner_id(bit):
    axis, step = bit
    place = {name: lax.axis_index(name) for name in ("pipe", "dp", "sub")}
    place[axis] = place[axis] ^ step
    return (place["pipe"], place["dp"], place["sub"])


def own_bit(bit):
    axis, step = bit
    return (lax.axis_index(axis) // step) % 2


def grad_blocks(width, hidden):
    blocks = [(3, 0, column) for column in range(width // block_cols)]
    blocks += [(2, 0, column) for column in range(3 * width // block_cols)]
    blocks += [(1, 0, column) for column in range(hidden // block_cols)]
    for row in range(hidden // block_rows):
        for column in range(width // block_cols):
            blocks.append((0, row, column))
    return blocks


opening_ticks = ((1, 3, 5, 7, 9, 11), (1, 3, 5, 7, 9, 11), (0, 0, 3, 9, 11, 12))
group_size = 2


def exchange_groups():
    groups = []
    for kind, ticks in enumerate(opening_ticks):
        for number, tick in enumerate(ticks):
            groups.append((kind + number % 2 if kind == 2 else kind, tick))
    return sorted(groups, key=lambda group: group[1])


def kind_steps(kind, near, sub, beyond):
    line = [("line", turn) for turn in range(line_length - 1)]
    halves = [("half", sub), ("half", near)] if kind in (1, 3) else [("half", near), ("half", sub)]
    there = halves + line if kind < 2 else line + halves
    there = there + [("whole", bit) for bit in beyond]
    return there


def arrival_rows(steps):
    rows, places, start, line_rows = block_rows, [], 0, 0
    for name, turn in steps:
        if name == "half":
            rows //= 2
            places.append((start, rows))
            start += rows
        elif name == "line":
            if turn == 0:
                line_rows = rows // line_length
                rows = line_rows
            places.append((start, line_rows))
            start += line_rows * (1 if turn == 0 else 2)
        else:
            places.append((start, rows))
            start += rows
    return places, start


def rows_at(offset, rows):
    return pl.ds(pl.multiple_of(offset, 16), rows)


class Exchange:
    def __init__(self, bits, groups, own, arrivals, send_sems, recv_sems, free_sems):
        near, sub, _, beyond = bits
        self.groups, self.own, self.arrivals = groups, own, arrivals
        self.send_sems, self.recv_sems, self.free_sems = send_sems, recv_sems, free_sems
        self.place = line_place()
        self.there = [kind_steps(kind, near, sub, beyond) for kind in range(4)]
        self.there_count = len(self.there[0])
        self.total_steps = 2 * self.there_count - len(beyond)
        self.arrival_places = [arrival_rows(steps)[0] for steps in self.there]
        self.starts = []
        start = 0
        for kind, _ in groups:
            self.starts.append(start)
            start += arrival_rows(self.there[kind])[1]
        self.offsets = []
        for steps in self.there:
            offset, rows, places = 0, block_rows, []
            for name, what in steps:
                if name == "half":
                    half = rows // 2
                    mine = own_bit(what)
                    keep = offset + mine * half
                    places.append((keep, offset + (1 - mine) * half, half))
                    offset, rows = keep, half
                elif name == "line":
                    if what == 0:
                        line_start, rows = offset, rows // line_length
                        offset = line_start + self.place * rows
                    places.append((line_start, line_start, rows))
                else:
                    places.append((offset, offset, rows))
            self.offsets.append(places)

    def step_of(self, index, step):
        kind = self.groups[index][0]
        if step < self.there_count:
            return kind, step, False
        beyond = self.total_steps - 2 * self.there_count
        return kind, self.there_count - 1 + beyond - (step - self.there_count), True

    def rows(self, index, offset, rows):
        return self.own.at[pl.ds(group_size * index, group_size), rows_at(offset, rows)]

    def copy(self, index, step, side, source, target, device):
        return pltpu.make_async_remote_copy(
            src_ref=source,
            dst_ref=target,
            send_sem=self.send_sems.at[index, step, side],
            recv_sem=self.recv_sems.at[index, step, side],
            device_id=device,
            device_id_type=MESH,
        )

    def arrival(self, index, there, side):
        kind = self.groups[index][0]
        start, rows = self.arrival_places[kind][there]
        name, turn = self.there[kind][there]
        if name == "line" and turn > 0:
            start += side * rows
        return self.arrivals.at[:, pl.ds(self.starts[index] + start, rows)]

    def neighbour(self, side):
        shift = 2 if side else -2
        return (lax.axis_index("pipe"), lax.axis_index("dp") + shift, lax.axis_index("sub"))

    def line_sends(self, turn, back):
        place, top = self.place, line_length - 1
        if back:
            down = ((place + turn <= top) & (place > 0), place + turn)
            up = ((place - turn >= 0) & (place < top), place - turn)
        else:
            down = ((place >= top - turn) & (place > 0), place - top + turn)
            up = ((place <= turn) & (place < top), place + top - turn)
        return down, up

    def line_gets(self, turn, back):
        place, top = self.place, line_length - 1
        if back:
            below = ((place >= 1) & (place - 1 - turn >= 0), place - 1 - turn)
            above = ((place < top) & (place + 1 + turn <= top), place + 1 + turn)
        else:
            below = ((place >= 1) & (place - 1 <= turn), place + top - 1 - turn)
            above = ((place < top) & (place + 1 >= top - turn), place + 1 - top + turn)
        return below, above

    def line_copy(self, index, step, side, shard):
        kind, there, back = self.step_of(index, step)
        start, _, rows = self.offsets[kind][there]
        source = self.rows(index, start + shard * rows, rows)
        target = source if back else self.arrival(index, there, 1 - side)
        return pltpu.make_async_remote_copy(
            src_ref=source,
            dst_ref=target,
            send_sem=self.send_sems.at[index, step, side],
            recv_sem=self.recv_sems.at[index, step, 1 - side],
            device_id=self.neighbour(side),
            device_id_type=MESH,
        )

    def line_landing(self, index, step, side, shard):
        kind, there, back = self.step_of(index, step)
        start, _, rows = self.offsets[kind][there]
        place = self.rows(index, start + shard * rows, rows)
        target = place if back else self.arrival(index, there, side)
        return self.copy(index, step, side, place, target, self.neighbour(side))

    def pair_copy(self, index, step, landing):
        kind, there, back = self.step_of(index, step)
        keep, give, rows = self.offsets[kind][there]
        bit = self.there[kind][there][1]
        if back:
            source = self.rows(index, keep, rows)
            target = self.rows(index, give if landing else keep, rows)
        else:
            source = self.rows(index, give, rows)
            target = self.arrival(index, there, 0)
        return self.copy(index, step, 0, source, target, partner_id(bit))

    def add(self, index, there, side, offset, rows):
        total = self.rows(index, offset, rows)
        arrived = self.arrival(index, there, side)
        for member in range(group_size):
            total[member] = (
                total[member].astype(jnp.float32) + arrived[member].astype(jnp.float32)
            ).astype(jnp.bfloat16)

    def send(self, index, step):
        kind, there, back = self.step_of(index, step)
        name, what = self.there[kind][there]
        if name != "line":
            if back:
                pl.semaphore_wait(self.free_sems.at[index, there, 0], 1)
            self.pair_copy(index, step, False).start()
            return
        turn = line_length - 2 - what if back else what
        for side, (sends, shard) in enumerate(self.line_sends(turn, back)):

            @pl.when(sends)
            def _():
                if back:
                    pl.semaphore_wait(self.free_sems.at[index, there, side], 1)
                self.line_copy(index, step, side, shard).start()

    def receive(self, index, step):
        kind, there, back = self.step_of(index, step)
        name, what = self.there[kind][there]
        start, _, rows = self.offsets[kind][there]
        if name != "line":
            self.pair_copy(index, step, True).wait()
            if not back:
                self.add(index, there, 0, start, rows)
                if name == "half":
                    pl.semaphore_signal(
                        self.free_sems.at[index, there, 0],
                        inc=1,
                        device_id=partner_id(what),
                        device_id_type=MESH,
                    )
            return
        turn = line_length - 2 - what if back else what
        for side, (sends, shard) in enumerate(self.line_sends(turn, back)):

            @pl.when(sends)
            def _():
                self.line_copy(index, step, side, shard).wait_send()
                if not back:
                    pl.semaphore_signal(
                        self.free_sems.at[index, there, 1 - side],
                        inc=1,
                        device_id=self.neighbour(side),
                        device_id_type=MESH,
                    )

        for side, (gets, shard) in enumerate(self.line_gets(turn, back)):

            @pl.when(gets)
            def _():
                self.line_landing(index, step, side, shard).wait_recv()
                if not back:
                    self.add(index, there, side, start + shard * rows, rows)

    def advance(self, index, step):
        self.receive(index, step - 1)
        if step < self.total_steps:
            self.send(index, step)


def sum_kernel(bits, blocks, *refs):
    lefts, rights, small_in = refs[0:4], refs[4:8], refs[8]
    own, small_out = refs[9:11]
    left_bufs, right_bufs = refs[11:15], refs[15:19]
    arrivals, send_sems, recv_sems, free_sems = refs[19:23]
    small, small_got, load_sems, small_send, small_recv = refs[23:]
    near, sub, line, beyond = bits
    pairs = (near, sub, *line, *beyond)
    stage_count = len(pairs)

    loads = [None] * 4
    for index in reversed(range(4)):
        left_load = pltpu.make_async_copy(lefts[index], left_bufs[index], load_sems.at[2 * index])
        right_load = pltpu.make_async_copy(
            rights[index], right_bufs[index], load_sems.at[2 * index + 1]
        )
        left_load.start()
        right_load.start()
        loads[index] = (left_load, right_load)
    loaded = [False] * 4

    groups = exchange_groups()
    exchange = Exchange(bits, groups, own, arrivals, send_sems, recv_sems, free_sems)
    place = line_place()
    barrier = pltpu.get_barrier_semaphore()
    for bit in pairs:
        pl.semaphore_signal(barrier, inc=1, device_id=partner_id(bit), device_id_type=MESH)
    for side, near_end in enumerate((place > 0, place < line_length - 1)):

        @pl.when(near_end)
        def _():
            pl.semaphore_signal(
                barrier, inc=1, device_id=exchange.neighbour(side), device_id_type=MESH
            )

    ends = jnp.where((place == 0) | (place == line_length - 1), 1, 2)
    pl.semaphore_wait(barrier, stage_count + ends)

    def produce(block):
        index, row, column = blocks[block]
        if not loaded[index]:
            loads[index][0].wait()
            loads[index][1].wait()
            loaded[index] = True
        left = left_bufs[index][:, row * block_rows : (row + 1) * block_rows]
        right = right_bufs[index][:, column * block_cols : (column + 1) * block_cols]
        own[block] = lax.dot_general(
            left, right, (((0,), (0,)), ((), ())), preferred_element_type=jnp.float32
        ).astype(jnp.bfloat16)

    def small_copy(stage):
        return pltpu.make_async_remote_copy(
            src_ref=small.at[stage],
            dst_ref=small_got.at[stage],
            send_sem=small_send.at[stage],
            recv_sem=small_recv.at[stage],
            device_id=partner_id(pairs[stage]),
            device_id_type=MESH,
        )

    last = max(tick for _, tick in groups) + exchange.total_steps
    for tick in range(last + 1):
        for index, (kind, begin) in enumerate(groups):
            if begin == tick:
                for block in range(group_size * index, group_size * (index + 1)):
                    produce(block)
                exchange.send(index, 0)
        if tick == 0:
            small[0] = small_in[...]
        elif tick <= stage_count:
            small_copy(tick - 1).wait()
            total = small[tick - 1] + small_got[tick - 1]
            if tick < stage_count:
                small[tick] = total
            else:
                small_out[...] = total
        if tick < stage_count:
            small_copy(tick).start()
        for step in range(1, exchange.total_steps + 1):
            for index, (kind, begin) in enumerate(groups):
                if begin + step == tick:
                    exchange.advance(index, step)


def summed_grads(lefts, rights, small, dp_count, sub_count):
    tokens, width = lefts[3].shape
    hidden = lefts[0].shape[1]
    bits = exchange_bits(dp_count, sub_count)
    near, sub, line, beyond = bits
    stage_count = 2 + len(line) + len(beyond)
    blocks = grad_blocks(width, hidden)
    block_count = len(blocks)
    groups = exchange_groups()
    assert group_size * len(groups) == block_count
    there = kind_steps(0, near, sub, beyond)
    steps = 2 * len(there) - len(beyond)
    rows = sum(arrival_rows(kind_steps(kind, near, sub, beyond))[1] for kind, _ in groups)
    low = jnp.bfloat16
    hbm = pl.BlockSpec(memory_space=pl.ANY)
    vmem = pl.BlockSpec(memory_space=pltpu.VMEM)
    return pl.pallas_call(
        functools.partial(sum_kernel, bits, blocks),
        name="grad_sums",
        out_shape=(
            pltpu.VMEM((block_count, block_rows, block_cols), low),
            pltpu.VMEM(small.shape, jnp.float32),
        ),
        in_specs=[hbm] * 8 + [vmem],
        out_specs=(vmem, vmem),
        scratch_shapes=[pltpu.VMEM(array.shape, low) for array in lefts]
        + [pltpu.VMEM(array.shape, low) for array in rights]
        + [
            pltpu.VMEM((group_size, rows, block_cols), low),
            pltpu.SemaphoreType.DMA((len(groups), steps, 2)),
            pltpu.SemaphoreType.DMA((len(groups), steps, 2)),
            pltpu.SemaphoreType.REGULAR((len(groups), len(there), 2)),
            pltpu.VMEM((stage_count, *small.shape), jnp.float32),
            pltpu.VMEM((stage_count, *small.shape), jnp.float32),
            pltpu.SemaphoreType.DMA((8,)),
            pltpu.SemaphoreType.DMA((stage_count,)),
            pltpu.SemaphoreType.DMA((stage_count,)),
        ],
        compiler_params=pltpu.CompilerParams(
            collective_id=0, has_side_effects=True, vmem_limit_bytes=46 * 2**20
        ),
    )(*lefts, *rights, small)


stage_count_out = 6


def finish_kernel(
    blocks,
    own,
    small,
    outputs_in,
    grads_in,
    outputs,
    input_grads,
    attend_gain,
    attend_shift,
    joint,
    joint_bias,
    project,
    project_bias,
    feed_gain,
    feed_shift,
    expand,
    expand_bias,
    shrink,
    shrink_bias,
    stages,
    stage_sems,
    pass_sems,
    outputs_buf,
    grads_buf,
):
    places = (shrink, expand, joint, project)
    width = shrink_bias.shape[1]
    pass_loads = [
        pltpu.make_async_copy(outputs_in, outputs_buf, pass_sems.at[0]),
        pltpu.make_async_copy(grads_in, grads_buf, pass_sems.at[1]),
    ]
    passes = [
        pltpu.make_async_copy(outputs_buf, outputs, pass_sems.at[2]),
        pltpu.make_async_copy(grads_buf, input_grads, pass_sems.at[3]),
    ]
    for copy in pass_loads:
        copy.start()

    def block_copy(block):
        index, row, column = blocks[block]
        slot = block % stage_count_out
        return pltpu.make_async_copy(
            stages.at[slot],
            places[index].at[
                pl.ds(row * block_rows, block_rows), pl.ds(column * block_cols, block_cols)
            ],
            stage_sems.at[slot],
        )

    for block in range(len(blocks)):
        if block >= stage_count_out:
            block_copy(block - stage_count_out).wait()
        stages[block % stage_count_out] = own[block].astype(jnp.float32)
        block_copy(block).start()
        if block == len(blocks) // 2:
            for load, copy in zip(pass_loads, passes):
                load.wait()
                copy.start()
    for row, place in (
        (0, attend_gain),
        (1, attend_shift),
        (2, project_bias),
        (3, feed_gain),
        (4, feed_shift),
        (5, shrink_bias),
        (6, joint_bias),
        (8, expand_bias),
    ):
        for part in range(place.shape[1] // width):
            place[:, part * width : (part + 1) * width] = small[row + part : row + part + 1]
    for block in range(max(0, len(blocks) - stage_count_out), len(blocks)):
        block_copy(block).wait()
    for copy in passes:
        copy.wait()


def finished(own, small, outputs, input_grads, width, hidden):
    blocks = grad_blocks(width, hidden)
    hbm = pl.BlockSpec(memory_space=pl.ANY)
    vmem = pl.BlockSpec(memory_space=pltpu.VMEM)

    def shape(*dims):
        return jax.ShapeDtypeStruct(dims, jnp.float32)

    return pl.pallas_call(
        functools.partial(finish_kernel, blocks),
        name="finish",
        out_shape=(
            jax.ShapeDtypeStruct(outputs.shape, outputs.dtype),
            jax.ShapeDtypeStruct(input_grads.shape, input_grads.dtype),
            shape(1, width),
            shape(1, width),
            shape(width, 3 * width),
            shape(1, 2 * width),
            shape(width, width),
            shape(1, width),
            shape(1, width),
            shape(1, width),
            shape(width, hidden),
            shape(1, hidden),
            shape(hidden, width),
            shape(1, width),
        ),
        in_specs=[vmem, vmem, hbm, hbm],
        out_specs=(
            hbm, hbm, vmem, vmem, hbm, vmem, hbm, vmem, vmem, vmem, hbm, vmem, hbm, vmem
        ),
        scratch_shapes=[
            pltpu.VMEM((stage_count_out, block_rows, block_cols), jnp.float32),
            pltpu.SemaphoreType.DMA((stage_count_out,)),
            pltpu.SemaphoreType.DMA((4,)),
            pltpu.VMEM(outputs.shape, outputs.dtype),
            pltpu.VMEM(input_grads.shape, input_grads.dtype),
        ],
        compiler_params=pltpu.CompilerParams(vmem_limit_bytes=16 * 2**20),
    )(
        pltpu.with_memory_space_constraint(own, pltpu.VMEM),
        pltpu.with_memory_space_constraint(small, pltpu.VMEM),
        pltpu.with_memory_space_constraint(outputs, pltpu.HBM),
        pltpu.with_memory_space_constraint(input_grads, pltpu.HBM),
    )


weight_names = (
    "attend_gain",
    "attend_shift",
    "joint_weight",
    "joint_bias",
    "project_weight",
    "project_bias",
    "feed_gain",
    "feed_shift",
    "expand_weight",
    "expand_bias",
    "shrink_weight",
    "shrink_bias",
)


def body(inputs, cotangent, lengths, *params):
    weights = {name: param[0] for name, param in zip(weight_names, params)}
    micro_count, _, seq_rows, width = inputs.shape
    (
        outputs,
        input_grads,
        normed,
        attended,
        normed_two,
        active,
        shrink_grad,
        hidden_grad,
        joint_grad,
        branch_grad,
        small,
        *_,
    ) = run_sections(lengths, inputs[:, 0], cotangent[:, 0], weights)
    hidden = active.shape[1]
    own, small_sum = summed_grads(
        (active, normed_two, normed, attended),
        (shrink_grad, hidden_grad, joint_grad, branch_grad),
        small,
        lax.axis_size("dp"),
        lax.axis_size("sub"),
    )
    outputs, input_grads, *full_grads = finished(
        own, small_sum, outputs, input_grads, width, hidden
    )
    return (
        outputs[None, :, None],
        input_grads.reshape(1, micro_count, 1, seq_rows, width),
        *(grad if grad.shape[0] == 1 else grad[None] for grad in full_grads),
    )


def solution(mesh):
    in_specs = (
        P(None, ("dp", "sub"), None, None),
        P(None, ("dp", "sub"), None, None),
        P(None, ("dp", "sub")),
        P("pipe", None),
        P("pipe", None),
        P("pipe", None, None),
        P("pipe", None),
        P("pipe", None, None),
        P("pipe", None),
        P("pipe", None),
        P("pipe", None),
        P("pipe", None, None),
        P("pipe", None),
        P("pipe", None, None),
        P("pipe", None),
    )
    out_specs = (
        P("pipe", None, ("dp", "sub"), None, None),
        P("pipe", None, ("dp", "sub"), None, None),
        P("pipe", None),
        P("pipe", None),
        P("pipe", None, None),
        P("pipe", None),
        P("pipe", None, None),
        P("pipe", None),
        P("pipe", None),
        P("pipe", None),
        P("pipe", None, None),
        P("pipe", None),
        P("pipe", None, None),
        P("pipe", None),
    )
    return jax.shard_map(body, mesh=mesh, in_specs=in_specs, out_specs=out_specs, check_vma=False)
```

```python
import functools

import jax
import jax.numpy as jnp
from jax import lax
from jax.experimental import pallas as pl
from jax.experimental.pallas import tpu as pltpu
from jax.sharding import PartitionSpec as P

MESH = pl.DeviceIdType.MESH
branch_scale = 24.0 ** (-0.5)
head_scale = 0.125
norm_eps = 1e-05
gelu_scale = (2.0 / 3.141592653589793) ** 0.5
gelu_cubic = 0.044715
masked_score = -1e30
low = jnp.bfloat16
wide = jnp.float32
head_width = 64
pair_width = 128
query_rows = 256
block_rows = 768
block_cols = 256


def product(left, right):
    return jnp.dot(left, right, preferred_element_type=wide)


def back_product(left, right):
    return lax.dot_general(left, right, (((1,), (1,)), ((), ())), preferred_element_type=wide)


def flipped(matrix):
    return matrix.astype(wide).T


def sibling():
    return (1 - lax.axis_index("pipe"), lax.axis_index("dp"), lax.axis_index("sub"))


def greet_sibling():
    barrier = pltpu.get_barrier_semaphore()
    pl.semaphore_signal(barrier, inc=1, device_id=sibling(), device_id_type=MESH)
    pl.semaphore_wait(barrier, 1)


def pair_mask(half, value):
    lane = lax.broadcasted_iota(jnp.int32, (1, pair_width), 1)
    return jnp.where((lane // head_width) == half, value, 0.0).astype(low)


def score_rows(block):
    first = query_rows * (block * (block + 1) // 2)
    return first, query_rows * (block + 1)


def normalize(values):
    center = values - jnp.mean(values, axis=-1, keepdims=True)
    inverse = lax.rsqrt(jnp.mean(center * center, axis=-1, keepdims=True) + norm_eps)
    return center * inverse, inverse


def norm_slope(graded, normal, inverse):
    return inverse * (
        graded
        - jnp.mean(graded, axis=-1, keepdims=True)
        - normal * jnp.mean(graded * normal, axis=-1, keepdims=True)
    )


def half_stack(matrix, value):
    return jnp.concatenate(
        [matrix * pair_mask(0, value), matrix * pair_mask(1, value)], axis=0
    )


def sections_kernel(
    lengths_in,
    inputs,
    cotangent,
    joint_weight,
    project_weight,
    expand_weight,
    shrink_weight,
    attend_gain,
    attend_shift,
    joint_bias,
    project_bias,
    feed_gain,
    feed_shift,
    expand_bias,
    shrink_bias,
    outputs,
    input_grads,
    normed_out,
    attended_out,
    normed_two_out,
    active_out,
    shrink_grad_out,
    hidden_grad_out,
    joint_grad_out,
    branch_grad_out,
    small,
    normal_out,
    inverse_out,
    joint_out,
    probs_out,
    normal_two_out,
    inverse_two_out,
    slope_out,
    joint_w,
    project_w,
    expand_w,
    shrink_w,
    source,
    result,
    top_grad,
    normed,
    normal,
    inverse,
    joint,
    probs,
    attended,
    middle,
    normed_two,
    normal_two,
    inverse_two,
    active,
    slope,
    mask,
    shrink_grad,
    hidden_grad,
    joint_grad,
    branch_grad,
    attended_grad,
    source_grad,
    key_part,
    value_part,
    weight_sems,
    source_sems,
    send_sems,
    recv_sems,
    result_sems,
    left_sems,
    keep_sems,
    load_sems,
    grad_sems,
    lengths,
    lengths_sem,
):
    first = lax.axis_index("pipe") == 0
    second = jnp.logical_not(first)
    micro_count, seq_rows, width = source.shape
    hidden_width = expand_w.shape[1]
    pair_count = width // pair_width
    block_count = seq_rows // query_rows
    last = micro_count - 1
    weight_loads = [
        pltpu.make_async_copy(place, buffer, weight_sems.at[index])
        for index, (place, buffer) in enumerate(
            (
                (joint_weight, joint_w),
                (project_weight, project_w),
                (expand_weight, expand_w),
                (shrink_weight, shrink_w),
            )
        )
    ]
    lefts = (
        (normed, normed_out),
        (attended, attended_out),
        (normed_two, normed_two_out),
        (active, active_out),
    )
    kept = (
        (normal, normal_out),
        (inverse, inverse_out),
        (joint, joint_out),
        (probs, probs_out),
        (normal_two, normal_two_out),
        (inverse_two, inverse_two_out),
        (slope, slope_out),
        (attended, attended_out),
    )
    grads = (
        (shrink_grad, shrink_grad_out),
        (hidden_grad, hidden_grad_out),
        (branch_grad, branch_grad_out),
        (joint_grad, joint_grad_out),
        (source_grad, input_grads),
    )

    def block_span(block):
        return slice(block * query_rows, (block + 1) * query_rows)

    def micro_rows(micro):
        return pl.ds(pl.multiple_of(micro * seq_rows, seq_rows), seq_rows)

    def input_load(micro):
        return pltpu.make_async_copy(inputs.at[micro], source.at[micro], source_sems.at[micro])

    def cotangent_load(micro):
        return pltpu.make_async_copy(
            cotangent.at[micro], top_grad.at[micro], source_sems.at[micro]
        )

    def onward(target, phase, micro, block):
        return pltpu.make_async_remote_copy(
            src_ref=result.at[micro, block_span(block)],
            dst_ref=target.at[micro, block_span(block)],
            send_sem=send_sems.at[micro, block],
            recv_sem=recv_sems.at[micro, block],
            device_id=sibling(),
            device_id_type=MESH,
        )

    def result_out(micro):
        return pltpu.make_async_copy(
            result.at[micro], outputs.at[micro], result_sems.at[micro]
        )

    def left_out(index, micro):
        buffer, place = lefts[index]
        return pltpu.make_async_copy(buffer, place.at[micro_rows(micro)], left_sems.at[index])

    def keep_place(index, micro):
        place = kept[index][1]
        return place.at[micro_rows(micro)] if index == 7 else place.at[micro]

    def keep_out(index, micro):
        return pltpu.make_async_copy(kept[index][0], keep_place(index, micro), keep_sems.at[index])

    def keep_load(index, micro):
        return pltpu.make_async_copy(keep_place(index, micro), kept[index][0], load_sems.at[index])

    def grad_out(index, micro):
        buffer, place = grads[index]
        return pltpu.make_async_copy(buffer, place.at[micro_rows(micro)], grad_sems.at[index])

    lengths_load = pltpu.make_async_copy(lengths_in, lengths, lengths_sem)
    lengths_load.start()

    @pl.when(first)
    def _():
        for micro in range(micro_count):
            input_load(micro).start()

    weight_loads[0].start()

    @pl.when(second)
    def _():
        for micro in range(micro_count):
            cotangent_load(micro).start()

    greet_sibling()
    small[...] = jnp.zeros_like(small)
    lengths_load.wait()

    def pair_columns(part, pair):
        start = part * width + pair * pair_width
        return slice(start, start + pair_width)

    def attend_block(block):
        start, rows = score_rows(block)
        span = block_span(block)

        def scores_of(pair):
            keys = half_stack(joint[:rows, pair_columns(1, pair)], head_scale)
            return back_product(keys, joint[span, pair_columns(0, pair)])

        def mix(pair, weights):
            values = flipped(joint[:rows, pair_columns(2, pair)]).astype(low)
            halves = [
                product(values[half * head_width : (half + 1) * head_width], weights[half])
                for half in range(2)
            ]
            attended[span, pair_columns(0, pair)] = (
                jnp.concatenate(halves, axis=0).T.astype(low)
            )

        ahead = scores_of(0)
        behind = None
        for pair in range(pair_count):
            scores = ahead
            if pair + 1 < pair_count:
                ahead = scores_of(pair + 1)
            if behind is not None:
                mix(*behind)
            weights = []
            for half in range(2):
                masked = scores[half * rows : (half + 1) * rows] + mask[start : start + rows]
                exponent = jnp.exp(masked - jnp.max(masked, axis=0, keepdims=True))
                part = exponent * (1.0 / jnp.sum(exponent, axis=0, keepdims=True))
                part = part.astype(low)
                probs[2 * pair + half, start : start + rows] = part
                weights.append(part)
            behind = (pair, weights)
        mix(*behind)

    def forward_micro(micro, _):
        def before_write(left_indices, keep_indices):
            @pl.when(micro > 0)
            def _():
                for index in left_indices:
                    left_out(index, micro - 1).wait()
                for index in keep_indices:
                    keep_out(index, micro - 1).wait()

        def after_write(left_indices, keep_indices):
            for index in left_indices:
                left_out(index, micro).start()

            @pl.when(micro < last)
            def _():
                for index in keep_indices:
                    keep_out(index, micro).start()

        def weight_ready(index):
            @pl.when(micro == 0)
            def _():
                weight_loads[index].wait()
                if index == 0:
                    for load in weight_loads[1:]:
                        load.start()

        length = lengths[0, micro]
        for block in range(block_count):
            start, rows = score_rows(block)
            key_pos = lax.broadcasted_iota(jnp.int32, (rows, query_rows), 0)
            query_pos = block * query_rows + lax.broadcasted_iota(
                jnp.int32, (rows, query_rows), 1
            )
            allowed = (key_pos <= query_pos) & (key_pos < length)
            mask[start : start + rows] = jnp.where(allowed, 0.0, masked_score)

        @pl.when(first)
        def _():
            input_load(micro).wait()

        for block in range(block_count):
            span = block_span(block)
            final = block == block_count - 1

            @pl.when(second)
            def _():
                onward(source, 0, micro, block).wait_recv()

            if block == 0:
                before_write((0,), (0, 1))
            normal_one, inverse_one = normalize(source[micro, span].astype(wide))
            normal[span] = normal_one.astype(low)
            inverse[span] = jnp.broadcast_to(inverse_one, (query_rows, inverse.shape[1]))
            normed[span] = (normal_one * attend_gain[...] + attend_shift[...]).astype(low)
            if final:
                after_write((0,), (0, 1))
            if block == 0:
                before_write((), (2,))
                weight_ready(0)
            for part in range(3):
                columns = slice(part * width, (part + 1) * width)
                piece = product(normed[span], joint_w[:, columns])
                if part == 0:
                    piece = piece + joint_bias[:, :width]
                elif part == 2:
                    piece = piece + joint_bias[:, width:]
                joint[span, columns] = piece.astype(low)
            if final:
                after_write((), (2,))
            if block == 0:
                before_write((1,), (3,))
            attend_block(block)
            if final:
                after_write((1,), (3,))
            if block == 0:
                before_write((2,), (4, 5))
                weight_ready(1)
            middle[span] = source[micro, span].astype(wide) + branch_scale * (
                product(attended[span], project_w[...]) + project_bias[...]
            )
            normal_both, inverse_both = normalize(middle[span])
            normal_two[span] = normal_both.astype(low)
            inverse_two[span] = jnp.broadcast_to(inverse_both, (query_rows, inverse.shape[1]))
            normed_two[span] = (normal_both * feed_gain[...] + feed_shift[...]).astype(low)
            if final:
                after_write((2,), (4, 5))
            if block == 0:
                before_write((3,), (6,))
                weight_ready(2)
            for part in range(hidden_width // width):
                columns = slice(part * width, (part + 1) * width)
                hidden = product(normed_two[span], expand_w[:, columns]) + expand_bias[:, columns]
                square = hidden * hidden
                inner = jnp.tanh(hidden * (gelu_scale + (gelu_scale * gelu_cubic) * square))
                gate = 0.5 + 0.5 * inner
                value = hidden * gate
                active[span, columns] = value.astype(low)
                slope[span, columns] = (
                    gate
                    + value
                    * (1.0 - inner)
                    * (gelu_scale + (3.0 * gelu_scale * gelu_cubic) * square)
                ).astype(low)
            if final:
                after_write((3,), (6,))
            if block == 0:
                weight_ready(3)
            result[micro, span] = (
                middle[span]
                + branch_scale * (product(active[span], shrink_w[...]) + shrink_bias[...])
            ).astype(low)

            @pl.when(first)
            def _():
                onward(source, 0, micro, block).start()

        result_out(micro).start()
        return 0

    lax.fori_loop(0, micro_count, forward_micro, 0)
    for micro in range(micro_count):
        result_out(micro).wait()

    @pl.when(first)
    def _():
        for micro in range(micro_count):
            for block in range(block_count):
                onward(source, 0, micro, block).wait_send()

    def add_sum(row, values):
        small[row : row + 1] += jnp.sum(values, axis=0, keepdims=True)

    def attend_block_back(block):
        start, rows = score_rows(block)
        span = block_span(block)
        bottom = block == block_count - 1

        def weight_grad_of(pair):
            values = half_stack(joint[:rows, pair_columns(2, pair)], 1.0)
            return back_product(values, attended_grad[span, pair_columns(0, pair)])

        lane = lax.broadcasted_iota(jnp.int32, (1, pair_width), 1)
        upper = lane >= head_width
        ahead = weight_grad_of(0)
        for pair in range(pair_count):
            weight_grad = ahead
            if pair + 1 < pair_count:
                ahead = weight_grad_of(pair + 1)
            flat = pair_columns(0, pair)
            query = joint[span, flat]
            keys = flipped(joint[:rows, pair_columns(1, pair)]).astype(low)
            out_grad = attended_grad[span, flat]
            inner = (out_grad.astype(wide) * attended[span, flat].astype(wide)).T
            key_halves, value_halves, query_halves = [], [], []
            for half in range(2):
                head = slice(half * head_width, (half + 1) * head_width)
                delta = jnp.sum(inner[head], axis=0, keepdims=True)
                weights = probs[2 * pair + half, start : start + rows]
                score_grad = (
                    weights.astype(wide)
                    * (weight_grad[half * rows : (half + 1) * rows] - delta)
                ).astype(low)
                value_halves.append(product(weights, out_grad))
                key_halves.append(product(score_grad, query))
                query_halves.append(product(keys[head], score_grad))
            joint_grad[span, flat] = (
                jnp.concatenate(query_halves, axis=0).T * head_scale
            ).astype(low)
            key_grad = jnp.where(upper, key_halves[1], key_halves[0]) * head_scale
            value_grad = jnp.where(upper, value_halves[1], value_halves[0])
            done = rows - query_rows
            key_done, value_done = key_grad[done:], value_grad[done:]
            if not bottom:
                key_done = key_done + key_part[done:rows, flat]
                value_done = value_done + value_part[done:rows, flat]
            joint_grad[span, pair_columns(1, pair)] = key_done.astype(low)
            joint_grad[span, pair_columns(2, pair)] = value_done.astype(low)
            if done:
                if bottom:
                    key_part[:done, flat] = key_grad[:done]
                    value_part[:done, flat] = value_grad[:done]
                else:
                    key_part[:done, flat] += key_grad[:done]
                    value_part[:done, flat] += value_grad[:done]

    def backward_micro(step, _):
        micro = last - step

        def before_write(index):
            @pl.when(step > 0)
            def _():
                grad_out(index, micro + 1).wait()

        def loaded(*indices):
            @pl.when(step > 0)
            def _():
                for index in indices:
                    keep_load(index, micro).wait()

        def load_next(*indices):
            @pl.when(micro > 0)
            def _():
                for index in indices:
                    keep_load(index, micro - 1).start()

        last_row = jnp.where(first, seq_rows, lengths[0, micro])

        @pl.when(second)
        def _():
            cotangent_load(micro).wait()

        for block in reversed(range(block_count)):
            span = block_span(block)
            opening = block == block_count - 1
            closing = block == 0

            @pl.when(first)
            def _():
                onward(top_grad, 1, micro, block).wait_recv()

            row_pos = block * query_rows + lax.broadcasted_iota(jnp.int32, (query_rows, 1), 0)
            output_grad = jnp.where(row_pos < last_row, top_grad[micro, span].astype(wide), 0.0)
            if opening:
                before_write(0)
            shrink_low = (branch_scale * output_grad).astype(low)
            shrink_grad[span] = shrink_low
            add_sum(5, shrink_low.astype(wide))
            middle[span] = output_grad
            if closing:
                grad_out(0, micro).start()
            if opening:
                before_write(1)
                loaded(6)
            for part in range(hidden_width // width):
                columns = slice(part * width, (part + 1) * width)
                grad = back_product(shrink_grad[span], shrink_w[columns, :])
                grad_low = (grad * slope[span, columns].astype(wide)).astype(low)
                hidden_grad[span, columns] = grad_low
                add_sum(8 + part, grad_low.astype(wide))
            if closing:
                load_next(6)
                grad_out(1, micro).start()
            normed_grad = back_product(hidden_grad[span], expand_w[...])
            if opening:
                loaded(4, 5)
            normal_wide = normal_two[span].astype(wide)
            add_sum(3, normed_grad * normal_wide)
            add_sum(4, normed_grad)
            middle[span] += norm_slope(
                normed_grad * feed_gain[...], normal_wide, inverse_two[span, :1]
            )
            if closing:
                load_next(4, 5)
            if opening:
                before_write(2)
            branch_low = (branch_scale * middle[span]).astype(low)
            branch_grad[span] = branch_low
            add_sum(2, branch_low.astype(wide))
            if closing:
                grad_out(2, micro).start()
            attended_grad[span] = back_product(branch_grad[span], project_w[...]).astype(low)
            if opening:
                before_write(3)
                loaded(2, 3, 7)
            attend_block_back(block)
            if closing:
                load_next(2, 3, 7)
                grad_out(3, micro).start()
            add_sum(6, joint_grad[span, :width].astype(wide))
            add_sum(7, joint_grad[span, 2 * width :].astype(wide))
            normed_grad = back_product(joint_grad[span], joint_w[...])
            if opening:
                before_write(4)
                loaded(0, 1)
            normal_wide = normal[span].astype(wide)
            add_sum(0, normed_grad * normal_wide)
            add_sum(1, normed_grad)
            total = middle[span] + norm_slope(
                normed_grad * attend_gain[...], normal_wide, inverse[span, :1]
            )
            if closing:
                load_next(0, 1)
            source_grad[span] = total
            result[micro, span] = total.astype(low)

            @pl.when(second)
            def _():
                onward(top_grad, 1, micro, block).start()

        grad_out(4, micro).start()
        return 0

    left_out(1, last).wait()
    lax.fori_loop(0, micro_count, backward_micro, 0)
    for index in (0, 2, 3):
        left_out(index, last).wait()
    for index in range(len(grads)):
        grad_out(index, 0).wait()

    @pl.when(second)
    def _():
        for micro in range(micro_count):
            for block in range(block_count):
                onward(top_grad, 1, micro, block).wait_send()


def run_sections(lengths, inputs, cotangent, weights):
    micro_count, seq_rows, width = inputs.shape
    hidden = weights["expand_weight"].shape[1]
    heads = width // head_width
    tokens = micro_count * seq_rows
    blocks = seq_rows // query_rows
    score_total = score_rows(blocks)[0]
    small_rows = -(-(8 + hidden // width) // 8) * 8
    hbm = pl.BlockSpec(memory_space=pl.ANY)
    vmem = pl.BlockSpec(memory_space=pltpu.VMEM)

    def row(name):
        return weights[name].reshape(1, -1)

    def shape(*dims, kind=low):
        return jax.ShapeDtypeStruct(dims, kind)

    return pl.pallas_call(
        sections_kernel,
        name="sections",
        out_shape=(
            shape(micro_count, seq_rows, width),
            shape(tokens, width, kind=wide),
            shape(tokens, width),
            shape(tokens, width),
            shape(tokens, width),
            shape(tokens, hidden),
            shape(tokens, width),
            shape(tokens, hidden),
            shape(tokens, 3 * width),
            shape(tokens, width),
            shape(small_rows, width, kind=wide),
            shape(micro_count, seq_rows, width),
            shape(micro_count, seq_rows, 128, kind=wide),
            shape(micro_count, seq_rows, 3 * width),
            shape(micro_count, heads, score_total, query_rows),
            shape(micro_count, seq_rows, width),
            shape(micro_count, seq_rows, 128, kind=wide),
            shape(micro_count, seq_rows, hidden),
        ),
        in_specs=[hbm] * 7 + [vmem] * 8,
        out_specs=tuple([hbm] * 10 + [vmem] + [hbm] * 7),
        scratch_shapes=[
            pltpu.VMEM((width, 3 * width), low),
            pltpu.VMEM((width, width), low),
            pltpu.VMEM((width, hidden), low),
            pltpu.VMEM((hidden, width), low),
            pltpu.VMEM((micro_count, seq_rows, width), low),
            pltpu.VMEM((micro_count, seq_rows, width), low),
            pltpu.VMEM((micro_count, seq_rows, width), low),
            pltpu.VMEM((seq_rows, width), low),
            pltpu.VMEM((seq_rows, width), low),
            pltpu.VMEM((seq_rows, 128), wide),
            pltpu.VMEM((seq_rows, 3 * width), low),
            pltpu.VMEM((heads, score_total, query_rows), low),
            pltpu.VMEM((seq_rows, width), low),
            pltpu.VMEM((seq_rows, width), wide),
            pltpu.VMEM((seq_rows, width), low),
            pltpu.VMEM((seq_rows, width), low),
            pltpu.VMEM((seq_rows, 128), wide),
            pltpu.VMEM((seq_rows, hidden), low),
            pltpu.VMEM((seq_rows, hidden), low),
            pltpu.VMEM((score_total, query_rows), wide),
            pltpu.VMEM((seq_rows, width), low),
            pltpu.VMEM((seq_rows, hidden), low),
            pltpu.VMEM((seq_rows, 3 * width), low),
            pltpu.VMEM((seq_rows, width), low),
            pltpu.VMEM((seq_rows, width), low),
            pltpu.VMEM((seq_rows, width), wide),
            pltpu.VMEM((max(seq_rows - query_rows, 8), width), wide),
            pltpu.VMEM((max(seq_rows - query_rows, 8), width), wide),
            pltpu.SemaphoreType.DMA((4,)),
            pltpu.SemaphoreType.DMA((micro_count,)),
            pltpu.SemaphoreType.DMA((micro_count, blocks)),
            pltpu.SemaphoreType.DMA((micro_count, blocks)),
            pltpu.SemaphoreType.DMA((micro_count,)),
            pltpu.SemaphoreType.DMA((4,)),
            pltpu.SemaphoreType.DMA((8,)),
            pltpu.SemaphoreType.DMA((8,)),
            pltpu.SemaphoreType.DMA((5,)),
            pltpu.SMEM((1, micro_count), jnp.int32),
            pltpu.SemaphoreType.DMA,
        ],
        compiler_params=pltpu.CompilerParams(
            collective_id=1, has_side_effects=True, vmem_limit_bytes=62 * 2**20
        ),
    )(
        lengths.reshape(1, micro_count),
        inputs,
        cotangent,
        weights["joint_weight"],
        weights["project_weight"],
        weights["expand_weight"],
        weights["shrink_weight"],
        row("attend_gain"),
        row("attend_shift"),
        row("joint_bias"),
        row("project_bias"),
        row("feed_gain"),
        row("feed_shift"),
        row("expand_bias"),
        row("shrink_bias"),
    )


def axis_bits(count):
    bits = []
    step = 1
    while step < count:
        bits.append(step)
        step *= 2
    assert step == count
    return bits


line_length = 4


def line_place():
    return (lax.axis_index("dp") // 2) % line_length


def exchange_bits(dp_count, sub_count):
    bits = [("dp", step) for step in axis_bits(dp_count)]
    near, line, beyond = bits[0], bits[1:3], bits[3:]
    assert len(line) == 2 and sub_count == 2
    return near, ("sub", 1), line, beyond


def partner_id(bit):
    axis, step = bit
    place = {name: lax.axis_index(name) for name in ("pipe", "dp", "sub")}
    place[axis] = place[axis] ^ step
    return (place["pipe"], place["dp"], place["sub"])


def own_bit(bit):
    axis, step = bit
    return (lax.axis_index(axis) // step) % 2


def grad_blocks(width, hidden):
    blocks = [(3, 0, column) for column in range(width // block_cols)]
    blocks += [(2, 0, column) for column in range(3 * width // block_cols)]
    blocks += [(1, 0, column) for column in range(hidden // block_cols)]
    for row in range(hidden // block_rows):
        for column in range(width // block_cols):
            blocks.append((0, row, column))
    return blocks


schedule = (
    (2, 2, 0),
    (0, 2, 1),
    (1, 2, 1),
    (3, 1, 1),
    (0, 2, 2),
    (3, 2, 2),
    (1, 1, 2),
    (0, 1, 4),
    (1, 1, 4),
    (0, 2, 5),
    (1, 2, 5),
    (0, 2, 7),
    (1, 2, 7),
    (3, 2, 8),
    (0, 2, 9),
    (1, 2, 9),
    (0, 2, 10),
    (2, 2, 10),
    (1, 2, 10),
    (3, 2, 11),
)
most_blocks = 2


def exchange_groups():
    groups, start = [], 0
    for kind, size, tick in schedule:
        groups.append((kind, start, size, tick))
        start += size
    return groups


def kind_steps(kind, near, sub, beyond):
    line = [("line", turn) for turn in range(line_length - 1)]
    halves = [("half", sub), ("half", near)] if kind in (1, 3) else [("half", near), ("half", sub)]
    there = halves + line if kind < 2 else line + halves
    there = there + [("whole", bit) for bit in beyond]
    return there


def arrival_rows(steps):
    rows, places, start, line_rows = block_rows, [], 0, 0
    for name, turn in steps:
        if name == "half":
            rows //= 2
            places.append((start, rows))
            start += rows
        elif name == "line":
            if turn == 0:
                line_rows = rows // line_length
                rows = line_rows
            places.append((start, line_rows))
            start += line_rows * (1 if turn == 0 else 2)
        else:
            places.append((start, rows))
            start += rows
    return places, start


def rows_at(offset, rows):
    return pl.ds(pl.multiple_of(offset, 16), rows)


class Exchange:
    def __init__(self, bits, groups, own, arrivals, send_sems, recv_sems, free_sems):
        near, sub, _, beyond = bits
        self.groups, self.own, self.arrivals = groups, own, arrivals
        self.send_sems, self.recv_sems, self.free_sems = send_sems, recv_sems, free_sems
        self.place = line_place()
        self.there = [kind_steps(kind, near, sub, beyond) for kind in range(4)]
        self.there_count = len(self.there[0])
        self.total_steps = 2 * self.there_count - len(beyond)
        self.arrival_places = [arrival_rows(steps)[0] for steps in self.there]
        self.starts = []
        start = 0
        for kind, *_ in groups:
            self.starts.append(start)
            start += arrival_rows(self.there[kind])[1]
        self.offsets = []
        for steps in self.there:
            offset, rows, places = 0, block_rows, []
            for name, what in steps:
                if name == "half":
                    half = rows // 2
                    mine = own_bit(what)
                    keep = offset + mine * half
                    places.append((keep, offset + (1 - mine) * half, half))
                    offset, rows = keep, half
                elif name == "line":
                    if what == 0:
                        line_start, rows = offset, rows // line_length
                        offset = line_start + self.place * rows
                    places.append((line_start, line_start, rows))
                else:
                    places.append((offset, offset, rows))
            self.offsets.append(places)

    def step_of(self, index, step):
        kind = self.groups[index][0]
        if step < self.there_count:
            return kind, step, False
        beyond = self.total_steps - 2 * self.there_count
        return kind, self.there_count - 1 + beyond - (step - self.there_count), True

    def rows(self, index, offset, rows):
        _, first_block, size, _ = self.groups[index]
        return self.own.at[pl.ds(first_block, size), rows_at(offset, rows)]

    def copy(self, index, step, side, source, target, device):
        return pltpu.make_async_remote_copy(
            src_ref=source,
            dst_ref=target,
            send_sem=self.send_sems.at[index, step, side],
            recv_sem=self.recv_sems.at[index, step, side],
            device_id=device,
            device_id_type=MESH,
        )

    def arrival(self, index, there, side):
        kind = self.groups[index][0]
        start, rows = self.arrival_places[kind][there]
        name, turn = self.there[kind][there]
        if name == "line" and turn > 0:
            start += side * rows
        size = self.groups[index][2]
        return self.arrivals.at[pl.ds(0, size), pl.ds(self.starts[index] + start, rows)]

    def neighbour(self, side):
        shift = 2 if side else -2
        return (lax.axis_index("pipe"), lax.axis_index("dp") + shift, lax.axis_index("sub"))

    def line_sends(self, turn, back):
        place, top = self.place, line_length - 1
        if back:
            down = ((place + turn <= top) & (place > 0), place + turn)
            up = ((place - turn >= 0) & (place < top), place - turn)
        else:
            down = ((place >= top - turn) & (place > 0), place - top + turn)
            up = ((place <= turn) & (place < top), place + top - turn)
        return down, up

    def line_gets(self, turn, back):
        place, top = self.place, line_length - 1
        if back:
            below = ((place >= 1) & (place - 1 - turn >= 0), place - 1 - turn)
            above = ((place < top) & (place + 1 + turn <= top), place + 1 + turn)
        else:
            below = ((place >= 1) & (place - 1 <= turn), place + top - 1 - turn)
            above = ((place < top) & (place + 1 >= top - turn), place + 1 - top + turn)
        return below, above

    def line_copy(self, index, step, side, shard):
        kind, there, back = self.step_of(index, step)
        start, _, rows = self.offsets[kind][there]
        source = self.rows(index, start + shard * rows, rows)
        target = source if back else self.arrival(index, there, 1 - side)
        return pltpu.make_async_remote_copy(
            src_ref=source,
            dst_ref=target,
            send_sem=self.send_sems.at[index, step, side],
            recv_sem=self.recv_sems.at[index, step, 1 - side],
            device_id=self.neighbour(side),
            device_id_type=MESH,
        )

    def line_landing(self, index, step, side, shard):
        kind, there, back = self.step_of(index, step)
        start, _, rows = self.offsets[kind][there]
        place = self.rows(index, start + shard * rows, rows)
        target = place if back else self.arrival(index, there, side)
        return self.copy(index, step, side, place, target, self.neighbour(side))

    def pair_copy(self, index, step, landing):
        kind, there, back = self.step_of(index, step)
        keep, give, rows = self.offsets[kind][there]
        bit = self.there[kind][there][1]
        if back:
            source = self.rows(index, keep, rows)
            target = self.rows(index, give if landing else keep, rows)
        else:
            source = self.rows(index, give, rows)
            target = self.arrival(index, there, 0)
        return self.copy(index, step, 0, source, target, partner_id(bit))

    def add(self, index, there, side, offset, rows):
        total = self.rows(index, offset, rows)
        arrived = self.arrival(index, there, side)
        for member in range(self.groups[index][2]):
            total[member] = (
                total[member].astype(jnp.float32) + arrived[member].astype(jnp.float32)
            ).astype(jnp.bfloat16)

    def send(self, index, step):
        kind, there, back = self.step_of(index, step)
        name, what = self.there[kind][there]
        if name != "line":
            if back:
                pl.semaphore_wait(self.free_sems.at[index, there, 0], 1)
            self.pair_copy(index, step, False).start()
            return
        turn = line_length - 2 - what if back else what
        for side, (sends, shard) in enumerate(self.line_sends(turn, back)):

            @pl.when(sends)
            def _():
                if back:
                    pl.semaphore_wait(self.free_sems.at[index, there, side], 1)
                self.line_copy(index, step, side, shard).start()

    def receive(self, index, step):
        kind, there, back = self.step_of(index, step)
        name, what = self.there[kind][there]
        start, _, rows = self.offsets[kind][there]
        if name != "line":
            self.pair_copy(index, step, True).wait()
            if not back:
                self.add(index, there, 0, start, rows)
                if name == "half":
                    pl.semaphore_signal(
                        self.free_sems.at[index, there, 0],
                        inc=1,
                        device_id=partner_id(what),
                        device_id_type=MESH,
                    )
            return
        turn = line_length - 2 - what if back else what
        for side, (sends, shard) in enumerate(self.line_sends(turn, back)):

            @pl.when(sends)
            def _():
                self.line_copy(index, step, side, shard).wait_send()
                if not back:
                    pl.semaphore_signal(
                        self.free_sems.at[index, there, 1 - side],
                        inc=1,
                        device_id=self.neighbour(side),
                        device_id_type=MESH,
                    )

        for side, (gets, shard) in enumerate(self.line_gets(turn, back)):

            @pl.when(gets)
            def _():
                self.line_landing(index, step, side, shard).wait_recv()
                if not back:
                    self.add(index, there, side, start + shard * rows, rows)

    def advance(self, index, step):
        self.receive(index, step - 1)
        if step < self.total_steps:
            self.send(index, step)


def sum_kernel(bits, blocks, *refs):
    lefts, rights, small_in = refs[0:4], refs[4:8], refs[8]
    own, small_out = refs[9:11]
    left_bufs, right_bufs = refs[11:15], refs[15:19]
    arrivals, send_sems, recv_sems, free_sems = refs[19:23]
    small, small_got, load_sems, small_send, small_recv = refs[23:]
    near, sub, line, beyond = bits
    pairs = (near, sub, *line, *beyond)
    stage_count = len(pairs)

    loads = [None] * 4
    for index in reversed(range(4)):
        left_load = pltpu.make_async_copy(lefts[index], left_bufs[index], load_sems.at[2 * index])
        right_load = pltpu.make_async_copy(
            rights[index], right_bufs[index], load_sems.at[2 * index + 1]
        )
        loads[index] = (left_load, right_load)

    def start_load(index):
        if index >= 0:
            for load in loads[index]:
                load.start()

    start_load(3)
    start_load(2)
    loaded = [False] * 4

    groups = exchange_groups()
    exchange = Exchange(bits, groups, own, arrivals, send_sems, recv_sems, free_sems)
    place = line_place()
    barrier = pltpu.get_barrier_semaphore()
    for bit in pairs:
        pl.semaphore_signal(barrier, inc=1, device_id=partner_id(bit), device_id_type=MESH)
    for side, near_end in enumerate((place > 0, place < line_length - 1)):

        @pl.when(near_end)
        def _():
            pl.semaphore_signal(
                barrier, inc=1, device_id=exchange.neighbour(side), device_id_type=MESH
            )

    ends = jnp.where((place == 0) | (place == line_length - 1), 1, 2)
    pl.semaphore_wait(barrier, stage_count + ends)

    def produce(block):
        index, row, column = blocks[block]
        if not loaded[index]:
            loads[index][0].wait()
            loads[index][1].wait()
            loaded[index] = True
            start_load(index - 2)
        left = left_bufs[index][:, row * block_rows : (row + 1) * block_rows]
        right = right_bufs[index][:, column * block_cols : (column + 1) * block_cols]
        own[block] = lax.dot_general(
            left, right, (((0,), (0,)), ((), ())), preferred_element_type=jnp.float32
        ).astype(jnp.bfloat16)

    def small_copy(stage):
        return pltpu.make_async_remote_copy(
            src_ref=small.at[stage],
            dst_ref=small_got.at[stage],
            send_sem=small_send.at[stage],
            recv_sem=small_recv.at[stage],
            device_id=partner_id(pairs[stage]),
            device_id_type=MESH,
        )

    last = max(group[3] for group in groups) + exchange.total_steps
    for tick in range(last + 1):
        for index, (_, start, size, begin) in enumerate(groups):
            if begin == tick:
                for block in range(start, start + size):
                    produce(block)
                exchange.send(index, 0)
        if tick == 0:
            small[0] = small_in[...]
        elif tick <= stage_count:
            small_copy(tick - 1).wait()
            total = small[tick - 1] + small_got[tick - 1]
            if tick < stage_count:
                small[tick] = total
            else:
                small_out[...] = total
        if tick < stage_count:
            small_copy(tick).start()
        for step in range(1, exchange.total_steps + 1):
            for index, (*_, begin) in enumerate(groups):
                if begin + step == tick:
                    exchange.advance(index, step)


def summed_grads(lefts, rights, small, dp_count, sub_count):
    tokens, width = lefts[3].shape
    hidden = lefts[0].shape[1]
    bits = exchange_bits(dp_count, sub_count)
    near, sub, line, beyond = bits
    stage_count = 2 + len(line) + len(beyond)
    blocks = grad_blocks(width, hidden)
    block_count = len(blocks)
    groups = exchange_groups()
    assert sum(group[2] for group in groups) == block_count
    there = kind_steps(0, near, sub, beyond)
    steps = 2 * len(there) - len(beyond)
    rows = sum(arrival_rows(kind_steps(kind, near, sub, beyond))[1] for kind, *_ in groups)
    low = jnp.bfloat16
    hbm = pl.BlockSpec(memory_space=pl.ANY)
    vmem = pl.BlockSpec(memory_space=pltpu.VMEM)
    return pl.pallas_call(
        functools.partial(sum_kernel, bits, blocks),
        name="grad_sums",
        out_shape=(
            pltpu.VMEM((block_count, block_rows, block_cols), low),
            pltpu.VMEM(small.shape, jnp.float32),
        ),
        in_specs=[hbm] * 8 + [vmem],
        out_specs=(vmem, vmem),
        scratch_shapes=[pltpu.VMEM(array.shape, low) for array in lefts]
        + [pltpu.VMEM(array.shape, low) for array in rights]
        + [
            pltpu.VMEM((most_blocks, rows, block_cols), low),
            pltpu.SemaphoreType.DMA((len(groups), steps, 2)),
            pltpu.SemaphoreType.DMA((len(groups), steps, 2)),
            pltpu.SemaphoreType.REGULAR((len(groups), len(there), 2)),
            pltpu.VMEM((stage_count, *small.shape), jnp.float32),
            pltpu.VMEM((stage_count, *small.shape), jnp.float32),
            pltpu.SemaphoreType.DMA((8,)),
            pltpu.SemaphoreType.DMA((stage_count,)),
            pltpu.SemaphoreType.DMA((stage_count,)),
        ],
        compiler_params=pltpu.CompilerParams(
            collective_id=0, has_side_effects=True, vmem_limit_bytes=46 * 2**20
        ),
    )(*lefts, *rights, small)


stage_count_out = 6


def finish_kernel(
    blocks,
    own,
    small,
    outputs_in,
    grads_in,
    outputs,
    input_grads,
    attend_gain,
    attend_shift,
    joint,
    joint_bias,
    project,
    project_bias,
    feed_gain,
    feed_shift,
    expand,
    expand_bias,
    shrink,
    shrink_bias,
    stages,
    stage_sems,
    pass_sems,
    outputs_buf,
    grads_buf,
):
    places = (shrink, expand, joint, project)
    width = shrink_bias.shape[1]
    pass_loads = [
        pltpu.make_async_copy(outputs_in, outputs_buf, pass_sems.at[0]),
        pltpu.make_async_copy(grads_in, grads_buf, pass_sems.at[1]),
    ]
    passes = [
        pltpu.make_async_copy(outputs_buf, outputs, pass_sems.at[2]),
        pltpu.make_async_copy(grads_buf, input_grads, pass_sems.at[3]),
    ]
    for copy in pass_loads:
        copy.start()

    def block_copy(block):
        index, row, column = blocks[block]
        slot = block % stage_count_out
        return pltpu.make_async_copy(
            stages.at[slot],
            places[index].at[
                pl.ds(row * block_rows, block_rows), pl.ds(column * block_cols, block_cols)
            ],
            stage_sems.at[slot],
        )

    for block in range(len(blocks)):
        if block >= stage_count_out:
            block_copy(block - stage_count_out).wait()
        stages[block % stage_count_out] = own[block].astype(jnp.float32)
        block_copy(block).start()
        if block == len(blocks) // 2:
            for load, copy in zip(pass_loads, passes):
                load.wait()
                copy.start()
    for row, place in (
        (0, attend_gain),
        (1, attend_shift),
        (2, project_bias),
        (3, feed_gain),
        (4, feed_shift),
        (5, shrink_bias),
        (6, joint_bias),
        (8, expand_bias),
    ):
        for part in range(place.shape[1] // width):
            place[:, part * width : (part + 1) * width] = small[row + part : row + part + 1]
    for block in range(max(0, len(blocks) - stage_count_out), len(blocks)):
        block_copy(block).wait()
    for copy in passes:
        copy.wait()


def finished(own, small, outputs, input_grads, width, hidden):
    blocks = grad_blocks(width, hidden)
    hbm = pl.BlockSpec(memory_space=pl.ANY)
    vmem = pl.BlockSpec(memory_space=pltpu.VMEM)

    def shape(*dims):
        return jax.ShapeDtypeStruct(dims, jnp.float32)

    return pl.pallas_call(
        functools.partial(finish_kernel, blocks),
        name="finish",
        out_shape=(
            jax.ShapeDtypeStruct(outputs.shape, outputs.dtype),
            jax.ShapeDtypeStruct(input_grads.shape, input_grads.dtype),
            shape(1, width),
            shape(1, width),
            shape(width, 3 * width),
            shape(1, 2 * width),
            shape(width, width),
            shape(1, width),
            shape(1, width),
            shape(1, width),
            shape(width, hidden),
            shape(1, hidden),
            shape(hidden, width),
            shape(1, width),
        ),
        in_specs=[vmem, vmem, hbm, hbm],
        out_specs=(
            hbm, hbm, vmem, vmem, hbm, vmem, hbm, vmem, vmem, vmem, hbm, vmem, hbm, vmem
        ),
        scratch_shapes=[
            pltpu.VMEM((stage_count_out, block_rows, block_cols), jnp.float32),
            pltpu.SemaphoreType.DMA((stage_count_out,)),
            pltpu.SemaphoreType.DMA((4,)),
            pltpu.VMEM(outputs.shape, outputs.dtype),
            pltpu.VMEM(input_grads.shape, input_grads.dtype),
        ],
        compiler_params=pltpu.CompilerParams(vmem_limit_bytes=16 * 2**20),
    )(
        pltpu.with_memory_space_constraint(own, pltpu.VMEM),
        pltpu.with_memory_space_constraint(small, pltpu.VMEM),
        pltpu.with_memory_space_constraint(outputs, pltpu.HBM),
        pltpu.with_memory_space_constraint(input_grads, pltpu.HBM),
    )


weight_names = (
    "attend_gain",
    "attend_shift",
    "joint_weight",
    "joint_bias",
    "project_weight",
    "project_bias",
    "feed_gain",
    "feed_shift",
    "expand_weight",
    "expand_bias",
    "shrink_weight",
    "shrink_bias",
)


def body(inputs, cotangent, lengths, *params):
    weights = {name: param[0] for name, param in zip(weight_names, params)}
    micro_count, _, seq_rows, width = inputs.shape
    (
        outputs,
        input_grads,
        normed,
        attended,
        normed_two,
        active,
        shrink_grad,
        hidden_grad,
        joint_grad,
        branch_grad,
        small,
        *_,
    ) = run_sections(lengths, inputs[:, 0], cotangent[:, 0], weights)
    hidden = active.shape[1]
    own, small_sum = summed_grads(
        (active, normed_two, normed, attended),
        (shrink_grad, hidden_grad, joint_grad, branch_grad),
        small,
        lax.axis_size("dp"),
        lax.axis_size("sub"),
    )
    outputs, input_grads, *full_grads = finished(
        own, small_sum, outputs, input_grads, width, hidden
    )
    return (
        outputs[None, :, None],
        input_grads.reshape(1, micro_count, 1, seq_rows, width),
        *(grad if grad.shape[0] == 1 else grad[None] for grad in full_grads),
    )


def solution(mesh):
    in_specs = (
        P(None, ("dp", "sub"), None, None),
        P(None, ("dp", "sub"), None, None),
        P(None, ("dp", "sub")),
        P("pipe", None),
        P("pipe", None),
        P("pipe", None, None),
        P("pipe", None),
        P("pipe", None, None),
        P("pipe", None),
        P("pipe", None),
        P("pipe", None),
        P("pipe", None, None),
        P("pipe", None),
        P("pipe", None, None),
        P("pipe", None),
    )
    out_specs = (
        P("pipe", None, ("dp", "sub"), None, None),
        P("pipe", None, ("dp", "sub"), None, None),
        P("pipe", None),
        P("pipe", None),
        P("pipe", None, None),
        P("pipe", None),
        P("pipe", None, None),
        P("pipe", None),
        P("pipe", None),
        P("pipe", None),
        P("pipe", None, None),
        P("pipe", None),
        P("pipe", None, None),
        P("pipe", None),
    )
    return jax.shard_map(body, mesh=mesh, in_specs=in_specs, out_specs=out_specs, check_vma=False)
```

```python
import functools

import jax
import jax.numpy as jnp
from jax import lax
from jax.experimental import pallas as pl
from jax.experimental.pallas import tpu as pltpu
from jax.sharding import PartitionSpec as P

MESH = pl.DeviceIdType.MESH
branch_scale = 24.0 ** (-0.5)
head_scale = 0.125
norm_eps = 1e-05
gelu_scale = (2.0 / 3.141592653589793) ** 0.5
gelu_cubic = 0.044715
masked_score = -1e30
low = jnp.bfloat16
wide = jnp.float32
head_width = 64
pair_width = 128
query_rows = 256
block_rows = 768
block_cols = 256


def product(left, right):
    return jnp.dot(left, right, preferred_element_type=wide)


def back_product(left, right):
    return lax.dot_general(left, right, (((1,), (1,)), ((), ())), preferred_element_type=wide)


def flipped(matrix):
    return matrix.astype(wide).T


def sibling():
    return (1 - lax.axis_index("pipe"), lax.axis_index("dp"), lax.axis_index("sub"))


def greet_sibling():
    barrier = pltpu.get_barrier_semaphore()
    pl.semaphore_signal(barrier, inc=1, device_id=sibling(), device_id_type=MESH)
    pl.semaphore_wait(barrier, 1)


def pair_mask(half, value):
    lane = lax.broadcasted_iota(jnp.int32, (1, pair_width), 1)
    return jnp.where((lane // head_width) == half, value, 0.0).astype(low)


def score_rows(block):
    first = query_rows * (block * (block + 1) // 2)
    return first, query_rows * (block + 1)


def normalize(values):
    center = values - jnp.mean(values, axis=-1, keepdims=True)
    inverse = lax.rsqrt(jnp.mean(center * center, axis=-1, keepdims=True) + norm_eps)
    return center * inverse, inverse


def norm_slope(graded, normal, inverse):
    return inverse * (
        graded
        - jnp.mean(graded, axis=-1, keepdims=True)
        - normal * jnp.mean(graded * normal, axis=-1, keepdims=True)
    )


def half_stack(matrix, value):
    return jnp.concatenate(
        [matrix * pair_mask(0, value), matrix * pair_mask(1, value)], axis=0
    )


def sections_kernel(
    lengths_in,
    inputs,
    cotangent,
    joint_weight,
    project_weight,
    expand_weight,
    shrink_weight,
    attend_gain,
    attend_shift,
    joint_bias,
    project_bias,
    feed_gain,
    feed_shift,
    expand_bias,
    shrink_bias,
    outputs,
    input_grads,
    normed_out,
    attended_out,
    normed_two_out,
    active_out,
    shrink_grad_out,
    hidden_grad_out,
    joint_grad_out,
    branch_grad_out,
    small,
    normal_out,
    inverse_out,
    joint_out,
    probs_out,
    normal_two_out,
    inverse_two_out,
    slope_out,
    joint_w,
    project_w,
    expand_w,
    shrink_w,
    source,
    result,
    top_grad,
    normed,
    normal,
    inverse,
    joint,
    probs,
    attended,
    middle,
    normed_two,
    normal_two,
    inverse_two,
    active,
    slope,
    mask,
    shrink_grad,
    hidden_grad,
    joint_grad,
    branch_grad,
    attended_grad,
    source_grad,
    key_part,
    value_part,
    weight_sems,
    source_sems,
    send_sems,
    recv_sems,
    result_sems,
    left_sems,
    keep_sems,
    load_sems,
    grad_sems,
    lengths,
    lengths_sem,
):
    first = lax.axis_index("pipe") == 0
    second = jnp.logical_not(first)
    micro_count, seq_rows, width = source.shape
    hidden_width = expand_w.shape[1]
    pair_count = width // pair_width
    block_count = seq_rows // query_rows
    last = micro_count - 1
    weight_loads = [
        pltpu.make_async_copy(place, buffer, weight_sems.at[index])
        for index, (place, buffer) in enumerate(
            (
                (joint_weight, joint_w),
                (project_weight, project_w),
                (expand_weight, expand_w),
                (shrink_weight, shrink_w),
            )
        )
    ]
    lefts = (
        (normed, normed_out),
        (attended, attended_out),
        (normed_two, normed_two_out),
        (active, active_out),
    )
    kept = (
        (normal, normal_out),
        (inverse, inverse_out),
        (joint, joint_out),
        (probs, probs_out),
        (normal_two, normal_two_out),
        (inverse_two, inverse_two_out),
        (slope, slope_out),
    )
    grads = (
        (shrink_grad, shrink_grad_out),
        (hidden_grad, hidden_grad_out),
        (branch_grad, branch_grad_out),
        (joint_grad, joint_grad_out),
        (source_grad, input_grads),
    )

    def block_span(block):
        return slice(block * query_rows, (block + 1) * query_rows)

    def micro_rows(micro):
        return pl.ds(pl.multiple_of(micro * seq_rows, seq_rows), seq_rows)

    def input_load(micro):
        return pltpu.make_async_copy(inputs.at[micro], source.at[micro], source_sems.at[micro])

    def cotangent_load(micro):
        return pltpu.make_async_copy(
            cotangent.at[micro], top_grad.at[micro], source_sems.at[micro]
        )

    def onward(target, phase, micro, block):
        return pltpu.make_async_remote_copy(
            src_ref=result.at[micro, block_span(block)],
            dst_ref=target.at[micro, block_span(block)],
            send_sem=send_sems.at[micro, block],
            recv_sem=recv_sems.at[micro, block],
            device_id=sibling(),
            device_id_type=MESH,
        )

    def result_out(micro):
        return pltpu.make_async_copy(
            result.at[micro], outputs.at[micro], result_sems.at[micro]
        )

    def left_out(index, micro):
        buffer, place = lefts[index]
        return pltpu.make_async_copy(buffer, place.at[micro_rows(micro)], left_sems.at[index])

    def keep_place(index, micro):
        return kept[index][1].at[micro]

    def keep_out(index, micro):
        return pltpu.make_async_copy(kept[index][0], keep_place(index, micro), keep_sems.at[index])

    def keep_load(index, micro):
        return pltpu.make_async_copy(keep_place(index, micro), kept[index][0], load_sems.at[index])

    def grad_out(index, micro):
        buffer, place = grads[index]
        return pltpu.make_async_copy(buffer, place.at[micro_rows(micro)], grad_sems.at[index])

    lengths_load = pltpu.make_async_copy(lengths_in, lengths, lengths_sem)
    lengths_load.start()

    @pl.when(first)
    def _():
        for micro in range(micro_count):
            input_load(micro).start()

    weight_loads[0].start()

    @pl.when(second)
    def _():
        for micro in range(micro_count):
            cotangent_load(micro).start()

    greet_sibling()
    small[...] = jnp.zeros_like(small)
    lengths_load.wait()

    def pair_columns(part, pair):
        start = part * width + pair * pair_width
        return slice(start, start + pair_width)

    def attend_block(block):
        start, rows = score_rows(block)
        span = block_span(block)

        def scores_of(pair):
            keys = half_stack(joint[:rows, pair_columns(1, pair)], head_scale)
            return back_product(keys, joint[span, pair_columns(0, pair)])

        def mix(pair, weights):
            values = flipped(joint[:rows, pair_columns(2, pair)]).astype(low)
            halves = [
                product(values[half * head_width : (half + 1) * head_width], weights[half])
                for half in range(2)
            ]
            attended[span, pair_columns(0, pair)] = (
                jnp.concatenate(halves, axis=0).T.astype(low)
            )

        ahead = scores_of(0)
        behind = None
        for pair in range(pair_count):
            scores = ahead
            if pair + 1 < pair_count:
                ahead = scores_of(pair + 1)
            if behind is not None:
                mix(*behind)
            weights = []
            for half in range(2):
                masked = scores[half * rows : (half + 1) * rows] + mask[start : start + rows]
                exponent = jnp.exp(masked - jnp.max(masked, axis=0, keepdims=True))
                part = exponent * (1.0 / jnp.sum(exponent, axis=0, keepdims=True))
                part = part.astype(low)
                probs[2 * pair + half, start : start + rows] = part
                weights.append(part)
            behind = (pair, weights)
        mix(*behind)

    def forward_micro(micro, _):
        def before_write(left_indices, keep_indices):
            @pl.when(micro > 0)
            def _():
                for index in left_indices:
                    left_out(index, micro - 1).wait()
                for index in keep_indices:
                    keep_out(index, micro - 1).wait()

        def after_write(left_indices, keep_indices):
            for index in left_indices:
                left_out(index, micro).start()

            @pl.when(micro < last)
            def _():
                for index in keep_indices:
                    keep_out(index, micro).start()

        def weight_ready(index):
            @pl.when(micro == 0)
            def _():
                weight_loads[index].wait()
                if index == 0:
                    for load in weight_loads[1:]:
                        load.start()

        length = lengths[0, micro]
        for block in range(block_count):
            start, rows = score_rows(block)
            key_pos = lax.broadcasted_iota(jnp.int32, (rows, query_rows), 0)
            query_pos = block * query_rows + lax.broadcasted_iota(
                jnp.int32, (rows, query_rows), 1
            )
            allowed = (key_pos <= query_pos) & (key_pos < length)
            mask[start : start + rows] = jnp.where(allowed, 0.0, masked_score)

        @pl.when(first)
        def _():
            input_load(micro).wait()

        for block in range(block_count):
            span = block_span(block)
            final = block == block_count - 1

            @pl.when(second)
            def _():
                onward(source, 0, micro, block).wait_recv()

            if block == 0:
                before_write((0,), (0, 1))
            normal_one, inverse_one = normalize(source[micro, span].astype(wide))
            normal[span] = normal_one.astype(low)
            inverse[span] = jnp.broadcast_to(inverse_one, (query_rows, inverse.shape[1]))
            normed[span] = (normal_one * attend_gain[...] + attend_shift[...]).astype(low)
            if final:
                after_write((0,), (0, 1))
            if block == 0:
                before_write((), (2,))
                weight_ready(0)
            for part in range(3):
                columns = slice(part * width, (part + 1) * width)
                piece = product(normed[span], joint_w[:, columns])
                if part == 0:
                    piece = piece + joint_bias[:, :width]
                elif part == 2:
                    piece = piece + joint_bias[:, width:]
                joint[span, columns] = piece.astype(low)
            if final:
                after_write((), (2,))
            if block == 0:
                before_write((1,), (3,))
            attend_block(block)
            if final:
                after_write((1,), (3,))
            if block == 0:
                before_write((2,), (4, 5))
                weight_ready(1)
            middle[span] = source[micro, span].astype(wide) + branch_scale * (
                product(attended[span], project_w[...]) + project_bias[...]
            )
            normal_both, inverse_both = normalize(middle[span])
            normal_two[span] = normal_both.astype(low)
            inverse_two[span] = jnp.broadcast_to(inverse_both, (query_rows, inverse.shape[1]))
            normed_two[span] = (normal_both * feed_gain[...] + feed_shift[...]).astype(low)
            if final:
                after_write((2,), (4, 5))
            if block == 0:
                before_write((3,), (6,))
                weight_ready(2)
            for part in range(hidden_width // width):
                columns = slice(part * width, (part + 1) * width)
                hidden = product(normed_two[span], expand_w[:, columns]) + expand_bias[:, columns]
                square = hidden * hidden
                inner = jnp.tanh(hidden * (gelu_scale + (gelu_scale * gelu_cubic) * square))
                gate = 0.5 + 0.5 * inner
                value = hidden * gate
                active[span, columns] = value.astype(low)
                slope[span, columns] = (
                    gate
                    + value
                    * (1.0 - inner)
                    * (gelu_scale + (3.0 * gelu_scale * gelu_cubic) * square)
                ).astype(low)
            if final:
                after_write((3,), (6,))
            if block == 0:
                weight_ready(3)
            result[micro, span] = (
                middle[span]
                + branch_scale * (product(active[span], shrink_w[...]) + shrink_bias[...])
            ).astype(low)

            @pl.when(first)
            def _():
                onward(source, 0, micro, block).start()

        result_out(micro).start()
        return 0

    lax.fori_loop(0, micro_count, forward_micro, 0)
    for micro in range(micro_count):
        result_out(micro).wait()

    @pl.when(first)
    def _():
        for micro in range(micro_count):
            for block in range(block_count):
                onward(source, 0, micro, block).wait_send()

    def add_sum(row, values):
        small[row : row + 1] += jnp.sum(values, axis=0, keepdims=True)

    def attend_block_back(block):
        start, rows = score_rows(block)
        span = block_span(block)
        bottom = block == block_count - 1

        def weight_grad_of(pair):
            values = half_stack(joint[:rows, pair_columns(2, pair)], 1.0)
            return back_product(values, attended_grad[span, pair_columns(0, pair)])

        lane = lax.broadcasted_iota(jnp.int32, (1, pair_width), 1)
        upper = lane >= head_width
        ahead = weight_grad_of(0)
        for pair in range(pair_count):
            weight_grad = ahead
            if pair + 1 < pair_count:
                ahead = weight_grad_of(pair + 1)
            flat = pair_columns(0, pair)
            query = joint[span, flat]
            keys = flipped(joint[:rows, pair_columns(1, pair)]).astype(low)
            out_grad = attended_grad[span, flat]
            key_halves, value_halves, query_halves = [], [], []
            for half in range(2):
                head = slice(half * head_width, (half + 1) * head_width)
                weights = probs[2 * pair + half, start : start + rows]
                weights_wide = weights.astype(wide)
                part_grad = weight_grad[half * rows : (half + 1) * rows]
                delta = jnp.sum(weights_wide * part_grad, axis=0, keepdims=True)
                score_grad = (weights_wide * (part_grad - delta)).astype(low)
                value_halves.append(product(weights, out_grad))
                key_halves.append(product(score_grad, query))
                query_halves.append(product(keys[head], score_grad))
            joint_grad[span, flat] = (
                jnp.concatenate(query_halves, axis=0).T * head_scale
            ).astype(low)
            key_grad = jnp.where(upper, key_halves[1], key_halves[0]) * head_scale
            value_grad = jnp.where(upper, value_halves[1], value_halves[0])
            done = rows - query_rows
            key_done, value_done = key_grad[done:], value_grad[done:]
            if not bottom:
                key_done = key_done + key_part[done:rows, flat]
                value_done = value_done + value_part[done:rows, flat]
            joint_grad[span, pair_columns(1, pair)] = key_done.astype(low)
            joint_grad[span, pair_columns(2, pair)] = value_done.astype(low)
            if done:
                if bottom:
                    key_part[:done, flat] = key_grad[:done]
                    value_part[:done, flat] = value_grad[:done]
                else:
                    key_part[:done, flat] += key_grad[:done]
                    value_part[:done, flat] += value_grad[:done]

    def backward_micro(step, _):
        micro = last - step

        def before_write(index):
            @pl.when(step > 0)
            def _():
                grad_out(index, micro + 1).wait()

        def loaded(*indices):
            @pl.when(step > 0)
            def _():
                for index in indices:
                    keep_load(index, micro).wait()

        def load_next(*indices):
            @pl.when(micro > 0)
            def _():
                for index in indices:
                    keep_load(index, micro - 1).start()

        last_row = jnp.where(first, seq_rows, lengths[0, micro])

        @pl.when(second)
        def _():
            cotangent_load(micro).wait()

        for block in reversed(range(block_count)):
            span = block_span(block)
            opening = block == block_count - 1
            closing = block == 0

            @pl.when(first)
            def _():
                onward(top_grad, 1, micro, block).wait_recv()

            row_pos = block * query_rows + lax.broadcasted_iota(jnp.int32, (query_rows, 1), 0)
            output_grad = jnp.where(row_pos < last_row, top_grad[micro, span].astype(wide), 0.0)
            if opening:
                before_write(0)
            shrink_low = (branch_scale * output_grad).astype(low)
            shrink_grad[span] = shrink_low
            add_sum(5, shrink_low.astype(wide))
            middle[span] = output_grad
            if closing:
                grad_out(0, micro).start()
            if opening:
                before_write(1)
                loaded(6)
            for part in range(hidden_width // width):
                columns = slice(part * width, (part + 1) * width)
                grad = back_product(shrink_grad[span], shrink_w[columns, :])
                grad_low = (grad * slope[span, columns].astype(wide)).astype(low)
                hidden_grad[span, columns] = grad_low
                add_sum(8 + part, grad_low.astype(wide))
            if closing:
                load_next(6)
                grad_out(1, micro).start()
            normed_grad = back_product(hidden_grad[span], expand_w[...])
            if opening:
                loaded(4, 5)
            normal_wide = normal_two[span].astype(wide)
            add_sum(3, normed_grad * normal_wide)
            add_sum(4, normed_grad)
            middle[span] += norm_slope(
                normed_grad * feed_gain[...], normal_wide, inverse_two[span, :1]
            )
            if closing:
                load_next(4, 5)
            if opening:
                before_write(2)
            branch_low = (branch_scale * middle[span]).astype(low)
            branch_grad[span] = branch_low
            add_sum(2, branch_low.astype(wide))
            if closing:
                grad_out(2, micro).start()
            attended_grad[span] = back_product(branch_grad[span], project_w[...]).astype(low)
            if opening:
                before_write(3)
                loaded(2, 3)
            attend_block_back(block)
            if closing:
                load_next(2, 3)
                grad_out(3, micro).start()
            add_sum(6, joint_grad[span, :width].astype(wide))
            add_sum(7, joint_grad[span, 2 * width :].astype(wide))
            normed_grad = back_product(joint_grad[span], joint_w[...])
            if opening:
                before_write(4)
                loaded(0, 1)
            normal_wide = normal[span].astype(wide)
            add_sum(0, normed_grad * normal_wide)
            add_sum(1, normed_grad)
            total = middle[span] + norm_slope(
                normed_grad * attend_gain[...], normal_wide, inverse[span, :1]
            )
            if closing:
                load_next(0, 1)
            source_grad[span] = total
            result[micro, span] = total.astype(low)

            @pl.when(second)
            def _():
                onward(top_grad, 1, micro, block).start()

        grad_out(4, micro).start()
        return 0

    left_out(1, last).wait()
    lax.fori_loop(0, micro_count, backward_micro, 0)
    for index in (0, 2, 3):
        left_out(index, last).wait()
    for index in range(len(grads)):
        grad_out(index, 0).wait()

    @pl.when(second)
    def _():
        for micro in range(micro_count):
            for block in range(block_count):
                onward(top_grad, 1, micro, block).wait_send()


def run_sections(lengths, inputs, cotangent, weights):
    micro_count, seq_rows, width = inputs.shape
    hidden = weights["expand_weight"].shape[1]
    heads = width // head_width
    tokens = micro_count * seq_rows
    blocks = seq_rows // query_rows
    score_total = score_rows(blocks)[0]
    small_rows = -(-(8 + hidden // width) // 8) * 8
    hbm = pl.BlockSpec(memory_space=pl.ANY)
    vmem = pl.BlockSpec(memory_space=pltpu.VMEM)

    def row(name):
        return weights[name].reshape(1, -1)

    def shape(*dims, kind=low):
        return jax.ShapeDtypeStruct(dims, kind)

    return pl.pallas_call(
        sections_kernel,
        name="sections",
        out_shape=(
            shape(micro_count, seq_rows, width),
            shape(tokens, width, kind=wide),
            shape(tokens, width),
            shape(tokens, width),
            shape(tokens, width),
            shape(tokens, hidden),
            shape(tokens, width),
            shape(tokens, hidden),
            shape(tokens, 3 * width),
            shape(tokens, width),
            shape(small_rows, width, kind=wide),
            shape(micro_count, seq_rows, width),
            shape(micro_count, seq_rows, 128, kind=wide),
            shape(micro_count, seq_rows, 3 * width),
            shape(micro_count, heads, score_total, query_rows),
            shape(micro_count, seq_rows, width),
            shape(micro_count, seq_rows, 128, kind=wide),
            shape(micro_count, seq_rows, hidden),
        ),
        in_specs=[hbm] * 7 + [vmem] * 8,
        out_specs=tuple([hbm] * 10 + [vmem] + [hbm] * 7),
        scratch_shapes=[
            pltpu.VMEM((width, 3 * width), low),
            pltpu.VMEM((width, width), low),
            pltpu.VMEM((width, hidden), low),
            pltpu.VMEM((hidden, width), low),
            pltpu.VMEM((micro_count, seq_rows, width), low),
            pltpu.VMEM((micro_count, seq_rows, width), low),
            pltpu.VMEM((micro_count, seq_rows, width), low),
            pltpu.VMEM((seq_rows, width), low),
            pltpu.VMEM((seq_rows, width), low),
            pltpu.VMEM((seq_rows, 128), wide),
            pltpu.VMEM((seq_rows, 3 * width), low),
            pltpu.VMEM((heads, score_total, query_rows), low),
            pltpu.VMEM((seq_rows, width), low),
            pltpu.VMEM((seq_rows, width), wide),
            pltpu.VMEM((seq_rows, width), low),
            pltpu.VMEM((seq_rows, width), low),
            pltpu.VMEM((seq_rows, 128), wide),
            pltpu.VMEM((seq_rows, hidden), low),
            pltpu.VMEM((seq_rows, hidden), low),
            pltpu.VMEM((score_total, query_rows), wide),
            pltpu.VMEM((seq_rows, width), low),
            pltpu.VMEM((seq_rows, hidden), low),
            pltpu.VMEM((seq_rows, 3 * width), low),
            pltpu.VMEM((seq_rows, width), low),
            pltpu.VMEM((seq_rows, width), low),
            pltpu.VMEM((seq_rows, width), wide),
            pltpu.VMEM((max(seq_rows - query_rows, 8), width), wide),
            pltpu.VMEM((max(seq_rows - query_rows, 8), width), wide),
            pltpu.SemaphoreType.DMA((4,)),
            pltpu.SemaphoreType.DMA((micro_count,)),
            pltpu.SemaphoreType.DMA((micro_count, blocks)),
            pltpu.SemaphoreType.DMA((micro_count, blocks)),
            pltpu.SemaphoreType.DMA((micro_count,)),
            pltpu.SemaphoreType.DMA((4,)),
            pltpu.SemaphoreType.DMA((8,)),
            pltpu.SemaphoreType.DMA((8,)),
            pltpu.SemaphoreType.DMA((5,)),
            pltpu.SMEM((1, micro_count), jnp.int32),
            pltpu.SemaphoreType.DMA,
        ],
        compiler_params=pltpu.CompilerParams(
            collective_id=1, has_side_effects=True, vmem_limit_bytes=62 * 2**20
        ),
    )(
        lengths.reshape(1, micro_count),
        inputs,
        cotangent,
        weights["joint_weight"],
        weights["project_weight"],
        weights["expand_weight"],
        weights["shrink_weight"],
        row("attend_gain"),
        row("attend_shift"),
        row("joint_bias"),
        row("project_bias"),
        row("feed_gain"),
        row("feed_shift"),
        row("expand_bias"),
        row("shrink_bias"),
    )


def axis_bits(count):
    bits = []
    step = 1
    while step < count:
        bits.append(step)
        step *= 2
    assert step == count
    return bits


line_length = 4


def line_place():
    return (lax.axis_index("dp") // 2) % line_length


def exchange_bits(dp_count, sub_count):
    bits = [("dp", step) for step in axis_bits(dp_count)]
    near, line, beyond = bits[0], bits[1:3], bits[3:]
    assert len(line) == 2 and sub_count == 2
    return near, ("sub", 1), line, beyond


def partner_id(bit):
    axis, step = bit
    place = {name: lax.axis_index(name) for name in ("pipe", "dp", "sub")}
    place[axis] = place[axis] ^ step
    return (place["pipe"], place["dp"], place["sub"])


def own_bit(bit):
    axis, step = bit
    return (lax.axis_index(axis) // step) % 2


def grad_blocks(width, hidden):
    blocks = [(3, 0, column) for column in range(width // block_cols)]
    blocks += [(2, 0, column) for column in range(3 * width // block_cols)]
    blocks += [(1, 0, column) for column in range(hidden // block_cols)]
    for row in range(hidden // block_rows):
        for column in range(width // block_cols):
            blocks.append((0, row, column))
    return blocks


schedule = (
    (2, 2, 0),
    (0, 2, 1),
    (1, 2, 1),
    (3, 1, 1),
    (0, 2, 2),
    (3, 2, 2),
    (1, 1, 2),
    (0, 1, 4),
    (1, 1, 4),
    (0, 2, 5),
    (1, 2, 5),
    (0, 2, 7),
    (1, 2, 7),
    (3, 2, 8),
    (0, 2, 9),
    (1, 2, 9),
    (0, 2, 10),
    (2, 2, 10),
    (1, 2, 10),
    (3, 2, 11),
)
most_blocks = 2


def exchange_groups():
    groups, start = [], 0
    for kind, size, tick in schedule:
        groups.append((kind, start, size, tick))
        start += size
    return groups


def kind_steps(kind, near, sub, beyond):
    line = [("line", turn) for turn in range(line_length - 1)]
    halves = [("half", sub), ("half", near)] if kind in (1, 3) else [("half", near), ("half", sub)]
    there = halves + line if kind < 2 else line + halves
    there = there + [("whole", bit) for bit in beyond]
    return there


def arrival_rows(steps):
    rows, places, start, line_rows = block_rows, [], 0, 0
    for name, turn in steps:
        if name == "half":
            rows //= 2
            places.append((start, rows))
            start += rows
        elif name == "line":
            if turn == 0:
                line_rows = rows // line_length
                rows = line_rows
            places.append((start, line_rows))
            start += line_rows * (1 if turn == 0 else 2)
        else:
            places.append((start, rows))
            start += rows
    return places, start


def rows_at(offset, rows):
    return pl.ds(pl.multiple_of(offset, 16), rows)


class Exchange:
    def __init__(self, bits, groups, own, arrivals, send_sems, recv_sems, free_sems):
        near, sub, _, beyond = bits
        self.groups, self.own, self.arrivals = groups, own, arrivals
        self.send_sems, self.recv_sems, self.free_sems = send_sems, recv_sems, free_sems
        self.place = line_place()
        self.there = [kind_steps(kind, near, sub, beyond) for kind in range(4)]
        self.there_count = len(self.there[0])
        self.total_steps = 2 * self.there_count - len(beyond)
        self.arrival_places = [arrival_rows(steps)[0] for steps in self.there]
        self.starts = []
        start = 0
        for kind, *_ in groups:
            self.starts.append(start)
            start += arrival_rows(self.there[kind])[1]
        self.offsets = []
        for steps in self.there:
            offset, rows, places = 0, block_rows, []
            for name, what in steps:
                if name == "half":
                    half = rows // 2
                    mine = own_bit(what)
                    keep = offset + mine * half
                    places.append((keep, offset + (1 - mine) * half, half))
                    offset, rows = keep, half
                elif name == "line":
                    if what == 0:
                        line_start, rows = offset, rows // line_length
                        offset = line_start + self.place * rows
                    places.append((line_start, line_start, rows))
                else:
                    places.append((offset, offset, rows))
            self.offsets.append(places)

    def step_of(self, index, step):
        kind = self.groups[index][0]
        if step < self.there_count:
            return kind, step, False
        beyond = self.total_steps - 2 * self.there_count
        return kind, self.there_count - 1 + beyond - (step - self.there_count), True

    def rows(self, index, offset, rows):
        _, first_block, size, _ = self.groups[index]
        return self.own.at[pl.ds(first_block, size), rows_at(offset, rows)]

    def copy(self, index, step, side, source, target, device):
        return pltpu.make_async_remote_copy(
            src_ref=source,
            dst_ref=target,
            send_sem=self.send_sems.at[index, step, side],
            recv_sem=self.recv_sems.at[index, step, side],
            device_id=device,
            device_id_type=MESH,
        )

    def arrival(self, index, there, side):
        kind = self.groups[index][0]
        start, rows = self.arrival_places[kind][there]
        name, turn = self.there[kind][there]
        if name == "line" and turn > 0:
            start += side * rows
        size = self.groups[index][2]
        return self.arrivals.at[pl.ds(0, size), pl.ds(self.starts[index] + start, rows)]

    def neighbour(self, side):
        shift = 2 if side else -2
        return (lax.axis_index("pipe"), lax.axis_index("dp") + shift, lax.axis_index("sub"))

    def line_sends(self, turn, back):
        place, top = self.place, line_length - 1
        if back:
            down = ((place + turn <= top) & (place > 0), place + turn)
            up = ((place - turn >= 0) & (place < top), place - turn)
        else:
            down = ((place >= top - turn) & (place > 0), place - top + turn)
            up = ((place <= turn) & (place < top), place + top - turn)
        return down, up

    def line_gets(self, turn, back):
        place, top = self.place, line_length - 1
        if back:
            below = ((place >= 1) & (place - 1 - turn >= 0), place - 1 - turn)
            above = ((place < top) & (place + 1 + turn <= top), place + 1 + turn)
        else:
            below = ((place >= 1) & (place - 1 <= turn), place + top - 1 - turn)
            above = ((place < top) & (place + 1 >= top - turn), place + 1 - top + turn)
        return below, above

    def line_copy(self, index, step, side, shard):
        kind, there, back = self.step_of(index, step)
        start, _, rows = self.offsets[kind][there]
        source = self.rows(index, start + shard * rows, rows)
        target = source if back else self.arrival(index, there, 1 - side)
        return pltpu.make_async_remote_copy(
            src_ref=source,
            dst_ref=target,
            send_sem=self.send_sems.at[index, step, side],
            recv_sem=self.recv_sems.at[index, step, 1 - side],
            device_id=self.neighbour(side),
            device_id_type=MESH,
        )

    def line_landing(self, index, step, side, shard):
        kind, there, back = self.step_of(index, step)
        start, _, rows = self.offsets[kind][there]
        place = self.rows(index, start + shard * rows, rows)
        target = place if back else self.arrival(index, there, side)
        return self.copy(index, step, side, place, target, self.neighbour(side))

    def pair_copy(self, index, step, landing):
        kind, there, back = self.step_of(index, step)
        keep, give, rows = self.offsets[kind][there]
        bit = self.there[kind][there][1]
        if back:
            source = self.rows(index, keep, rows)
            target = self.rows(index, give if landing else keep, rows)
        else:
            source = self.rows(index, give, rows)
            target = self.arrival(index, there, 0)
        return self.copy(index, step, 0, source, target, partner_id(bit))

    def add(self, index, there, side, offset, rows):
        total = self.rows(index, offset, rows)
        arrived = self.arrival(index, there, side)
        for member in range(self.groups[index][2]):
            total[member] = (
                total[member].astype(jnp.float32) + arrived[member].astype(jnp.float32)
            ).astype(jnp.bfloat16)

    def send(self, index, step):
        kind, there, back = self.step_of(index, step)
        name, what = self.there[kind][there]
        if name != "line":
            if back:
                pl.semaphore_wait(self.free_sems.at[index, there, 0], 1)
            self.pair_copy(index, step, False).start()
            return
        turn = line_length - 2 - what if back else what
        for side, (sends, shard) in enumerate(self.line_sends(turn, back)):

            @pl.when(sends)
            def _():
                if back:
                    pl.semaphore_wait(self.free_sems.at[index, there, side], 1)
                self.line_copy(index, step, side, shard).start()

    def receive(self, index, step):
        kind, there, back = self.step_of(index, step)
        name, what = self.there[kind][there]
        start, _, rows = self.offsets[kind][there]
        if name != "line":
            self.pair_copy(index, step, True).wait()
            if not back:
                self.add(index, there, 0, start, rows)
                if name == "half":
                    pl.semaphore_signal(
                        self.free_sems.at[index, there, 0],
                        inc=1,
                        device_id=partner_id(what),
                        device_id_type=MESH,
                    )
            return
        turn = line_length - 2 - what if back else what
        for side, (sends, shard) in enumerate(self.line_sends(turn, back)):

            @pl.when(sends)
            def _():
                self.line_copy(index, step, side, shard).wait_send()
                if not back:
                    pl.semaphore_signal(
                        self.free_sems.at[index, there, 1 - side],
                        inc=1,
                        device_id=self.neighbour(side),
                        device_id_type=MESH,
                    )

        for side, (gets, shard) in enumerate(self.line_gets(turn, back)):

            @pl.when(gets)
            def _():
                self.line_landing(index, step, side, shard).wait_recv()
                if not back:
                    self.add(index, there, side, start + shard * rows, rows)

    def advance(self, index, step):
        self.receive(index, step - 1)
        if step < self.total_steps:
            self.send(index, step)


def sum_kernel(bits, blocks, *refs):
    lefts, rights, small_in = refs[0:4], refs[4:8], refs[8]
    own, small_out = refs[9:11]
    left_bufs, right_bufs = refs[11:15], refs[15:19]
    arrivals, send_sems, recv_sems, free_sems = refs[19:23]
    small, small_got, load_sems, small_send, small_recv = refs[23:]
    near, sub, line, beyond = bits
    pairs = (near, sub, *line, *beyond)
    stage_count = len(pairs)

    loads = [None] * 4
    for index in reversed(range(4)):
        left_load = pltpu.make_async_copy(lefts[index], left_bufs[index], load_sems.at[2 * index])
        right_load = pltpu.make_async_copy(
            rights[index], right_bufs[index], load_sems.at[2 * index + 1]
        )
        loads[index] = (left_load, right_load)

    def start_load(index):
        if index >= 0:
            for load in loads[index]:
                load.start()

    start_load(3)
    start_load(2)
    loaded = [False] * 4

    groups = exchange_groups()
    exchange = Exchange(bits, groups, own, arrivals, send_sems, recv_sems, free_sems)
    place = line_place()
    barrier = pltpu.get_barrier_semaphore()
    for bit in pairs:
        pl.semaphore_signal(barrier, inc=1, device_id=partner_id(bit), device_id_type=MESH)
    for side, near_end in enumerate((place > 0, place < line_length - 1)):

        @pl.when(near_end)
        def _():
            pl.semaphore_signal(
                barrier, inc=1, device_id=exchange.neighbour(side), device_id_type=MESH
            )

    ends = jnp.where((place == 0) | (place == line_length - 1), 1, 2)
    pl.semaphore_wait(barrier, stage_count + ends)

    def produce(block):
        index, row, column = blocks[block]
        if not loaded[index]:
            loads[index][0].wait()
            loads[index][1].wait()
            loaded[index] = True
            start_load(index - 2)
        left = left_bufs[index][:, row * block_rows : (row + 1) * block_rows]
        right = right_bufs[index][:, column * block_cols : (column + 1) * block_cols]
        own[block] = lax.dot_general(
            left, right, (((0,), (0,)), ((), ())), preferred_element_type=jnp.float32
        ).astype(jnp.bfloat16)

    def small_copy(stage):
        return pltpu.make_async_remote_copy(
            src_ref=small.at[stage],
            dst_ref=small_got.at[stage],
            send_sem=small_send.at[stage],
            recv_sem=small_recv.at[stage],
            device_id=partner_id(pairs[stage]),
            device_id_type=MESH,
        )

    last = max(group[3] for group in groups) + exchange.total_steps
    for tick in range(last + 1):
        for index, (_, start, size, begin) in enumerate(groups):
            if begin == tick:
                for block in range(start, start + size):
                    produce(block)
                exchange.send(index, 0)
        if tick == 0:
            small[0] = small_in[...]
        elif tick <= stage_count:
            small_copy(tick - 1).wait()
            total = small[tick - 1] + small_got[tick - 1]
            if tick < stage_count:
                small[tick] = total
            else:
                small_out[...] = total
        if tick < stage_count:
            small_copy(tick).start()
        for step in range(1, exchange.total_steps + 1):
            for index, (*_, begin) in enumerate(groups):
                if begin + step == tick:
                    exchange.advance(index, step)


def summed_grads(lefts, rights, small, dp_count, sub_count):
    tokens, width = lefts[3].shape
    hidden = lefts[0].shape[1]
    bits = exchange_bits(dp_count, sub_count)
    near, sub, line, beyond = bits
    stage_count = 2 + len(line) + len(beyond)
    blocks = grad_blocks(width, hidden)
    block_count = len(blocks)
    groups = exchange_groups()
    assert sum(group[2] for group in groups) == block_count
    there = kind_steps(0, near, sub, beyond)
    steps = 2 * len(there) - len(beyond)
    rows = sum(arrival_rows(kind_steps(kind, near, sub, beyond))[1] for kind, *_ in groups)
    low = jnp.bfloat16
    hbm = pl.BlockSpec(memory_space=pl.ANY)
    vmem = pl.BlockSpec(memory_space=pltpu.VMEM)
    return pl.pallas_call(
        functools.partial(sum_kernel, bits, blocks),
        name="grad_sums",
        out_shape=(
            pltpu.VMEM((block_count, block_rows, block_cols), low),
            pltpu.VMEM(small.shape, jnp.float32),
        ),
        in_specs=[hbm] * 8 + [vmem],
        out_specs=(vmem, vmem),
        scratch_shapes=[pltpu.VMEM(array.shape, low) for array in lefts]
        + [pltpu.VMEM(array.shape, low) for array in rights]
        + [
            pltpu.VMEM((most_blocks, rows, block_cols), low),
            pltpu.SemaphoreType.DMA((len(groups), steps, 2)),
            pltpu.SemaphoreType.DMA((len(groups), steps, 2)),
            pltpu.SemaphoreType.REGULAR((len(groups), len(there), 2)),
            pltpu.VMEM((stage_count, *small.shape), jnp.float32),
            pltpu.VMEM((stage_count, *small.shape), jnp.float32),
            pltpu.SemaphoreType.DMA((8,)),
            pltpu.SemaphoreType.DMA((stage_count,)),
            pltpu.SemaphoreType.DMA((stage_count,)),
        ],
        compiler_params=pltpu.CompilerParams(
            collective_id=0, has_side_effects=True, vmem_limit_bytes=46 * 2**20
        ),
    )(*lefts, *rights, small)


stage_count_out = 6


def finish_kernel(
    blocks,
    own,
    small,
    outputs_in,
    grads_in,
    outputs,
    input_grads,
    attend_gain,
    attend_shift,
    joint,
    joint_bias,
    project,
    project_bias,
    feed_gain,
    feed_shift,
    expand,
    expand_bias,
    shrink,
    shrink_bias,
    stages,
    stage_sems,
    pass_sems,
    outputs_buf,
    grads_buf,
):
    places = (shrink, expand, joint, project)
    width = shrink_bias.shape[1]
    pass_loads = [
        pltpu.make_async_copy(outputs_in, outputs_buf, pass_sems.at[0]),
        pltpu.make_async_copy(grads_in, grads_buf, pass_sems.at[1]),
    ]
    passes = [
        pltpu.make_async_copy(outputs_buf, outputs, pass_sems.at[2]),
        pltpu.make_async_copy(grads_buf, input_grads, pass_sems.at[3]),
    ]
    for copy in pass_loads:
        copy.start()

    def block_copy(block):
        index, row, column = blocks[block]
        slot = block % stage_count_out
        return pltpu.make_async_copy(
            stages.at[slot],
            places[index].at[
                pl.ds(row * block_rows, block_rows), pl.ds(column * block_cols, block_cols)
            ],
            stage_sems.at[slot],
        )

    for block in range(len(blocks)):
        if block >= stage_count_out:
            block_copy(block - stage_count_out).wait()
        stages[block % stage_count_out] = own[block].astype(jnp.float32)
        block_copy(block).start()
        if block == len(blocks) // 2:
            for load, copy in zip(pass_loads, passes):
                load.wait()
                copy.start()
    for row, place in (
        (0, attend_gain),
        (1, attend_shift),
        (2, project_bias),
        (3, feed_gain),
        (4, feed_shift),
        (5, shrink_bias),
        (6, joint_bias),
        (8, expand_bias),
    ):
        for part in range(place.shape[1] // width):
            place[:, part * width : (part + 1) * width] = small[row + part : row + part + 1]
    for block in range(max(0, len(blocks) - stage_count_out), len(blocks)):
        block_copy(block).wait()
    for copy in passes:
        copy.wait()


def finished(own, small, outputs, input_grads, width, hidden):
    blocks = grad_blocks(width, hidden)
    hbm = pl.BlockSpec(memory_space=pl.ANY)
    vmem = pl.BlockSpec(memory_space=pltpu.VMEM)

    def shape(*dims):
        return jax.ShapeDtypeStruct(dims, jnp.float32)

    return pl.pallas_call(
        functools.partial(finish_kernel, blocks),
        name="finish",
        out_shape=(
            jax.ShapeDtypeStruct(outputs.shape, outputs.dtype),
            jax.ShapeDtypeStruct(input_grads.shape, input_grads.dtype),
            shape(1, width),
            shape(1, width),
            shape(width, 3 * width),
            shape(1, 2 * width),
            shape(width, width),
            shape(1, width),
            shape(1, width),
            shape(1, width),
            shape(width, hidden),
            shape(1, hidden),
            shape(hidden, width),
            shape(1, width),
        ),
        in_specs=[vmem, vmem, hbm, hbm],
        out_specs=(
            hbm, hbm, vmem, vmem, hbm, vmem, hbm, vmem, vmem, vmem, hbm, vmem, hbm, vmem
        ),
        scratch_shapes=[
            pltpu.VMEM((stage_count_out, block_rows, block_cols), jnp.float32),
            pltpu.SemaphoreType.DMA((stage_count_out,)),
            pltpu.SemaphoreType.DMA((4,)),
            pltpu.VMEM(outputs.shape, outputs.dtype),
            pltpu.VMEM(input_grads.shape, input_grads.dtype),
        ],
        compiler_params=pltpu.CompilerParams(vmem_limit_bytes=16 * 2**20),
    )(
        pltpu.with_memory_space_constraint(own, pltpu.VMEM),
        pltpu.with_memory_space_constraint(small, pltpu.VMEM),
        pltpu.with_memory_space_constraint(outputs, pltpu.HBM),
        pltpu.with_memory_space_constraint(input_grads, pltpu.HBM),
    )


weight_names = (
    "attend_gain",
    "attend_shift",
    "joint_weight",
    "joint_bias",
    "project_weight",
    "project_bias",
    "feed_gain",
    "feed_shift",
    "expand_weight",
    "expand_bias",
    "shrink_weight",
    "shrink_bias",
)


def body(inputs, cotangent, lengths, *params):
    weights = {name: param[0] for name, param in zip(weight_names, params)}
    micro_count, _, seq_rows, width = inputs.shape
    (
        outputs,
        input_grads,
        normed,
        attended,
        normed_two,
        active,
        shrink_grad,
        hidden_grad,
        joint_grad,
        branch_grad,
        small,
        *_,
    ) = run_sections(lengths, inputs[:, 0], cotangent[:, 0], weights)
    hidden = active.shape[1]
    own, small_sum = summed_grads(
        (active, normed_two, normed, attended),
        (shrink_grad, hidden_grad, joint_grad, branch_grad),
        small,
        lax.axis_size("dp"),
        lax.axis_size("sub"),
    )
    outputs, input_grads, *full_grads = finished(
        own, small_sum, outputs, input_grads, width, hidden
    )
    return (
        outputs[None, :, None],
        input_grads.reshape(1, micro_count, 1, seq_rows, width),
        *(grad if grad.shape[0] == 1 else grad[None] for grad in full_grads),
    )


def solution(mesh):
    in_specs = (
        P(None, ("dp", "sub"), None, None),
        P(None, ("dp", "sub"), None, None),
        P(None, ("dp", "sub")),
        P("pipe", None),
        P("pipe", None),
        P("pipe", None, None),
        P("pipe", None),
        P("pipe", None, None),
        P("pipe", None),
        P("pipe", None),
        P("pipe", None),
        P("pipe", None, None),
        P("pipe", None),
        P("pipe", None, None),
        P("pipe", None),
    )
    out_specs = (
        P("pipe", None, ("dp", "sub"), None, None),
        P("pipe", None, ("dp", "sub"), None, None),
        P("pipe", None),
        P("pipe", None),
        P("pipe", None, None),
        P("pipe", None),
        P("pipe", None, None),
        P("pipe", None),
        P("pipe", None),
        P("pipe", None),
        P("pipe", None, None),
        P("pipe", None),
        P("pipe", None, None),
        P("pipe", None),
    )
    return jax.shard_map(body, mesh=mesh, in_specs=in_specs, out_specs=out_specs, check_vma=False)
```

```python
import functools

import jax
import jax.numpy as jnp
from jax import lax
from jax.experimental import pallas as pl
from jax.experimental.pallas import tpu as pltpu
from jax.sharding import PartitionSpec as P

MESH = pl.DeviceIdType.MESH
branch_scale = 24.0 ** (-0.5)
head_scale = 0.125
norm_eps = 1e-05
gelu_scale = (2.0 / 3.141592653589793) ** 0.5
gelu_cubic = 0.044715
masked_score = -1e30
low = jnp.bfloat16
wide = jnp.float32
head_width = 64
pair_width = 128
query_rows = 256
block_rows = 768
block_cols = 256


def product(left, right):
    return jnp.dot(left, right, preferred_element_type=wide)


def back_product(left, right):
    return lax.dot_general(left, right, (((1,), (1,)), ((), ())), preferred_element_type=wide)


def flipped(matrix):
    return matrix.astype(wide).T


def sibling():
    return (1 - lax.axis_index("pipe"), lax.axis_index("dp"), lax.axis_index("sub"))


def greet_sibling():
    barrier = pltpu.get_barrier_semaphore()
    pl.semaphore_signal(barrier, inc=1, device_id=sibling(), device_id_type=MESH)
    pl.semaphore_wait(barrier, 1)


def pair_mask(half, value):
    lane = lax.broadcasted_iota(jnp.int32, (1, pair_width), 1)
    return jnp.where((lane // head_width) == half, value, 0.0).astype(low)


def score_rows(block):
    first = query_rows * (block * (block + 1) // 2)
    return first, query_rows * (block + 1)


def normalize(values):
    center = values - jnp.mean(values, axis=-1, keepdims=True)
    inverse = lax.rsqrt(jnp.mean(center * center, axis=-1, keepdims=True) + norm_eps)
    return center * inverse, inverse


def norm_slope(graded, normal, inverse):
    return inverse * (
        graded
        - jnp.mean(graded, axis=-1, keepdims=True)
        - normal * jnp.mean(graded * normal, axis=-1, keepdims=True)
    )


def half_stack(matrix, value):
    return jnp.concatenate(
        [matrix * pair_mask(0, value), matrix * pair_mask(1, value)], axis=0
    )


def sections_kernel(
    lengths_in,
    inputs,
    cotangent,
    joint_weight,
    project_weight,
    expand_weight,
    shrink_weight,
    attend_gain,
    attend_shift,
    joint_bias,
    project_bias,
    feed_gain,
    feed_shift,
    expand_bias,
    shrink_bias,
    outputs,
    input_grads,
    normed_out,
    attended_out,
    normed_two_out,
    active_out,
    shrink_grad_out,
    hidden_grad_out,
    joint_grad_out,
    branch_grad_out,
    small,
    normal_out,
    inverse_out,
    joint_out,
    probs_out,
    normal_two_out,
    inverse_two_out,
    slope_out,
    joint_w,
    project_w,
    expand_w,
    shrink_w,
    source,
    result,
    top_grad,
    normed,
    normal,
    inverse,
    joint,
    probs,
    attended,
    middle,
    normed_two,
    normal_two,
    inverse_two,
    active,
    slope,
    mask,
    shrink_grad,
    hidden_grad,
    joint_grad,
    branch_grad,
    attended_grad,
    source_grad,
    key_part,
    value_part,
    weight_sems,
    source_sems,
    send_sems,
    recv_sems,
    result_sems,
    left_sems,
    keep_sems,
    load_sems,
    grad_sems,
    lengths,
    lengths_sem,
):
    first = lax.axis_index("pipe") == 0
    second = jnp.logical_not(first)
    micro_count, seq_rows, width = source.shape
    hidden_width = expand_w.shape[1]
    pair_count = width // pair_width
    block_count = seq_rows // query_rows
    last = micro_count - 1
    weight_loads = [
        pltpu.make_async_copy(place, buffer, weight_sems.at[index])
        for index, (place, buffer) in enumerate(
            (
                (joint_weight, joint_w),
                (project_weight, project_w),
                (expand_weight, expand_w),
                (shrink_weight, shrink_w),
            )
        )
    ]
    lefts = (
        (normed, normed_out),
        (attended, attended_out),
        (normed_two, normed_two_out),
        (active, active_out),
    )
    kept = (
        (normal, normal_out),
        (inverse, inverse_out),
        (joint, joint_out),
        (probs, probs_out),
        (normal_two, normal_two_out),
        (inverse_two, inverse_two_out),
        (slope, slope_out),
    )
    grads = (
        (shrink_grad, shrink_grad_out),
        (hidden_grad, hidden_grad_out),
        (branch_grad, branch_grad_out),
        (joint_grad, joint_grad_out),
        (source_grad, input_grads),
    )

    def block_span(block):
        return slice(block * query_rows, (block + 1) * query_rows)

    def micro_rows(micro):
        return pl.ds(pl.multiple_of(micro * seq_rows, seq_rows), seq_rows)

    def input_load(micro):
        return pltpu.make_async_copy(inputs.at[micro], source.at[micro], source_sems.at[micro])

    def cotangent_load(micro):
        return pltpu.make_async_copy(
            cotangent.at[micro], top_grad.at[micro], source_sems.at[micro]
        )

    def onward(target, phase, micro, block):
        return pltpu.make_async_remote_copy(
            src_ref=result.at[micro, block_span(block)],
            dst_ref=target.at[micro, block_span(block)],
            send_sem=send_sems.at[micro, block],
            recv_sem=recv_sems.at[micro, block],
            device_id=sibling(),
            device_id_type=MESH,
        )

    def result_out(micro):
        return pltpu.make_async_copy(
            result.at[micro], outputs.at[micro], result_sems.at[micro]
        )

    def left_out(index, micro):
        buffer, place = lefts[index]
        return pltpu.make_async_copy(buffer, place.at[micro_rows(micro)], left_sems.at[index])

    def keep_place(index, micro):
        return kept[index][1].at[micro]

    def keep_out(index, micro):
        return pltpu.make_async_copy(kept[index][0], keep_place(index, micro), keep_sems.at[index])

    def keep_load(index, micro):
        return pltpu.make_async_copy(keep_place(index, micro), kept[index][0], load_sems.at[index])

    def grad_out(index, micro):
        buffer, place = grads[index]
        return pltpu.make_async_copy(buffer, place.at[micro_rows(micro)], grad_sems.at[index])

    lengths_load = pltpu.make_async_copy(lengths_in, lengths, lengths_sem)
    lengths_load.start()

    @pl.when(first)
    def _():
        for micro in range(micro_count):
            input_load(micro).start()

    weight_loads[0].start()

    @pl.when(second)
    def _():
        for micro in range(micro_count):
            cotangent_load(micro).start()

    greet_sibling()
    small[...] = jnp.zeros_like(small)
    lengths_load.wait()

    def pair_columns(part, pair):
        start = part * width + pair * pair_width
        return slice(start, start + pair_width)

    def attend_block(block):
        start, rows = score_rows(block)
        span = block_span(block)

        def scores_of(pair):
            keys = half_stack(joint[:rows, pair_columns(1, pair)], head_scale)
            return back_product(keys, joint[span, pair_columns(0, pair)])

        def mix(pair, weights):
            values = flipped(joint[:rows, pair_columns(2, pair)]).astype(low)
            halves = [
                product(values[half * head_width : (half + 1) * head_width], weights[half])
                for half in range(2)
            ]
            attended[span, pair_columns(0, pair)] = (
                jnp.concatenate(halves, axis=0).T.astype(low)
            )

        ahead = scores_of(0)
        behind = None
        for pair in range(pair_count):
            scores = ahead
            if pair + 1 < pair_count:
                ahead = scores_of(pair + 1)
            if behind is not None:
                mix(*behind)
            weights = []
            for half in range(2):
                masked = scores[half * rows : (half + 1) * rows] + mask[start : start + rows]
                exponent = jnp.exp(masked - jnp.max(masked, axis=0, keepdims=True))
                part = exponent * (1.0 / jnp.sum(exponent, axis=0, keepdims=True))
                part = part.astype(low)
                probs[2 * pair + half, start : start + rows] = part
                weights.append(part)
            behind = (pair, weights)
        mix(*behind)

    def forward_micro(micro, _):
        def before_write(left_indices, keep_indices):
            @pl.when(micro > 0)
            def _():
                for index in left_indices:
                    left_out(index, micro - 1).wait()
                for index in keep_indices:
                    keep_out(index, micro - 1).wait()

        def after_write(left_indices, keep_indices):
            for index in left_indices:
                left_out(index, micro).start()

            @pl.when(micro < last)
            def _():
                for index in keep_indices:
                    keep_out(index, micro).start()

        def weight_ready(index):
            @pl.when(micro == 0)
            def _():
                weight_loads[index].wait()
                if index == 0:
                    for load in weight_loads[1:]:
                        load.start()

        length = lengths[0, micro]
        for block in range(block_count):
            start, rows = score_rows(block)
            key_pos = lax.broadcasted_iota(jnp.int32, (rows, query_rows), 0)
            query_pos = block * query_rows + lax.broadcasted_iota(
                jnp.int32, (rows, query_rows), 1
            )
            allowed = (key_pos <= query_pos) & (key_pos < length)
            mask[start : start + rows] = jnp.where(allowed, 0.0, masked_score)

        @pl.when(first)
        def _():
            input_load(micro).wait()

        for block in range(block_count):
            span = block_span(block)
            final = block == block_count - 1

            @pl.when(second)
            def _():
                onward(source, 0, micro, block).wait_recv()

            if block == 0:
                before_write((0,), (0, 1))
            normal_one, inverse_one = normalize(source[micro, span].astype(wide))
            normal[span] = normal_one.astype(low)
            inverse[span] = jnp.broadcast_to(inverse_one, (query_rows, inverse.shape[1]))
            normed[span] = (normal_one * attend_gain[...] + attend_shift[...]).astype(low)
            if final:
                after_write((0,), (0, 1))
            if block == 0:
                before_write((), (2,))
                weight_ready(0)
            for part in range(3):
                columns = slice(part * width, (part + 1) * width)
                piece = product(normed[span], joint_w[:, columns])
                if part == 0:
                    piece = piece + joint_bias[:, :width]
                elif part == 2:
                    piece = piece + joint_bias[:, width:]
                joint[span, columns] = piece.astype(low)
            if final:
                after_write((), (2,))
            if block == 0:
                before_write((1,), (3,))
            attend_block(block)
            if final:
                after_write((1,), (3,))
            if block == 0:
                before_write((2,), (4, 5))
                weight_ready(1)
            middle[span] = source[micro, span].astype(wide) + branch_scale * (
                product(attended[span], project_w[...]) + project_bias[...]
            )
            normal_both, inverse_both = normalize(middle[span])
            normal_two[span] = normal_both.astype(low)
            inverse_two[span] = jnp.broadcast_to(inverse_both, (query_rows, inverse.shape[1]))
            normed_two[span] = (normal_both * feed_gain[...] + feed_shift[...]).astype(low)
            if final:
                after_write((2,), (4, 5))
            if block == 0:
                before_write((3,), (6,))
                weight_ready(2)
            for part in range(hidden_width // width):
                columns = slice(part * width, (part + 1) * width)
                hidden = product(normed_two[span], expand_w[:, columns]) + expand_bias[:, columns]
                square = hidden * hidden
                inner = jnp.tanh(hidden * (gelu_scale + (gelu_scale * gelu_cubic) * square))
                gate = 0.5 + 0.5 * inner
                value = hidden * gate
                active[span, columns] = value.astype(low)
                slope[span, columns] = (
                    gate
                    + value
                    * (1.0 - inner)
                    * (gelu_scale + (3.0 * gelu_scale * gelu_cubic) * square)
                ).astype(low)
            if final:
                after_write((3,), (6,))
            if block == 0:
                weight_ready(3)
            result[micro, span] = (
                middle[span]
                + branch_scale * (product(active[span], shrink_w[...]) + shrink_bias[...])
            ).astype(low)

            @pl.when(first)
            def _():
                onward(source, 0, micro, block).start()

        result_out(micro).start()
        return 0

    lax.fori_loop(0, micro_count, forward_micro, 0)
    for micro in range(micro_count):
        result_out(micro).wait()

    @pl.when(first)
    def _():
        for micro in range(micro_count):
            for block in range(block_count):
                onward(source, 0, micro, block).wait_send()

    def add_sum(row, values):
        small[row : row + 1] += jnp.sum(values, axis=0, keepdims=True)

    def attend_block_back(block):
        start, rows = score_rows(block)
        span = block_span(block)
        bottom = block == block_count - 1

        def weight_grad_of(pair):
            values = half_stack(joint[:rows, pair_columns(2, pair)], 1.0)
            return back_product(values, attended_grad[span, pair_columns(0, pair)])

        lane = lax.broadcasted_iota(jnp.int32, (1, pair_width), 1)
        upper = lane >= head_width
        ahead = weight_grad_of(0)
        for pair in range(pair_count):
            weight_grad = ahead
            if pair + 1 < pair_count:
                ahead = weight_grad_of(pair + 1)
            flat = pair_columns(0, pair)
            query = joint[span, flat]
            keys = flipped(joint[:rows, pair_columns(1, pair)]).astype(low)
            out_grad = attended_grad[span, flat]
            key_halves, value_halves, query_halves = [], [], []
            for half in range(2):
                head = slice(half * head_width, (half + 1) * head_width)
                weights = probs[2 * pair + half, start : start + rows]
                weights_wide = weights.astype(wide)
                part_grad = weight_grad[half * rows : (half + 1) * rows]
                delta = jnp.sum(weights_wide * part_grad, axis=0, keepdims=True)
                score_grad = (weights_wide * (part_grad - delta)).astype(low)
                value_halves.append(product(weights, out_grad))
                key_halves.append(product(score_grad, query))
                query_halves.append(product(keys[head], score_grad))
            joint_grad[span, flat] = (
                jnp.concatenate(query_halves, axis=0).T * head_scale
            ).astype(low)
            key_grad = jnp.where(upper, key_halves[1], key_halves[0]) * head_scale
            value_grad = jnp.where(upper, value_halves[1], value_halves[0])
            done = rows - query_rows
            key_done, value_done = key_grad[done:], value_grad[done:]
            if not bottom:
                key_done = key_done + key_part[done:rows, flat]
                value_done = value_done + value_part[done:rows, flat]
            joint_grad[span, pair_columns(1, pair)] = key_done.astype(low)
            joint_grad[span, pair_columns(2, pair)] = value_done.astype(low)
            if done:
                if bottom:
                    key_part[:done, flat] = key_grad[:done]
                    value_part[:done, flat] = value_grad[:done]
                else:
                    key_part[:done, flat] += key_grad[:done]
                    value_part[:done, flat] += value_grad[:done]

    def backward_micro(step, _):
        micro = last - step

        def before_write(index):
            @pl.when(step > 0)
            def _():
                grad_out(index, micro + 1).wait()

        def loaded(*indices):
            @pl.when(step > 0)
            def _():
                for index in indices:
                    keep_load(index, micro).wait()

        def load_next(*indices):
            @pl.when(micro > 0)
            def _():
                for index in indices:
                    keep_load(index, micro - 1).start()

        last_row = jnp.where(first, seq_rows, lengths[0, micro])

        @pl.when(second)
        def _():
            cotangent_load(micro).wait()

        for block in reversed(range(block_count)):
            span = block_span(block)
            opening = block == block_count - 1
            closing = block == 0

            @pl.when(first)
            def _():
                onward(top_grad, 1, micro, block).wait_recv()

            row_pos = block * query_rows + lax.broadcasted_iota(jnp.int32, (query_rows, 1), 0)
            output_grad = jnp.where(row_pos < last_row, top_grad[micro, span].astype(wide), 0.0)
            if opening:
                before_write(0)
            shrink_low = (branch_scale * output_grad).astype(low)
            shrink_grad[span] = shrink_low
            add_sum(5, shrink_low.astype(wide))
            middle[span] = output_grad
            if closing:
                grad_out(0, micro).start()
            if opening:
                before_write(1)
                loaded(6)
            for part in range(hidden_width // width):
                columns = slice(part * width, (part + 1) * width)
                grad = back_product(shrink_grad[span], shrink_w[columns, :])
                grad_low = (grad * slope[span, columns].astype(wide)).astype(low)
                hidden_grad[span, columns] = grad_low
                add_sum(8 + part, grad_low.astype(wide))
            if closing:
                load_next(6)
                grad_out(1, micro).start()
            normed_grad = back_product(hidden_grad[span], expand_w[...])
            if opening:
                loaded(4, 5)
            normal_wide = normal_two[span].astype(wide)
            add_sum(3, normed_grad * normal_wide)
            add_sum(4, normed_grad)
            middle[span] += norm_slope(
                normed_grad * feed_gain[...], normal_wide, inverse_two[span, :1]
            )
            if closing:
                load_next(4, 5)
            if opening:
                before_write(2)
            branch_low = (branch_scale * middle[span]).astype(low)
            branch_grad[span] = branch_low
            add_sum(2, branch_low.astype(wide))
            if closing:
                grad_out(2, micro).start()
            attended_grad[span] = back_product(branch_grad[span], project_w[...]).astype(low)
            if opening:
                before_write(3)
                loaded(2, 3)
            attend_block_back(block)
            if closing:
                load_next(2, 3)
                grad_out(3, micro).start()
            add_sum(6, joint_grad[span, :width].astype(wide))
            add_sum(7, joint_grad[span, 2 * width :].astype(wide))
            normed_grad = back_product(joint_grad[span], joint_w[...])
            if opening:
                before_write(4)
                loaded(0, 1)
            normal_wide = normal[span].astype(wide)
            add_sum(0, normed_grad * normal_wide)
            add_sum(1, normed_grad)
            total = middle[span] + norm_slope(
                normed_grad * attend_gain[...], normal_wide, inverse[span, :1]
            )
            if closing:
                load_next(0, 1)
            source_grad[span] = total
            result[micro, span] = total.astype(low)

            @pl.when(second)
            def _():
                onward(top_grad, 1, micro, block).start()

        grad_out(4, micro).start()
        return 0

    left_out(1, last).wait()
    lax.fori_loop(0, micro_count, backward_micro, 0)
    for index in (0, 2, 3):
        left_out(index, last).wait()
    for index in range(len(grads)):
        grad_out(index, 0).wait()

    @pl.when(second)
    def _():
        for micro in range(micro_count):
            for block in range(block_count):
                onward(top_grad, 1, micro, block).wait_send()


def run_sections(lengths, inputs, cotangent, weights):
    micro_count, seq_rows, width = inputs.shape
    hidden = weights["expand_weight"].shape[1]
    heads = width // head_width
    tokens = micro_count * seq_rows
    blocks = seq_rows // query_rows
    score_total = score_rows(blocks)[0]
    small_rows = -(-(8 + hidden // width) // 8) * 8
    hbm = pl.BlockSpec(memory_space=pl.ANY)
    vmem = pl.BlockSpec(memory_space=pltpu.VMEM)

    def row(name):
        return weights[name].reshape(1, -1)

    def shape(*dims, kind=low):
        return jax.ShapeDtypeStruct(dims, kind)

    return pl.pallas_call(
        sections_kernel,
        name="sections",
        out_shape=(
            shape(micro_count, seq_rows, width),
            shape(tokens, width, kind=wide),
            shape(tokens, width),
            shape(tokens, width),
            shape(tokens, width),
            shape(tokens, hidden),
            shape(tokens, width),
            shape(tokens, hidden),
            shape(tokens, 3 * width),
            shape(tokens, width),
            shape(small_rows, width, kind=wide),
            shape(micro_count, seq_rows, width),
            shape(micro_count, seq_rows, 128, kind=wide),
            shape(micro_count, seq_rows, 3 * width),
            shape(micro_count, heads, score_total, query_rows),
            shape(micro_count, seq_rows, width),
            shape(micro_count, seq_rows, 128, kind=wide),
            shape(micro_count, seq_rows, hidden),
        ),
        in_specs=[hbm] * 7 + [vmem] * 8,
        out_specs=tuple([hbm] * 10 + [vmem] + [hbm] * 7),
        scratch_shapes=[
            pltpu.VMEM((width, 3 * width), low),
            pltpu.VMEM((width, width), low),
            pltpu.VMEM((width, hidden), low),
            pltpu.VMEM((hidden, width), low),
            pltpu.VMEM((micro_count, seq_rows, width), low),
            pltpu.VMEM((micro_count, seq_rows, width), low),
            pltpu.VMEM((micro_count, seq_rows, width), low),
            pltpu.VMEM((seq_rows, width), low),
            pltpu.VMEM((seq_rows, width), low),
            pltpu.VMEM((seq_rows, 128), wide),
            pltpu.VMEM((seq_rows, 3 * width), low),
            pltpu.VMEM((heads, score_total, query_rows), low),
            pltpu.VMEM((seq_rows, width), low),
            pltpu.VMEM((seq_rows, width), wide),
            pltpu.VMEM((seq_rows, width), low),
            pltpu.VMEM((seq_rows, width), low),
            pltpu.VMEM((seq_rows, 128), wide),
            pltpu.VMEM((seq_rows, hidden), low),
            pltpu.VMEM((seq_rows, hidden), low),
            pltpu.VMEM((score_total, query_rows), wide),
            pltpu.VMEM((seq_rows, width), low),
            pltpu.VMEM((seq_rows, hidden), low),
            pltpu.VMEM((seq_rows, 3 * width), low),
            pltpu.VMEM((seq_rows, width), low),
            pltpu.VMEM((seq_rows, width), low),
            pltpu.VMEM((seq_rows, width), wide),
            pltpu.VMEM((max(seq_rows - query_rows, 8), width), wide),
            pltpu.VMEM((max(seq_rows - query_rows, 8), width), wide),
            pltpu.SemaphoreType.DMA((4,)),
            pltpu.SemaphoreType.DMA((micro_count,)),
            pltpu.SemaphoreType.DMA((micro_count, blocks)),
            pltpu.SemaphoreType.DMA((micro_count, blocks)),
            pltpu.SemaphoreType.DMA((micro_count,)),
            pltpu.SemaphoreType.DMA((4,)),
            pltpu.SemaphoreType.DMA((8,)),
            pltpu.SemaphoreType.DMA((8,)),
            pltpu.SemaphoreType.DMA((5,)),
            pltpu.SMEM((1, micro_count), jnp.int32),
            pltpu.SemaphoreType.DMA,
        ],
        compiler_params=pltpu.CompilerParams(
            collective_id=1, has_side_effects=True, vmem_limit_bytes=62 * 2**20
        ),
    )(
        lengths.reshape(1, micro_count),
        inputs,
        cotangent,
        weights["joint_weight"],
        weights["project_weight"],
        weights["expand_weight"],
        weights["shrink_weight"],
        row("attend_gain"),
        row("attend_shift"),
        row("joint_bias"),
        row("project_bias"),
        row("feed_gain"),
        row("feed_shift"),
        row("expand_bias"),
        row("shrink_bias"),
    )


def axis_bits(count):
    bits = []
    step = 1
    while step < count:
        bits.append(step)
        step *= 2
    assert step == count
    return bits


line_length = 4


def line_place():
    return (lax.axis_index("dp") // 2) % line_length


def exchange_bits(dp_count, sub_count):
    bits = [("dp", step) for step in axis_bits(dp_count)]
    near, line, beyond = bits[0], bits[1:3], bits[3:]
    assert len(line) == 2 and sub_count == 2
    return near, ("sub", 1), line, beyond


def partner_id(bit):
    axis, step = bit
    place = {name: lax.axis_index(name) for name in ("pipe", "dp", "sub")}
    place[axis] = place[axis] ^ step
    return (place["pipe"], place["dp"], place["sub"])


def own_bit(bit):
    axis, step = bit
    return (lax.axis_index(axis) // step) % 2


def grad_blocks(width, hidden):
    blocks = [(3, 0, column) for column in range(width // block_cols)]
    blocks += [(2, 0, column) for column in range(3 * width // block_cols)]
    blocks += [(1, 0, column) for column in range(hidden // block_cols)]
    for row in range(hidden // block_rows):
        for column in range(width // block_cols):
            blocks.append((0, row, column))
    return blocks


schedule = (
    (2, 2, 0),
    (0, 2, 1),
    (1, 2, 1),
    (3, 1, 1),
    (0, 2, 2),
    (3, 2, 2),
    (1, 1, 2),
    (0, 1, 4),
    (1, 1, 4),
    (0, 2, 5),
    (1, 2, 5),
    (0, 2, 7),
    (1, 2, 7),
    (3, 2, 8),
    (0, 2, 9),
    (1, 2, 9),
    (0, 2, 10),
    (2, 2, 10),
    (1, 2, 10),
    (3, 2, 11),
)
most_blocks = 2


def exchange_groups():
    groups, start = [], 0
    for kind, size, tick in schedule:
        groups.append((kind, start, size, tick))
        start += size
    return groups


def kind_steps(kind, near, sub, beyond):
    line = [("line", turn) for turn in range(line_length - 1)]
    halves = [("half", sub), ("half", near)] if kind in (1, 3) else [("half", near), ("half", sub)]
    there = halves + line if kind < 2 else line + halves
    there = there + [("whole", bit) for bit in beyond]
    return there


def arrival_rows(steps):
    rows, places, start, line_rows = block_rows, [], 0, 0
    for name, turn in steps:
        if name == "half":
            rows //= 2
            places.append((start, rows))
            start += rows
        elif name == "line":
            if turn == 0:
                line_rows = rows // line_length
                rows = line_rows
            places.append((start, line_rows))
            start += line_rows * (1 if turn == 0 else 2)
        else:
            places.append((start, rows))
            start += rows
    return places, start


def rows_at(offset, rows):
    return pl.ds(pl.multiple_of(offset, 16), rows)


class Exchange:
    def __init__(self, bits, groups, own, arrivals, send_sems, recv_sems, free_sems):
        near, sub, _, beyond = bits
        self.groups, self.own, self.arrivals = groups, own, arrivals
        self.send_sems, self.recv_sems, self.free_sems = send_sems, recv_sems, free_sems
        self.place = line_place()
        self.there = [kind_steps(kind, near, sub, beyond) for kind in range(4)]
        self.there_count = len(self.there[0])
        self.total_steps = 2 * self.there_count - len(beyond)
        self.arrival_places = [arrival_rows(steps)[0] for steps in self.there]
        self.starts = []
        start = 0
        for kind, *_ in groups:
            self.starts.append(start)
            start += arrival_rows(self.there[kind])[1]
        self.offsets = []
        for steps in self.there:
            offset, rows, places = 0, block_rows, []
            for name, what in steps:
                if name == "half":
                    half = rows // 2
                    mine = own_bit(what)
                    keep = offset + mine * half
                    places.append((keep, offset + (1 - mine) * half, half))
                    offset, rows = keep, half
                elif name == "line":
                    if what == 0:
                        line_start, rows = offset, rows // line_length
                        offset = line_start + self.place * rows
                    places.append((line_start, line_start, rows))
                else:
                    places.append((offset, offset, rows))
            self.offsets.append(places)

    def step_of(self, index, step):
        kind = self.groups[index][0]
        if step < self.there_count:
            return kind, step, False
        beyond = self.total_steps - 2 * self.there_count
        return kind, self.there_count - 1 + beyond - (step - self.there_count), True

    def rows(self, index, offset, rows):
        _, first_block, size, _ = self.groups[index]
        return self.own.at[pl.ds(first_block, size), rows_at(offset, rows)]

    def copy(self, index, step, side, source, target, device):
        return pltpu.make_async_remote_copy(
            src_ref=source,
            dst_ref=target,
            send_sem=self.send_sems.at[index, step, side],
            recv_sem=self.recv_sems.at[index, step, side],
            device_id=device,
            device_id_type=MESH,
        )

    def arrival(self, index, there, side):
        kind = self.groups[index][0]
        start, rows = self.arrival_places[kind][there]
        name, turn = self.there[kind][there]
        if name == "line" and turn > 0:
            start += side * rows
        size = self.groups[index][2]
        return self.arrivals.at[pl.ds(0, size), pl.ds(self.starts[index] + start, rows)]

    def neighbour(self, side):
        shift = 2 if side else -2
        return (lax.axis_index("pipe"), lax.axis_index("dp") + shift, lax.axis_index("sub"))

    def line_sends(self, turn, back):
        place, top = self.place, line_length - 1
        if back:
            down = ((place + turn <= top) & (place > 0), place + turn)
            up = ((place - turn >= 0) & (place < top), place - turn)
        else:
            down = ((place >= top - turn) & (place > 0), place - top + turn)
            up = ((place <= turn) & (place < top), place + top - turn)
        return down, up

    def line_gets(self, turn, back):
        place, top = self.place, line_length - 1
        if back:
            below = ((place >= 1) & (place - 1 - turn >= 0), place - 1 - turn)
            above = ((place < top) & (place + 1 + turn <= top), place + 1 + turn)
        else:
            below = ((place >= 1) & (place - 1 <= turn), place + top - 1 - turn)
            above = ((place < top) & (place + 1 >= top - turn), place + 1 - top + turn)
        return below, above

    def line_copy(self, index, step, side, shard):
        kind, there, back = self.step_of(index, step)
        start, _, rows = self.offsets[kind][there]
        source = self.rows(index, start + shard * rows, rows)
        target = source if back else self.arrival(index, there, 1 - side)
        return pltpu.make_async_remote_copy(
            src_ref=source,
            dst_ref=target,
            send_sem=self.send_sems.at[index, step, side],
            recv_sem=self.recv_sems.at[index, step, 1 - side],
            device_id=self.neighbour(side),
            device_id_type=MESH,
        )

    def line_landing(self, index, step, side, shard):
        kind, there, back = self.step_of(index, step)
        start, _, rows = self.offsets[kind][there]
        place = self.rows(index, start + shard * rows, rows)
        target = place if back else self.arrival(index, there, side)
        return self.copy(index, step, side, place, target, self.neighbour(side))

    def pair_copy(self, index, step, landing):
        kind, there, back = self.step_of(index, step)
        keep, give, rows = self.offsets[kind][there]
        bit = self.there[kind][there][1]
        if back:
            source = self.rows(index, keep, rows)
            target = self.rows(index, give if landing else keep, rows)
        else:
            source = self.rows(index, give, rows)
            target = self.arrival(index, there, 0)
        return self.copy(index, step, 0, source, target, partner_id(bit))

    def add(self, index, there, side, offset, rows):
        total = self.rows(index, offset, rows)
        arrived = self.arrival(index, there, side)
        for member in range(self.groups[index][2]):
            total[member] = (
                total[member].astype(jnp.float32) + arrived[member].astype(jnp.float32)
            ).astype(jnp.bfloat16)

    def send(self, index, step):
        kind, there, back = self.step_of(index, step)
        name, what = self.there[kind][there]
        if name != "line":
            if back:
                pl.semaphore_wait(self.free_sems.at[index, there, 0], 1)
            self.pair_copy(index, step, False).start()
            return
        turn = line_length - 2 - what if back else what
        for side, (sends, shard) in enumerate(self.line_sends(turn, back)):

            @pl.when(sends)
            def _():
                if back:
                    pl.semaphore_wait(self.free_sems.at[index, there, side], 1)
                self.line_copy(index, step, side, shard).start()

    def receive(self, index, step):
        kind, there, back = self.step_of(index, step)
        name, what = self.there[kind][there]
        start, _, rows = self.offsets[kind][there]
        if name != "line":
            self.pair_copy(index, step, True).wait()
            if not back:
                self.add(index, there, 0, start, rows)
                if name == "half":
                    pl.semaphore_signal(
                        self.free_sems.at[index, there, 0],
                        inc=1,
                        device_id=partner_id(what),
                        device_id_type=MESH,
                    )
            return
        turn = line_length - 2 - what if back else what
        for side, (sends, shard) in enumerate(self.line_sends(turn, back)):

            @pl.when(sends)
            def _():
                self.line_copy(index, step, side, shard).wait_send()
                if not back:
                    pl.semaphore_signal(
                        self.free_sems.at[index, there, 1 - side],
                        inc=1,
                        device_id=self.neighbour(side),
                        device_id_type=MESH,
                    )

        for side, (gets, shard) in enumerate(self.line_gets(turn, back)):

            @pl.when(gets)
            def _():
                self.line_landing(index, step, side, shard).wait_recv()
                if not back:
                    self.add(index, there, side, start + shard * rows, rows)

    def advance(self, index, step):
        self.receive(index, step - 1)
        if step < self.total_steps:
            self.send(index, step)


def sum_kernel(bits, blocks, *refs):
    lefts, rights, small_in = refs[0:4], refs[4:8], refs[8]
    own, small_out = refs[9:11]
    left_bufs, right_bufs = refs[11:15], refs[15:19]
    arrivals, send_sems, recv_sems, free_sems = refs[19:23]
    small, small_got, load_sems, small_send, small_recv = refs[23:]
    near, sub, line, beyond = bits
    pairs = (near, sub, *line, *beyond)
    stage_count = len(pairs)

    loads = [None] * 4
    for index in reversed(range(4)):
        left_load = pltpu.make_async_copy(lefts[index], left_bufs[index], load_sems.at[2 * index])
        right_load = pltpu.make_async_copy(
            rights[index], right_bufs[index], load_sems.at[2 * index + 1]
        )
        loads[index] = (left_load, right_load)

    def start_load(index):
        if index >= 0:
            for load in loads[index]:
                load.start()

    start_load(3)
    start_load(2)
    loaded = [False] * 4

    groups = exchange_groups()
    exchange = Exchange(bits, groups, own, arrivals, send_sems, recv_sems, free_sems)
    place = line_place()
    barrier = pltpu.get_barrier_semaphore()
    for bit in pairs:
        pl.semaphore_signal(barrier, inc=1, device_id=partner_id(bit), device_id_type=MESH)
    for side, near_end in enumerate((place > 0, place < line_length - 1)):

        @pl.when(near_end)
        def _():
            pl.semaphore_signal(
                barrier, inc=1, device_id=exchange.neighbour(side), device_id_type=MESH
            )

    ends = jnp.where((place == 0) | (place == line_length - 1), 1, 2)
    pl.semaphore_wait(barrier, stage_count + ends)

    def produce(block):
        index, row, column = blocks[block]
        if not loaded[index]:
            loads[index][0].wait()
            loads[index][1].wait()
            loaded[index] = True
            start_load(index - 2)
        left = left_bufs[index][:, row * block_rows : (row + 1) * block_rows]
        right = right_bufs[index][:, column * block_cols : (column + 1) * block_cols]
        own[block] = lax.dot_general(
            left, right, (((0,), (0,)), ((), ())), preferred_element_type=jnp.float32
        ).astype(jnp.bfloat16)

    def small_copy(stage):
        return pltpu.make_async_remote_copy(
            src_ref=small.at[stage],
            dst_ref=small_got.at[stage],
            send_sem=small_send.at[stage],
            recv_sem=small_recv.at[stage],
            device_id=partner_id(pairs[stage]),
            device_id_type=MESH,
        )

    last = max(group[3] for group in groups) + exchange.total_steps
    for tick in range(last + 1):
        for index, (_, start, size, begin) in enumerate(groups):
            if begin == tick:
                for block in range(start, start + size):
                    produce(block)
                exchange.send(index, 0)
        if tick == 0:
            small[0] = small_in[...]
        elif tick <= stage_count:
            small_copy(tick - 1).wait()
            total = small[tick - 1] + small_got[tick - 1]
            if tick < stage_count:
                small[tick] = total
            else:
                small_out[...] = total
        if tick < stage_count:
            small_copy(tick).start()
        for step in range(1, exchange.total_steps + 1):
            for index, (*_, begin) in enumerate(groups):
                if begin + step == tick:
                    exchange.advance(index, step)


def summed_grads(lefts, rights, small, dp_count, sub_count):
    tokens, width = lefts[3].shape
    hidden = lefts[0].shape[1]
    bits = exchange_bits(dp_count, sub_count)
    near, sub, line, beyond = bits
    stage_count = 2 + len(line) + len(beyond)
    blocks = grad_blocks(width, hidden)
    block_count = len(blocks)
    groups = exchange_groups()
    assert sum(group[2] for group in groups) == block_count
    there = kind_steps(0, near, sub, beyond)
    steps = 2 * len(there) - len(beyond)
    rows = sum(arrival_rows(kind_steps(kind, near, sub, beyond))[1] for kind, *_ in groups)
    low = jnp.bfloat16
    hbm = pl.BlockSpec(memory_space=pl.ANY)
    vmem = pl.BlockSpec(memory_space=pltpu.VMEM)
    return pl.pallas_call(
        functools.partial(sum_kernel, bits, blocks),
        name="grad_sums",
        out_shape=(
            pltpu.VMEM((block_count, block_rows, block_cols), low),
            pltpu.VMEM(small.shape, jnp.float32),
        ),
        in_specs=[hbm] * 8 + [vmem],
        out_specs=(vmem, vmem),
        scratch_shapes=[pltpu.VMEM(array.shape, low) for array in lefts]
        + [pltpu.VMEM(array.shape, low) for array in rights]
        + [
            pltpu.VMEM((most_blocks, rows, block_cols), low),
            pltpu.SemaphoreType.DMA((len(groups), steps, 2)),
            pltpu.SemaphoreType.DMA((len(groups), steps, 2)),
            pltpu.SemaphoreType.REGULAR((len(groups), len(there), 2)),
            pltpu.VMEM((stage_count, *small.shape), jnp.float32),
            pltpu.VMEM((stage_count, *small.shape), jnp.float32),
            pltpu.SemaphoreType.DMA((8,)),
            pltpu.SemaphoreType.DMA((stage_count,)),
            pltpu.SemaphoreType.DMA((stage_count,)),
        ],
        compiler_params=pltpu.CompilerParams(
            collective_id=0, has_side_effects=True, vmem_limit_bytes=46 * 2**20
        ),
    )(*lefts, *rights, small)


stage_count_out = 6


def finish_kernel(
    blocks,
    own,
    small,
    outputs_in,
    grads_in,
    outputs,
    input_grads,
    attend_gain,
    attend_shift,
    joint,
    joint_bias,
    project,
    project_bias,
    feed_gain,
    feed_shift,
    expand,
    expand_bias,
    shrink,
    shrink_bias,
    stages,
    stage_sems,
    pass_sems,
    outputs_buf,
    grads_buf,
    vector_sems,
    *vector_bufs,
):
    places = (shrink, expand, joint, project)
    width = shrink_bias.shape[1]
    pass_loads = [
        pltpu.make_async_copy(outputs_in, outputs_buf, pass_sems.at[0]),
        pltpu.make_async_copy(grads_in, grads_buf, pass_sems.at[1]),
    ]
    passes = [
        pltpu.make_async_copy(outputs_buf, outputs, pass_sems.at[2]),
        pltpu.make_async_copy(grads_buf, input_grads, pass_sems.at[3]),
    ]
    for copy in pass_loads:
        copy.start()
    vectors = (
        (0, attend_gain),
        (1, attend_shift),
        (2, project_bias),
        (3, feed_gain),
        (4, feed_shift),
        (5, shrink_bias),
        (6, joint_bias),
        (8, expand_bias),
    )
    for index, (row, place) in enumerate(vectors):
        buffer = vector_bufs[index]
        for part in range(place.shape[1] // width):
            buffer[:, part * width : (part + 1) * width] = small[row + part : row + part + 1]
        copy = pltpu.make_async_copy(buffer, place, vector_sems.at[index])
        copy.start()
        passes.append(copy)

    def block_copy(block):
        index, row, column = blocks[block]
        slot = block % stage_count_out
        return pltpu.make_async_copy(
            stages.at[slot],
            places[index].at[
                pl.ds(row * block_rows, block_rows), pl.ds(column * block_cols, block_cols)
            ],
            stage_sems.at[slot],
        )

    for block in range(len(blocks)):
        if block >= stage_count_out:
            block_copy(block - stage_count_out).wait()
        stages[block % stage_count_out] = own[block].astype(jnp.float32)
        block_copy(block).start()
        if block == len(blocks) // 4:
            for load, copy in zip(pass_loads, passes):
                load.wait()
                copy.start()
    for block in range(max(0, len(blocks) - stage_count_out), len(blocks)):
        block_copy(block).wait()
    for copy in passes:
        copy.wait()


def finished(own, small, outputs, input_grads, width, hidden):
    blocks = grad_blocks(width, hidden)
    hbm = pl.BlockSpec(memory_space=pl.ANY)
    vmem = pl.BlockSpec(memory_space=pltpu.VMEM)

    def shape(*dims):
        return jax.ShapeDtypeStruct(dims, jnp.float32)

    return pl.pallas_call(
        functools.partial(finish_kernel, blocks),
        name="finish",
        out_shape=(
            jax.ShapeDtypeStruct(outputs.shape, outputs.dtype),
            jax.ShapeDtypeStruct(input_grads.shape, input_grads.dtype),
            shape(1, width),
            shape(1, width),
            shape(width, 3 * width),
            shape(1, 2 * width),
            shape(width, width),
            shape(1, width),
            shape(1, width),
            shape(1, width),
            shape(width, hidden),
            shape(1, hidden),
            shape(hidden, width),
            shape(1, width),
        ),
        in_specs=[vmem, vmem, hbm, hbm],
        out_specs=tuple([hbm] * 14),
        scratch_shapes=[
            pltpu.VMEM((stage_count_out, block_rows, block_cols), jnp.float32),
            pltpu.SemaphoreType.DMA((stage_count_out,)),
            pltpu.SemaphoreType.DMA((4,)),
            pltpu.VMEM(outputs.shape, outputs.dtype),
            pltpu.VMEM(input_grads.shape, input_grads.dtype),
            pltpu.SemaphoreType.DMA((8,)),
        ]
        + [pltpu.VMEM((1, width), jnp.float32) for _ in range(6)]
        + [
            pltpu.VMEM((1, 2 * width), jnp.float32),
            pltpu.VMEM((1, hidden), jnp.float32),
        ],
        compiler_params=pltpu.CompilerParams(vmem_limit_bytes=16 * 2**20),
    )(
        pltpu.with_memory_space_constraint(own, pltpu.VMEM),
        pltpu.with_memory_space_constraint(small, pltpu.VMEM),
        pltpu.with_memory_space_constraint(outputs, pltpu.HBM),
        pltpu.with_memory_space_constraint(input_grads, pltpu.HBM),
    )


weight_names = (
    "attend_gain",
    "attend_shift",
    "joint_weight",
    "joint_bias",
    "project_weight",
    "project_bias",
    "feed_gain",
    "feed_shift",
    "expand_weight",
    "expand_bias",
    "shrink_weight",
    "shrink_bias",
)


def body(inputs, cotangent, lengths, *params):
    weights = {name: param[0] for name, param in zip(weight_names, params)}
    micro_count, _, seq_rows, width = inputs.shape
    (
        outputs,
        input_grads,
        normed,
        attended,
        normed_two,
        active,
        shrink_grad,
        hidden_grad,
        joint_grad,
        branch_grad,
        small,
        *_,
    ) = run_sections(lengths, inputs[:, 0], cotangent[:, 0], weights)
    hidden = active.shape[1]
    own, small_sum = summed_grads(
        (active, normed_two, normed, attended),
        (shrink_grad, hidden_grad, joint_grad, branch_grad),
        small,
        lax.axis_size("dp"),
        lax.axis_size("sub"),
    )
    outputs, input_grads, *full_grads = finished(
        own, small_sum, outputs, input_grads, width, hidden
    )
    return (
        outputs[None, :, None],
        input_grads.reshape(1, micro_count, 1, seq_rows, width),
        *(grad if grad.shape[0] == 1 else grad[None] for grad in full_grads),
    )


def solution(mesh):
    in_specs = (
        P(None, ("dp", "sub"), None, None),
        P(None, ("dp", "sub"), None, None),
        P(None, ("dp", "sub")),
        P("pipe", None),
        P("pipe", None),
        P("pipe", None, None),
        P("pipe", None),
        P("pipe", None, None),
        P("pipe", None),
        P("pipe", None),
        P("pipe", None),
        P("pipe", None, None),
        P("pipe", None),
        P("pipe", None, None),
        P("pipe", None),
    )
    out_specs = (
        P("pipe", None, ("dp", "sub"), None, None),
        P("pipe", None, ("dp", "sub"), None, None),
        P("pipe", None),
        P("pipe", None),
        P("pipe", None, None),
        P("pipe", None),
        P("pipe", None, None),
        P("pipe", None),
        P("pipe", None),
        P("pipe", None),
        P("pipe", None, None),
        P("pipe", None),
        P("pipe", None, None),
        P("pipe", None),
    )
    return jax.shard_map(body, mesh=mesh, in_specs=in_specs, out_specs=out_specs, check_vma=False)
```
